32 devices in a mesh: dp: 8 (over y, x, core), fsdp: 4 (over z).
Axes of the slice: x: 2, y: 2, z: 4, core: 2. Of those that a mesh axis runs over, the one named last changes fastest.
Arguments:
- tokens: bfloat16 [8, 1536, 960], P('dp', 'fsdp'), may hold values from -6 to 6
- lengths: int32 [8], P('dp'), may hold values from 1153 to 1536, as said below
- cotangent: bfloat16 [8, 1536, 960], P('dp', 'fsdp'), may hold values from -6 to 6
- attention_gain: bfloat16 [960], P('fsdp'), may hold values from 0.5 to 1.5
- feedforward_gain: bfloat16 [960], P('fsdp'), may hold values from 0.5 to 1.5
- query_weight: bfloat16 [960, 960], P('fsdp'), may hold values from -0.1875 to 0.1875
- key_weight: bfloat16 [960, 320], P('fsdp'), may hold values from -0.1875 to 0.1875
- value_weight: bfloat16 [960, 320], P('fsdp'), may hold values from -0.1875 to 0.1875
- out_weight: bfloat16 [960, 960], P('fsdp'), may hold values from -3.5 to 3.5
- gate_weight: bfloat16 [960, 2560], P('fsdp'), may hold values from -0.1875 to 0.1875
- up_weight: bfloat16 [960, 2560], P('fsdp'), may hold values from -0.1875 to 0.1875
- down_weight: bfloat16 [2560, 960], P('fsdp'), may hold values from -0.125 to 0.125
Outputs:
- output: bfloat16 [8, 1536, 960], P('dp', 'fsdp')
- grad_tokens: bfloat16 [8, 1536, 960], P('dp', 'fsdp')
- grad_attention_gain: float32 [960], P('fsdp')
- grad_feedforward_gain: float32 [960], P('fsdp')
- grad_query_weight: float32 [960, 960], P('fsdp')
- grad_key_weight: float32 [960, 320], P('fsdp')
- grad_value_weight: float32 [960, 320], P('fsdp')
- grad_out_weight: float32 [960, 960], P('fsdp')
- grad_gate_weight: float32 [960, 2560], P('fsdp')
- grad_up_weight: float32 [960, 2560], P('fsdp')
- grad_down_weight: float32 [2560, 960], P('fsdp')
The draws below stay inside these ranges and needn't reach their ends.
Inputs may be any that keep to these rules, and one draw needn't show every extreme that they name: `lengths`: every length exceeds 1536 - 384, and some sequence has all 1536 positions real.
All inputs are finite; a program needn't handle non-finite values.
Results may differ from the reference program's by a relative error of at most 0.028.
Values may be sent and summed in bfloat16 or wider, within the bound.
No kernel may reach another device: no remote copies, remote signals or barrier semaphores. Data moves between devices by JAX's collectives and lax.ppermute only.
A program may use at most 256 MiB of HBM per device.

```python
import jax
import jax.numpy as jnp
from jax import lax

D = 960
HEADS = 15
KV_HEADS = 5
HD = 64
FF = 2560
TOK_DEV = 384
SEQ = 1536
GROUPS = 8


def draw_lengths(key, part):
    key = jax.random.fold_in(key, 7)
    first_key, second_key = jax.random.split(key)
    shortness = jax.random.randint(first_key, (GROUPS,), 0, TOK_DEV)
    shortfall = shortness * shortness // TOK_DEV * shortness // TOK_DEV
    chosen = jax.random.randint(second_key, (), 0, GROUPS)
    return jnp.where(jnp.arange(GROUPS) == chosen, SEQ, SEQ - shortfall).astype(jnp.int32)


def steps_of(own_key, extent, cuts, low, top_value):
    def one(dim, shards_of):
        heights = jax.random.uniform(jax.random.fold_in(jax.random.fold_in(own_key, 6), dim), (shards_of,), jnp.float32, low / len(cuts), top_value / len(cuts))
        return jnp.repeat(jnp.exp(heights), extent[dim] // shards_of).reshape((-1,) + (1,) * (len(extent) - dim - 1))

    factor_of = one(*cuts[0])
    for cut in cuts[1:]:
        factor_of = factor_of * one(*cut)
    return factor_of


def centred(stream_key, shape, spread, reach, shards=(), kind=jnp.bfloat16):
    entries = spread * jax.random.normal(stream_key, shape, jnp.float32)
    if shards:
        entries = entries * steps_of(stream_key, shape, shards, -0.22, 0.18)
    return jnp.clip(entries, -reach, reach).astype(kind)


def setup_inputs(seed: int = 0) -> dict:
    keys = jax.random.split(jax.random.key(seed), 13)
    tokens = centred(keys[0], (GROUPS, SEQ, D), 1.0, 6.0, ((0, 8), (1, 4)))
    lengths = draw_lengths(jax.random.fold_in(keys[12], 71), 0)
    cotangent = centred(keys[2], (GROUPS, SEQ, D), 1.0, 6.0, ((0, 8), (1, 4)))
    attention_gain = jnp.clip(1.0 + 0.1 * jax.random.normal(keys[3], (D,), jnp.float32), 0.5, 1.5).astype(jnp.bfloat16)
    feedforward_gain = jnp.clip(1.0 + 0.1 * jax.random.normal(keys[4], (D,), jnp.float32), 0.5, 1.5).astype(jnp.bfloat16)
    query_weight = centred(keys[5], (D, D), D ** -0.5, 0.1875, ((0, 4),))
    key_weight = centred(keys[6], (D, KV_HEADS * HD), D ** -0.5, 0.1875, ((0, 4),))
    value_weight = centred(keys[7], (D, KV_HEADS * HD), D ** -0.5, 0.1875, ((0, 4),))
    out_weight = centred(keys[8], (D, D), (max(D // 256, 1)) ** -0.5, 3.5, ((0, 4),))
    gate_weight = centred(keys[9], (D, FF), D ** -0.5, 0.1875, ((0, 4),))
    up_weight = centred(keys[10], (D, FF), D ** -0.5, 0.1875, ((0, 4),))
    down_weight = centred(keys[11], (FF, D), FF ** -0.5, 0.125, ((0, 4),))
    return dict(tokens=tokens, lengths=lengths, cotangent=cotangent, attention_gain=attention_gain, feedforward_gain=feedforward_gain, query_weight=query_weight, key_weight=key_weight, value_weight=value_weight, out_weight=out_weight, gate_weight=gate_weight, up_weight=up_weight, down_weight=down_weight)


@jax.custom_vjp
def low(v):
    return lax.optimization_barrier(v.astype(jnp.bfloat16)).astype(jnp.float32)

@jax.custom_vjp
def low_back(v):
    return v

def low_keep(v):
    return (low(v), None)

def low_pass(kept, grad):
    return (grad,)

def back_keep(v):
    return (v, None)

def back_low(kept, grad):
    return (low(grad),)
low.defvjp(low_keep, low_pass)
low_back.defvjp(back_keep, back_low)

def product(left, right):
    return jnp.dot(left, right, precision=lax.Precision.HIGHEST)

def rms_norm(inputs, norm_gain):
    return inputs * lax.rsqrt(lax.optimization_barrier(jnp.mean(inputs * inputs, axis=-1, keepdims=True)) + 1e-05) * norm_gain

def rotary(values, cosine, sine_part):
    half_size = values.shape[-1] // 2
    first_half = values[..., :half_size]
    second_half = values[..., half_size:]
    cos_rows = cosine[:, None, :]
    sin_rows = sine_part[:, None, :]
    return jnp.concatenate([first_half * cos_rows - second_half * sin_rows, second_half * cos_rows + first_half * sin_rows], axis=-1)

def block_layer(inputs, params, cosine, sine_part, key_mask):
    attention_gain, feedforward_gain, query_weight, key_weight, value_weight, out_weight, gate_weight, up_weight, down_weight = params
    length = inputs.shape[0]
    group_count = HEADS // KV_HEADS
    score_scale = HD ** (-0.5)
    normed = low(rms_norm(inputs, attention_gain))
    queries = low(rotary(low_back(product(normed, query_weight)).reshape(length, HEADS, HD), cosine, sine_part))
    key_rows = low(rotary(low_back(product(normed, key_weight)).reshape(length, KV_HEADS, HD), cosine, sine_part))
    value_rows = low(low_back(product(normed, value_weight))).reshape(length, KV_HEADS, HD)
    queries = queries.reshape(length, KV_HEADS, group_count, HD)
    block_rows = min(512, length)
    starts = (jnp.arange(length // block_rows) * block_rows).astype(jnp.int32)

    def one_block(start_row):
        query_block = lax.dynamic_slice_in_dim(queries, start_row, block_rows, 0)
        allowed = lax.dynamic_slice_in_dim(key_mask, start_row, block_rows, 0)
        scores = low_back(jnp.einsum('qhgd,khd->hgqk', query_block, key_rows, precision=lax.Precision.HIGHEST))
        scores = jnp.where(allowed[None, None], scores * score_scale, -1e+30)
        attention_probs = low(jax.nn.softmax(scores, axis=-1))
        return jnp.einsum('hgqk,khd->qhgd', attention_probs, value_rows, precision=lax.Precision.HIGHEST)
    mixture = lax.map(jax.checkpoint(one_block), starts).reshape(length, HEADS * HD)
    mixture = low_back(low(mixture))
    hidden = inputs + low_back(product(mixture, out_weight))
    normed_ffn = low(rms_norm(hidden, feedforward_gain))
    gate_rows = low_back(product(normed_ffn, gate_weight))
    up_rows = low_back(product(normed_ffn, up_weight))
    active = low(jax.nn.silu(gate_rows) * up_rows)
    return hidden + low_back(product(active, down_weight))

def reference(tokens, lengths, cotangent, attention_gain, feedforward_gain, query_weight, key_weight, value_weight, out_weight, gate_weight, up_weight, down_weight):
    params = tuple((weight.astype(jnp.float32) for weight in (attention_gain, feedforward_gain, query_weight, key_weight, value_weight, out_weight, gate_weight, up_weight, down_weight)))
    seq_span = tokens.shape[1]
    positions = jnp.arange(seq_span, dtype=jnp.int32)
    half_size = HD // 2
    frequency = 10000.0 ** (-jnp.arange(half_size, dtype=jnp.float32) * 2.0 / HD)
    angles = positions.astype(jnp.float32)[:, None] * frequency[None, :]
    cosine = jnp.cos(angles)
    sine_part = jnp.sin(angles)

    def one_sequence(totals, operands):
        inputs, seq_length, grad_rows = operands
        key_mask = (positions[None, :] <= positions[:, None]) & (positions[None, :] < seq_length)
        valid_rows = (positions < seq_length).astype(jnp.float32)

        def forward(start_rows, weights):
            middle_rows = block_layer(start_rows, weights, cosine, sine_part, key_mask)
            return block_layer(middle_rows, weights, cosine, sine_part, key_mask)
        result, pullback = jax.vjp(forward, inputs.astype(jnp.float32), params)
        grad_start, grad_weights = pullback(grad_rows.astype(jnp.float32) * valid_rows[:, None])
        totals = jax.tree.map(jnp.add, totals, grad_weights)
        return (totals, (result.astype(jnp.bfloat16), grad_start.astype(jnp.bfloat16)))
    zero_grads = tuple((jnp.zeros(weight.shape, jnp.float32) for weight in params))
    totals, (outputs, grad_inputs) = lax.scan(one_sequence, zero_grads, (tokens, lengths, cotangent))
    return (outputs, grad_inputs, totals[0], totals[1], totals[2], totals[3], totals[4], totals[5], totals[6], totals[7], totals[8])
```

```python
import jax
import jax.numpy as jnp
from jax import lax
from jax.experimental import pallas as pl
from jax.experimental.pallas import tpu as pltpu
from jax.sharding import PartitionSpec as P

HEADS = 15
KV_HEADS = 5
HD = 64
GROUP = HEADS // KV_HEADS
KV = KV_HEADS * HD

norm_epsilon = 1e-05
rotary_base = 10000.0

bf16 = jnp.bfloat16
f32 = jnp.float32


def first_hop(i):
    return i ^ (4 if i & 1 else 2)


def second_hop(i):
    return i ^ (2 if i & 1 else 4)


def sibling(i):
    return i ^ 1


def swap(value, hop):
    count = lax.axis_size("dp")
    return lax.ppermute(value, "dp", [(i, hop(i)) for i in range(count)])


def climb(value, step):
    count = lax.axis_size("fsdp")
    return lax.ppermute(value, "fsdp", [(i, i + 1) for i in range(step - 1, count - 1)])


def descend(value, step):
    count = lax.axis_size("fsdp")
    return lax.ppermute(value, "fsdp", [(i, i - 1) for i in range(1, count - step + 1)])


def place():
    low = lax.axis_index("dp") % 8
    core = low % 2
    one = jnp.where(core == 1, 4, 2)
    return low, core, one, 6 - one


def gather_pieces(own):
    count = lax.axis_size("fsdp")
    z = lax.axis_index("fsdp")
    low, core, one, two = place()
    below, above = [], []
    up = down = own
    for step in range(1, count):
        up = climb(up, step)
        down = descend(down, step)
        below.append(up)
        above.append(down)
    mine = jnp.stack(
        [
            jnp.where(z + o < count, above[o - 1], below[count - o - 1])
            for o in range(1, count)
        ]
    )
    a = swap(mine, first_hop)
    b = swap(mine, second_hop)
    ab = swap(a, second_hop)
    s, sa, sb, sab = (swap(v, sibling) for v in (mine, a, b, ab))
    odd = core == 1
    return [
        mine,
        s,
        jnp.where(odd, b, a),
        jnp.where(odd, sa, sb),
        jnp.where(odd, a, b),
        jnp.where(odd, sb, sa),
        ab,
        sab,
    ]


def in_order(pieces, low):
    stacked = jnp.stack(pieces)
    return jnp.stack(
        [lax.dynamic_index_in_dim(stacked, low ^ j, 0, keepdims=False) for j in range(8)]
    )


def all_blocks(others, own):
    count = lax.axis_size("fsdp")
    z = lax.axis_index("fsdp")
    both = jnp.concatenate([own[None], others])
    return jnp.stack(
        [
            lax.dynamic_index_in_dim(both, (k - z + count) % count, 0, keepdims=False)
            for k in range(count)
        ]
    )


def gather_whole(shard_pieces):
    low, core, one, two = place()
    own = lax.dynamic_index_in_dim(shard_pieces, low, 0, keepdims=False)
    pieces = in_order(gather_pieces(own), low)
    return all_blocks(jnp.moveaxis(pieces, 1, 0), shard_pieces)


def add(a, b):
    return (a.astype(f32) + b.astype(f32)).astype(bf16)


def reduce_pieces(keep, send, quarter):
    count = lax.axis_size("fsdp")
    z = lax.axis_index("fsdp")
    low, core, one, two = place()
    half = add(keep, swap(send, sibling))

    def part(flip):
        return quarter(half, (low ^ flip) // 2)

    got = swap(jnp.stack([part(one), part(6)]), first_hop)
    near = add(part(0), got[0])
    far = add(part(two), got[1])
    near = add(near, swap(far, second_hop))
    total = lax.dynamic_index_in_dim(near, z, 0, keepdims=False).astype(f32)
    for o in range(1, count):
        block = lax.dynamic_index_in_dim(near, (z + o) % count, 0, keepdims=False)
        total = total + lax.ppermute(
            block, "fsdp", [(i, (i + o) % count) for i in range(count)]
        ).astype(f32)
    wide = lax.axis_size("dp")
    mine = total.astype(bf16)
    if wide > 8:
        groups = [[i + 8 * k for k in range(wide // 8)] for i in range(8)]
        mine = lax.psum(mine, "dp", axis_index_groups=groups)
    b = swap(mine, second_hop)
    a, ba = swap(mine, first_hop), swap(b, first_hop)
    s, sa, sb, sab = (swap(v, sibling) for v in (mine, a, b, ba))
    odd = core == 1
    return in_order(
        [
            mine,
            s,
            jnp.where(odd, b, a),
            jnp.where(odd, sa, sb),
            jnp.where(odd, a, b),
            jnp.where(odd, sb, sa),
            ba,
            sab,
        ],
        low,
    )


def product(a, b, over_a, over_b):
    return lax.dot_general(
        a, b, (((over_a,), (over_b,)), ((), ())), preferred_element_type=f32
    )


def side_by_side(x):
    return jnp.concatenate([x[HD * g : HD * (g + 1)] for g in range(GROUP)], axis=1)


def diagonal_mask(scores, rows, room):
    key = lax.broadcasted_iota(jnp.int32, (rows, rows), 0)
    query = lax.broadcasted_iota(jnp.int32, (rows, rows), 1)
    seen = (key <= query) & (key < room)
    return jnp.where(jnp.concatenate([seen] * GROUP, axis=1), scores, -1e30)


def attend_kernel(place_ref, q_ref, *refs):
    kv_refs = refs[:-5]
    o_ref, lse_ref, m_ref, l_ref, a_ref = refs[-5:]
    z, room = place_ref[0], place_ref[1]
    rows = q_ref.shape[1]
    q = side_by_side(q_ref[...])
    s = diagonal_mask(product(kv_refs[0][0], q, 0, 0), rows, room)
    m = jnp.max(s, axis=0, keepdims=True)
    p = jnp.exp(s - m)
    m_ref[...] = m
    l_ref[...] = jnp.sum(p, axis=0, keepdims=True)
    a_ref[...] = product(kv_refs[0][1], p.astype(bf16), 1, 0)
    for d in range(1, len(kv_refs)):

        @pl.when(z >= d)
        def _():
            s = product(kv_refs[d][0], q, 0, 0)
            before = m_ref[...]
            m = jnp.maximum(before, jnp.max(s, axis=0, keepdims=True))
            p = jnp.exp(s - m)
            shrink = jnp.exp(before - m)
            m_ref[...] = m
            l_ref[...] = l_ref[...] * shrink + jnp.sum(p, axis=0, keepdims=True)
            a_ref[...] = a_ref[...] * shrink + product(kv_refs[d][1], p.astype(bf16), 1, 0)

    l = l_ref[...]
    o = (a_ref[...] / l).astype(bf16)
    lse = m_ref[...] + jnp.log(l)
    for g in range(GROUP):
        o_ref[HD * g : HD * (g + 1), :] = o[:, rows * g : rows * (g + 1)]
        lse_ref[0, g : g + 1, :] = lse[:, rows * g : rows * (g + 1)]


def specs(rows):
    return (
        pl.BlockSpec((GROUP * HD, rows), lambda h, s: (h, 0)),
        pl.BlockSpec((2, HD, rows), lambda h, s: (0, h, 0)),
        pl.BlockSpec((1, GROUP, rows), lambda h, s: (h, 0, 0)),
    )


def attend(where, q, kvs):
    rows = q.shape[1]
    q_spec, kv_spec, lse_spec = specs(rows)
    return pl.pallas_call(
        attend_kernel,
        grid_spec=pltpu.PrefetchScalarGridSpec(
            num_scalar_prefetch=1,
            grid=(KV_HEADS,),
            in_specs=[q_spec] + [kv_spec] * len(kvs),
            out_specs=[q_spec, lse_spec],
            scratch_shapes=[
                pltpu.VMEM((1, GROUP * rows), f32),
                pltpu.VMEM((1, GROUP * rows), f32),
                pltpu.VMEM((HD, GROUP * rows), f32),
            ],
        ),
        out_shape=[
            jax.ShapeDtypeStruct(q.shape, bf16),
            jax.ShapeDtypeStruct((KV_HEADS, GROUP, rows), f32),
        ],
        compiler_params=pltpu.CompilerParams(vmem_limit_bytes=40 * 2**20),
        name="attend",
    )(where, q, *kvs)


def attend_back_kernel(place_ref, q_ref, o_ref, do_ref, lse_ref, *refs):
    n = (len(refs) - 2) // 2
    kv_refs, dq_ref, dkv_refs, total_ref = refs[:n], refs[n], refs[n + 1 : -1], refs[-1]
    z, room = place_ref[0], place_ref[1]
    rows = q_ref.shape[1]
    q, do, o = side_by_side(q_ref[...]), side_by_side(do_ref[...]), side_by_side(o_ref[...])
    lse = jnp.concatenate([lse_ref[0, g : g + 1, :] for g in range(GROUP)], axis=1)
    delta = jnp.sum(do.astype(f32) * o.astype(f32), axis=0, keepdims=True)

    def block(d):
        k, v = kv_refs[d][0], kv_refs[d][1]
        s = product(k, q, 0, 0)
        if d == 0:
            s = diagonal_mask(s, rows, room)
        p = jnp.exp(s - lse)
        dp = product(v, do, 0, 0)
        ds = (p * (dp - delta)).astype(bf16)
        dkv_refs[d][1] = product(do, p.astype(bf16), 1, 1).astype(bf16)
        dkv_refs[d][0] = product(q, ds, 1, 1).astype(bf16)
        return product(k, ds, 1, 0)

    total_ref[...] = block(0)
    for d in range(1, n):

        @pl.when(z >= d)
        def _():
            total_ref[...] += block(d)

        @pl.when(z < d)
        def _():
            dkv_refs[d][...] = jnp.zeros(dkv_refs[d].shape, bf16)

    dq = total_ref[...] * HD ** (-0.5)
    for g in range(GROUP):
        dq_ref[HD * g : HD * (g + 1), :] = dq[:, rows * g : rows * (g + 1)]


def attend_back(where, q, o, do, lse, kvs):
    rows = q.shape[1]
    q_spec, kv_spec, lse_spec = specs(rows)
    n = len(kvs)
    out = pl.pallas_call(
        attend_back_kernel,
        grid_spec=pltpu.PrefetchScalarGridSpec(
            num_scalar_prefetch=1,
            grid=(KV_HEADS,),
            in_specs=[q_spec, q_spec, q_spec, lse_spec] + [kv_spec] * n,
            out_specs=[q_spec] + [kv_spec] * n,
            scratch_shapes=[pltpu.VMEM((HD, GROUP * rows), f32)],
        ),
        out_shape=[jax.ShapeDtypeStruct(q.shape, f32)]
        + [jax.ShapeDtypeStruct(kv.shape, bf16) for kv in kvs],
        compiler_params=pltpu.CompilerParams(vmem_limit_bytes=40 * 2**20),
        name="attend_back",
    )(where, q, o, do, lse, *kvs)
    return out[0], out[1:]


def dot(a, b, pattern):
    return jnp.einsum(pattern, a, b, preferred_element_type=f32)


def rotary(columns, cosine, sine):
    heads = columns.shape[0] // HD
    halves = columns.reshape(heads, 2, HD // 2, columns.shape[1])
    a, b = halves[:, 0], halves[:, 1]
    return jnp.stack([a * cosine - b * sine, b * cosine + a * sine], axis=1).reshape(
        columns.shape
    )


def normalize(x, gain):
    scale = lax.rsqrt(jnp.mean(x * x, axis=-1, keepdims=True) + norm_epsilon)
    unit = x * scale
    return (unit * gain).astype(bf16), unit, scale


def normalize_back(grad, gain, unit, scale):
    grad_unit = grad * gain
    return (
        scale * (grad_unit - unit * jnp.mean(grad_unit * unit, axis=-1, keepdims=True)),
        jnp.sum(grad * unit, axis=0),
    )


def forward(x, weights, where, tables):
    gains, w_kv, w_q, w_o, w_gu, w_down = weights
    cosine, sine = tables
    count = lax.axis_size("fsdp")
    normed, unit, scale = normalize(x, gains[0])
    kv = dot(normed, w_kv, "td,df->ft")
    kv = jnp.stack([rotary(kv[:KV], cosine, sine), kv[KV:]]).astype(bf16)
    kvs = [kv]
    for step in range(1, count):
        kvs.append(climb(kvs[-1], step))
    q = rotary(dot(normed, w_q, "td,df->ft"), cosine, sine).astype(bf16) * bf16(HD**-0.5)
    mixture, lse = attend(where, q, kvs)
    hidden = x + dot(mixture, w_o, "ft,fd->td")
    normed_ffn, unit_ffn, scale_ffn = normalize(hidden, gains[1])
    gate, up = (dot(normed_ffn, w_gu[k], "td,df->tf") for k in range(2))
    active = (jax.nn.silu(gate) * up).astype(bf16)
    result = hidden + dot(active, w_down, "td,df->tf")
    return result, (
        normed, unit, scale, q, kvs, mixture, lse, unit_ffn, scale_ffn, normed_ffn,
        gate, up, active,
    )


def backward(grad, saved, weights, where, tables):
    gains, w_kv, w_q, w_o, w_gu, w_down = weights
    (
        normed, unit, scale, q, kvs, mixture, lse, unit_ffn, scale_ffn, normed_ffn,
        gate, up, active,
    ) = saved
    cosine, sine = tables
    count = lax.axis_size("fsdp")
    low = grad.astype(bf16)
    g_down = dot(active, low, "tf,td->fd")
    d_active = dot(low, w_down, "td,fd->tf")
    sig = jax.nn.sigmoid(gate)
    d_gate = (d_active * up * sig * (1.0 + gate * (1.0 - sig))).astype(bf16)
    d_up = (d_active * gate * sig).astype(bf16)
    g_gate = dot(normed_ffn, d_gate, "td,tf->df")
    g_up = dot(normed_ffn, d_up, "td,tf->df")
    d_normed_ffn = dot(d_gate, w_gu[0], "tf,df->td") + dot(d_up, w_gu[1], "tf,df->td")
    d_norm, g_ffn_gain = normalize_back(d_normed_ffn, gains[1], unit_ffn, scale_ffn)
    d_hidden = grad + d_norm
    hidden_low = d_hidden.astype(bf16)
    g_out = dot(mixture, hidden_low, "ft,td->fd")
    d_mixture = dot(hidden_low, w_o, "td,fd->ft").astype(bf16)
    dq, dkvs = attend_back(where, q, mixture, d_mixture, lse, kvs)
    moving = dkvs[count - 1]
    for step in range(1, count):
        got = lax.ppermute(
            moving, "fsdp", [(i, i - 1) for i in range(count - step, count)]
        )
        moving = add(dkvs[count - 1 - step], got)
    dkv = moving.astype(f32)
    dq = rotary(dq, cosine, -sine).astype(bf16)
    dkv = jnp.concatenate([rotary(dkv[0], cosine, -sine), dkv[1]]).astype(bf16)
    g_q = dot(normed, dq, "td,ft->df")
    g_kv = dot(normed, dkv, "td,ft->df")
    d_normed = dot(dq, w_q, "ft,df->td") + dot(dkv, w_kv, "ft,df->td")
    d_norm, g_attn_gain = normalize_back(d_normed, gains[0], unit, scale)
    return d_hidden + d_norm, (g_attn_gain, g_ffn_gain, g_kv, g_q, g_out, g_gate, g_up, g_down)


def local(
    tokens,
    lengths,
    cotangent,
    attention_gain,
    feedforward_gain,
    query_weight,
    key_weight,
    value_weight,
    out_weight,
    gate_weight,
    up_weight,
    down_weight,
):
    rows = tokens.shape[1]
    count = lax.axis_size("fsdp")
    z = lax.axis_index("fsdp")
    low, core, one, two = place()
    positions = z * rows + jnp.arange(rows, dtype=jnp.int32)
    length = lengths[0]
    where = jnp.stack([z, length - z * rows]).astype(jnp.int32)
    frequency = rotary_base ** (-jnp.arange(HD // 2, dtype=f32) * 2.0 / HD)
    angles = frequency[:, None] * positions.astype(f32)[None, :]
    tables = (jnp.cos(angles), jnp.sin(angles))
    block = query_weight.shape[0]
    model = block * count
    hidden_units = gate_weight.shape[1]

    own_gains = jnp.stack([attention_gain, feedforward_gain])
    gains = all_blocks(
        jnp.stack(
            [
                lax.ppermute(own_gains, "fsdp", [(i, (i - o) % count) for i in range(count)])
                for o in range(1, count)
            ]
        ),
        own_gains,
    )
    gains = jnp.moveaxis(gains, 0, 1).reshape(2, model).astype(f32)

    def by_quarter(array, lanes):
        cut = array.reshape(2, array.shape[0] // 2, 4, lanes)
        return cut.transpose(2, 0, 1, 3).reshape(8, array.shape[0] // 2, lanes)

    projections = jnp.concatenate([key_weight, value_weight, query_weight, out_weight], axis=1)
    lanes = projections.shape[1] // 4
    projections = gather_whole(by_quarter(projections, lanes))
    projections = (
        projections.reshape(count, 4, 2, block // 2, lanes)
        .transpose(0, 2, 3, 1, 4)
        .reshape(model, 4 * lanes)
    )
    w_kv, w_q, w_o = (
        projections[:, : 2 * KV],
        projections[:, 2 * KV : 2 * KV + model],
        projections[:, 2 * KV + model :],
    )
    f_lanes = hidden_units // 4
    w_gu = jnp.stack([gate_weight, up_weight]).reshape(2, block, 4, f_lanes)
    w_gu = gather_whole(w_gu.transpose(2, 0, 1, 3).reshape(8, block, f_lanes))
    w_gu = (
        w_gu.reshape(count, 4, 2, block, f_lanes)
        .transpose(2, 0, 3, 1, 4)
        .reshape(2, model, hidden_units)
    )
    down_rows = down_weight.shape[0] // 8
    w_down = gather_whole(down_weight.reshape(8, down_rows, model)).reshape(hidden_units, model)
    weights = (gains, w_kv, w_q, w_o, w_gu, w_down)

    start = tokens[0].astype(f32)
    middle, saved_first = forward(start, weights, where, tables)
    final, saved_second = forward(middle, weights, where, tables)
    real = (positions < length).astype(f32)
    gradient = cotangent[0].astype(f32) * real[:, None]
    gradient, second = backward(gradient, saved_second, weights, where, tables)
    gradient, first = backward(gradient, saved_first, weights, where, tables)
    g_attn_gain, g_ffn_gain, g_kv, g_q, g_out, g_gate, g_up, g_down = (
        a + b for a, b in zip(first, second)
    )

    odd = core == 1

    def lane_quarter(half, q):
        return lax.dynamic_slice_in_dim(half, q * (half.shape[2] // 4), half.shape[2] // 4, 2)

    g_down = g_down.astype(bf16).reshape(count, 4, 2, down_rows, model)
    g_down = reduce_pieces(
        lax.dynamic_index_in_dim(g_down, core, 2, keepdims=False),
        lax.dynamic_index_in_dim(g_down, 1 - core, 2, keepdims=False),
        lambda half, q: lax.dynamic_index_in_dim(half, q, 1, keepdims=False),
    )
    g_down = g_down.reshape(down_rows * 8, model).astype(f32)

    g_gate, g_up = (
        g.astype(bf16).reshape(count, block, hidden_units) for g in (g_gate, g_up)
    )
    g_gu = reduce_pieces(
        jnp.where(odd, g_up, g_gate), jnp.where(odd, g_gate, g_up), lane_quarter
    )
    g_gu = (
        g_gu.reshape(4, 2, block, f_lanes).transpose(1, 2, 0, 3).reshape(2, block, hidden_units)
    ).astype(f32)

    g_proj = jnp.concatenate([g_kv, g_q, g_out], axis=1).astype(bf16)
    g_proj = g_proj.reshape(count, 2, block // 2, 4 * lanes)
    g_proj = reduce_pieces(
        lax.dynamic_index_in_dim(g_proj, core, 1, keepdims=False),
        lax.dynamic_index_in_dim(g_proj, 1 - core, 1, keepdims=False),
        lane_quarter,
    )
    g_proj = (
        g_proj.reshape(4, 2, block // 2, lanes).transpose(1, 2, 0, 3).reshape(block, 4 * lanes)
    ).astype(f32)

    g_gains = lax.psum(jnp.stack([g_attn_gain, g_ffn_gain]), ("dp", "fsdp"))
    g_gains = lax.dynamic_slice_in_dim(g_gains, z * block, block, 1)

    return (
        final.astype(bf16)[None],
        gradient.astype(bf16)[None],
        g_gains[0],
        g_gains[1],
        g_proj[:, 2 * KV : 2 * KV + model],
        g_proj[:, :KV],
        g_proj[:, KV : 2 * KV],
        g_proj[:, 2 * KV + model :],
        g_gu[0],
        g_gu[1],
        g_down,
    )


def solution(mesh):
    rows = P("fsdp", None)
    placed = (P("dp", "fsdp", None), P("dp"), P("dp", "fsdp", None), P("fsdp"), P("fsdp")) + (
        rows,
    ) * 7
    return jax.shard_map(
        local,
        mesh=mesh,
        in_specs=placed,
        out_specs=(P("dp", "fsdp", None), P("dp", "fsdp", None), P("fsdp"), P("fsdp"))
        + (rows,) * 7,
        check_vma=False,
    )
```

```python
import jax
import jax.numpy as jnp
from jax import lax
from jax.experimental import pallas as pl
from jax.experimental.pallas import tpu as pltpu
from jax.sharding import PartitionSpec as P

HEADS = 15
KV_HEADS = 5
HD = 64
GROUP = HEADS // KV_HEADS
KV = KV_HEADS * HD

norm_epsilon = 1e-05
rotary_base = 10000.0

bf16 = jnp.bfloat16
f32 = jnp.float32


def first_hop(i):
    return i ^ (4 if i & 1 else 2)


def second_hop(i):
    return i ^ (2 if i & 1 else 4)


def sibling(i):
    return i ^ 1


def swap(value, hop):
    count = lax.axis_size("dp")
    return lax.ppermute(value, "dp", [(i, hop(i)) for i in range(count)])


def climb(value, step):
    count = lax.axis_size("fsdp")
    return lax.ppermute(value, "fsdp", [(i, i + 1) for i in range(step - 1, count - 1)])


def descend(value, step):
    count = lax.axis_size("fsdp")
    return lax.ppermute(value, "fsdp", [(i, i - 1) for i in range(1, count - step + 1)])


def place():
    low = lax.axis_index("dp") % 8
    core = low % 2
    one = jnp.where(core == 1, 4, 2)
    return low, core, one, 6 - one


def around(value, distance):
    count = lax.axis_size("fsdp")
    return lax.ppermute(value, "fsdp", [(i, (i + distance) % count) for i in range(count)])


def after(value, *first):
    return lax.optimization_barrier((value, first))[0]


class Gather:
    def __init__(self, own):
        self.blocks = [around(own, o) for o in range(1, lax.axis_size("fsdp"))]

    def hop(self, *first):
        self.mine = jnp.stack(after(self.blocks, *first))
        self.a = swap(self.mine, first_hop)
        self.b = swap(self.mine, second_hop)

    def hop_on(self, *first):
        self.a = after(self.a, *first)
        self.ab = swap(self.a, second_hop)

    def cross(self, *first):
        b, ab = after((self.b, self.ab), *first)
        mine = [self.mine, self.a, b, ab]
        return mine + [swap(v, sibling) for v in mine]


def piece_ids(low):
    odd = low % 2
    one = 2 + 2 * odd
    two = 6 - one
    return [low, low ^ one, low ^ two, low ^ 6, low ^ 1, low ^ 1 ^ two, low ^ 1 ^ one, low ^ 7]


def lay_out(low, pieces, own, out_shapes, moves):
    count = lax.axis_size("fsdp")
    where = jnp.stack([lax.axis_index("fsdp"), low]).astype(jnp.int32)

    def kernel(where_ref, *refs):
        piece_refs, refs = refs[:8], refs[8:]
        own_refs, refs = refs[: len(own)], refs[len(own) :]
        outs, sem = refs[:-1], refs[-1]
        z, low = where_ref[0], where_ref[1]
        for core in range(2):

            @pl.when(low % 2 == core)
            def _():
                copies = []
                for k, pid in enumerate(piece_ids(low)):
                    own_core = core if k < 4 else 1 - core
                    for o in range(count - 1):
                        block = lax.rem(z + count - 1 - o, count)
                        copies += moves(piece_refs[k].at[o], block, pid // 2, own_core, pid, outs)
                copies += own_moves(own_refs, z, outs)
                handles = [
                    pltpu.make_async_copy(src, dst, sem.at[i])
                    for i, (src, dst) in enumerate(copies)
                ]
                for h in handles:
                    h.start()
                for h in handles:
                    h.wait()

    moves, own_moves = moves
    any_spec = pl.BlockSpec(memory_space=pl.ANY)
    return pl.pallas_call(
        kernel,
        in_specs=[pl.BlockSpec(memory_space=pltpu.SMEM)] + [any_spec] * (8 + len(own)),
        out_specs=[pl.BlockSpec(memory_space=pltpu.VMEM)] * len(out_shapes),
        out_shape=[jax.ShapeDtypeStruct(shape, bf16) for shape in out_shapes],
        scratch_shapes=[pltpu.SemaphoreType.DMA((8 * (count - 1) + len(own),))],
        compiler_params=pltpu.CompilerParams(vmem_limit_bytes=40 * 2**20),
        name="lay_out",
        cost_estimate=cost(5),
    )(where, *pieces, *own)


def rows_at(start, size):
    return pl.ds(pl.multiple_of(start, 16), size)


def lanes_at(start, size):
    return pl.ds(pl.multiple_of(start, 128), size)


def projection_piece(shard, low, core):
    block, width = shard.shape
    rest = block // 2 // 16 * 16
    lanes = width // 4
    return lax.dynamic_slice(shard, (core * rest, low // 2 * lanes), (block - rest, lanes))


def gate_up_piece(gate, up, low, core):
    lanes = gate.shape[1] // 4
    gate, up = (lax.dynamic_slice_in_dim(v, low // 2 * lanes, lanes, 1) for v in (gate, up))
    return jnp.where(core == 1, up, gate)


def down_piece(shard, low):
    rows = shard.shape[0] // 8
    return lax.dynamic_slice_in_dim(shard, low * rows, rows, 0)


def whole_projections(shard, low, pieces):
    count = lax.axis_size("fsdp")
    block, width = shard.shape
    lanes = width // 4
    rest = block // 2 // 16 * 16
    held = block - rest

    def moves(src, z, q, c, pid, outs):
        size = held if c else rest
        return [
            (
                src.at[pl.ds(0, size)],
                outs[0].at[rows_at(z * block + c * rest, size), lanes_at(q * lanes, lanes)],
            )
        ]

    def own_moves(refs, z, outs):
        return [(refs[0], outs[0].at[rows_at(z * block, block)])]

    return lay_out(low, pieces, [shard], [(count * block, width)], (moves, own_moves))[0]


def whole_gate_up(gate, up, low, pieces):
    count = lax.axis_size("fsdp")
    block, width = gate.shape
    lanes = width // 4

    def moves(src, z, q, c, pid, outs):
        return [(src, outs[c].at[rows_at(z * block, block), lanes_at(q * lanes, lanes)])]

    def own_moves(refs, z, outs):
        return [(refs[k], outs[k].at[rows_at(z * block, block)]) for k in range(2)]

    return lay_out(low, pieces, [gate, up], [(count * block, width)] * 2, (moves, own_moves))


def whole_down(shard, low, pieces):
    count = lax.axis_size("fsdp")
    block, width = shard.shape
    rows = block // 8

    def moves(src, z, q, c, pid, outs):
        return [(src, outs[0].at[rows_at(z * block + pid * rows, rows)])]

    def own_moves(refs, z, outs):
        return [(refs[0], outs[0].at[rows_at(z * block, block)])]

    return lay_out(low, pieces, [shard], [(count * block, width)], (moves, own_moves))[0]


def all_blocks(others, own):
    count = lax.axis_size("fsdp")
    z = lax.axis_index("fsdp")
    both = jnp.concatenate([own[None], others])
    return jnp.stack(
        [
            lax.dynamic_index_in_dim(both, (k - z + count) % count, 0, keepdims=False)
            for k in range(count)
        ]
    )


def add(a, b):
    return (a.astype(f32) + b.astype(f32)).astype(bf16)


def cost(us):
    return pl.CostEstimate(flops=int(us * 1e9), bytes_accessed=0, transcendentals=0)


class Reduction:
    def __init__(self, low, make):
        self.low, self.make = low, make
        self.one = 2 + 2 * (low % 2)
        self.two = 6 - self.one
        other = low ^ 1
        self.send = make([other ^ self.two, other ^ 6, other, other ^ self.one], None, 0)
        self.got = swap(self.send, sibling)

    def hop(self):
        self.away = self.make([self.low ^ self.one, self.low ^ 6], self.got, 0)
        self.came = swap(self.away, first_hop)

    def stay(self):
        self.home = self.make([self.low, self.low ^ self.two], self.got, 2)

    def hop_on(self):
        self.far = add(self.home[1], self.came[1])
        self.near = add(self.home[0], self.came[0])
        self.came = swap(self.far, second_hop)

    def shift(self):
        count, z = lax.axis_size("fsdp"), lax.axis_index("fsdp")
        self.near = add(self.near, self.came)
        self.cuts = [
            lax.dynamic_index_in_dim(self.near, (z + o) % count, 0, keepdims=False)
            for o in range(count)
        ]
        self.came = [around(self.cuts[o], o) for o in range(1, count)]

    def give(self):
        total = sum((v.astype(f32) for v in self.came), self.cuts[0].astype(f32))
        wide = lax.axis_size("dp")
        mine = total.astype(bf16)
        if wide > 8:
            groups = [[i + 8 * k for k in range(wide // 8)] for i in range(8)]
            mine = lax.psum(mine, "dp", axis_index_groups=groups)
        b = swap(mine, second_hop)
        a, ab = swap(mine, first_hop), swap(b, first_hop)
        return [mine, a, b, ab] + [swap(v, sibling) for v in (mine, a, b, ab)]


def spread(low, pieces, out_shapes, put):
    def kernel(where_ref, *refs):
        low = where_ref[0]
        for core in range(2):

            @pl.when(low % 2 == core)
            def _():
                for k, pid in enumerate(piece_ids(low)):
                    own_core = core if k < 4 else 1 - core
                    put(refs[8:], pid // 2, own_core, pid, refs[k][...].astype(f32))

    vmem = pl.BlockSpec(memory_space=pltpu.VMEM)
    return pl.pallas_call(
        kernel,
        in_specs=[pl.BlockSpec(memory_space=pltpu.SMEM)] + [vmem] * 8,
        out_specs=[vmem] * len(out_shapes),
        out_shape=[jax.ShapeDtypeStruct(shape, f32) for shape in out_shapes],
        compiler_params=pltpu.CompilerParams(vmem_limit_bytes=40 * 2**20),
        name="spread",
        cost_estimate=cost(3),
    )(low[None], *pieces)


def grad_kernel(left_ref, right_ref, *refs):
    left, right = left_ref[...], right_ref[...]
    left = left.reshape(-1, left.shape[-1])
    right = right.reshape(right.shape[-2:])
    total = product(left, right, 1, 0)
    if len(refs) == 2:
        total = total + refs[0][...].reshape(total.shape).astype(f32)
    refs[-1][...] = total.astype(bf16).reshape(refs[-1].shape)


def grad_pieces(ids, got, first, left, right, left_spec, right_spec, piece_shape):
    n = len(ids)
    block = (1,) + piece_shape
    zeros = (0,) * len(piece_shape)
    in_specs, operands = [left_spec, right_spec], [left, right]
    if got is not None:
        in_specs.append(pl.BlockSpec(block, lambda i, ids: (i + first,) + zeros))
        operands.append(got)
    return pl.pallas_call(
        lambda ids_ref, *refs: grad_kernel(*refs),
        grid_spec=pltpu.PrefetchScalarGridSpec(
            num_scalar_prefetch=1,
            grid=(n,),
            in_specs=in_specs,
            out_specs=pl.BlockSpec(block, lambda i, ids: (i,) + zeros),
        ),
        out_shape=jax.ShapeDtypeStruct((n,) + piece_shape, bf16),
        compiler_params=pltpu.CompilerParams(vmem_limit_bytes=40 * 2**20),
        name="weight_grad",
        cost_estimate=cost(1.6 * n),
    )(jnp.stack(ids).astype(jnp.int32), *operands)


def product(a, b, over_a, over_b):
    return lax.dot_general(
        a, b, (((over_a,), (over_b,)), ((), ())), preferred_element_type=f32
    )


def side_by_side(x):
    return jnp.concatenate([x[HD * g : HD * (g + 1)] for g in range(GROUP)], axis=1)


def diagonal_mask(scores, rows, room):
    key = lax.broadcasted_iota(jnp.int32, (rows, rows), 0)
    query = lax.broadcasted_iota(jnp.int32, (rows, rows), 1)
    seen = (key <= query) & (key < room)
    return jnp.where(jnp.concatenate([seen] * GROUP, axis=1), scores, -1e30)


SUMS = 16


def attend_kernel(d, n, place_ref, q_ref, kv_ref, *refs):
    first, last = d == 0, d == n - 1
    m1_ref, a1_ref = (None, None) if first else refs[:2]
    m2_ref, a2_ref = refs[-2:]
    z, room = place_ref[0], place_ref[1]
    rows = q_ref.shape[1]

    @pl.when(z >= d)
    def _():
        ones = jnp.ones((SUMS, rows), bf16)
        for h in range(KV_HEADS):
            q = side_by_side(q_ref[GROUP * HD * h : GROUP * HD * (h + 1), :])
            k, v = (kv_ref[i, HD * h : HD * (h + 1), :] for i in range(2))
            s = product(k, q, 0, 0)
            if first:
                s = diagonal_mask(s, rows, room)
            m = jnp.max(s, axis=0, keepdims=True)
            if not first:
                m = jnp.maximum(m, m1_ref[h])
            p = jnp.exp(s - m).astype(bf16)
            total = product(jnp.concatenate([v, ones], axis=0), p, 1, 0)
            if not first:
                total = total + a1_ref[h] * jnp.exp(m1_ref[h] - m)
            m2_ref[h] = m
            a2_ref[h] = total

    if not first:

        @pl.when(z < d)
        def _():
            m2_ref[...] = m1_ref[...]
            a2_ref[...] = a1_ref[...]

    if last:
        o_ref, lse_ref = refs[2:4]
        for h in range(KV_HEADS):
            l = a2_ref[h, HD : HD + 1, :]
            o = (a2_ref[h, :HD, :] / l).astype(bf16)
            lse = m2_ref[h] + jnp.log(l)
            for g in range(GROUP):
                here = slice(HD * (GROUP * h + g), HD * (GROUP * h + g + 1))
                o_ref[here, :] = o[:, rows * g : rows * (g + 1)]
                lse_ref[h, g : g + 1, :] = lse[:, rows * g : rows * (g + 1)]


def attend(d, n, where, q, kv, state):
    rows = q.shape[1]
    state_shapes = [(KV_HEADS, 1, GROUP * rows), (KV_HEADS, HD + SUMS, GROUP * rows)]
    out_shape = [jax.ShapeDtypeStruct(shape, f32) for shape in state_shapes]
    scratch = []
    if d == n - 1:
        scratch = [pltpu.VMEM(shape, f32) for shape in state_shapes]
        out_shape = [
            jax.ShapeDtypeStruct(q.shape, bf16),
            jax.ShapeDtypeStruct((KV_HEADS, GROUP, rows), f32),
        ]
    vmem = pl.BlockSpec(memory_space=pltpu.VMEM)
    return pl.pallas_call(
        lambda *refs: attend_kernel(d, n, *refs),
        in_specs=[pl.BlockSpec(memory_space=pltpu.SMEM)] + [vmem] * (2 + len(state)),
        out_specs=[vmem, vmem],
        out_shape=out_shape,
        scratch_shapes=scratch,
        compiler_params=pltpu.CompilerParams(vmem_limit_bytes=40 * 2**20),
        name="attend",
        cost_estimate=cost(4),
    )(where, q, kv, *state)


def specs(rows):
    return (
        pl.BlockSpec((GROUP * HD, rows), lambda h, s: (h, 0)),
        pl.BlockSpec((2, HD, rows), lambda h, s: (0, h, 0)),
        pl.BlockSpec((1, GROUP, rows), lambda h, s: (h, 0, 0)),
    )


def attend_back_kernel(d, place_ref, q_ref, o_ref, do_ref, lse_ref, kv_ref, *refs):
    before_ref = refs[0] if len(refs) == 3 else None
    dq_ref, dkv_ref = refs[-2:]
    z, room = place_ref[0], place_ref[1]
    rows = q_ref.shape[1]

    @pl.when(z >= d)
    def _():
        q, do, o = (side_by_side(r[...]) for r in (q_ref, do_ref, o_ref))
        lse = jnp.concatenate([lse_ref[0, g : g + 1, :] for g in range(GROUP)], axis=1)
        delta = jnp.sum(do.astype(f32) * o.astype(f32), axis=0, keepdims=True)
        k, v = kv_ref[0], kv_ref[1]
        s = product(k, q, 0, 0)
        if d == 0:
            s = diagonal_mask(s, rows, room)
        p = jnp.exp(s - lse)
        dp = product(v, do, 0, 0)
        ds = (p * (dp - delta)).astype(bf16)
        dkv_ref[1] = product(p.astype(bf16), do, 1, 1).T.astype(bf16)
        dkv_ref[0] = product(ds, q, 1, 1).T.astype(bf16)
        dq = product(k, ds, 1, 0) * HD ** (-0.5)
        for g in range(GROUP):
            here = slice(HD * g, HD * (g + 1))
            part = dq[:, rows * g : rows * (g + 1)]
            dq_ref[here, :] = part if before_ref is None else part + before_ref[here, :]

    @pl.when(z < d)
    def _():
        dkv_ref[...] = jnp.zeros(dkv_ref.shape, bf16)
        if before_ref is None:
            dq_ref[...] = jnp.zeros(dq_ref.shape, f32)
        else:
            dq_ref[...] = before_ref[...]


def attend_back(d, where, q, o, do, lse, kv, before):
    rows = q.shape[1]
    q_spec, kv_spec, lse_spec = specs(rows)
    carried = [] if before is None else [before]
    return pl.pallas_call(
        lambda *refs: attend_back_kernel(d, *refs),
        grid_spec=pltpu.PrefetchScalarGridSpec(
            num_scalar_prefetch=1,
            grid=(KV_HEADS,),
            in_specs=[q_spec, q_spec, q_spec, lse_spec, kv_spec] + [q_spec] * len(carried),
            out_specs=[q_spec, kv_spec],
        ),
        out_shape=[jax.ShapeDtypeStruct(q.shape, f32), jax.ShapeDtypeStruct(kv.shape, bf16)],
        compiler_params=pltpu.CompilerParams(vmem_limit_bytes=40 * 2**20),
        name="attend_back",
        cost_estimate=cost(7),
    )(where, q, o, do, lse, kv, *carried)


def dot(a, b, pattern):
    return jnp.einsum(pattern, a, b, preferred_element_type=f32)


def rotary(columns, cosine, sine):
    heads = columns.shape[0] // HD
    halves = columns.reshape(heads, 2, HD // 2, columns.shape[1])
    a, b = halves[:, 0], halves[:, 1]
    return jnp.stack([a * cosine - b * sine, b * cosine + a * sine], axis=1).reshape(
        columns.shape
    )


def normalize(x, gain):
    scale = lax.rsqrt(jnp.mean(x * x, axis=-1, keepdims=True) + norm_epsilon)
    unit = x * scale
    return (unit * gain).astype(bf16), unit, scale


def normalize_back(grad, gain, unit, scale):
    grad_unit = grad * gain
    return (
        scale * (grad_unit - unit * jnp.mean(grad_unit * unit, axis=-1, keepdims=True)),
        jnp.sum(grad * unit, axis=0),
    )


def feed_forward_kernel(x_ref, mix_ref, wo_ref, gain_ref, wg_ref, wu_ref, wd_ref, *refs):
    result_ref, hidden_ref, gate_ref, up_ref, nft_ref, active_ref, nf_ref = refs[-7:]

    @pl.when(pl.program_id(0) == 0)
    def _():
        hidden = x_ref[...] + product(mix_ref[...], wo_ref[...], 0, 0)
        hidden_ref[...] = hidden
        normed, _, _ = normalize(hidden, gain_ref[...])
        nf_ref[...] = normed
        nft_ref[...] = normed.T
        result_ref[...] = hidden

    normed = nf_ref[...]
    gate = product(normed, wg_ref[...], 1, 0)
    up = product(normed, wu_ref[...], 1, 0)
    active = (gate * jax.nn.sigmoid(gate) * up).astype(bf16)
    gate_ref[...] = gate.astype(bf16)
    up_ref[...] = up.astype(bf16)
    active_ref[...] = active.T
    result_ref[...] += product(active, wd_ref[...], 1, 0)


def feed_forward(x, mixture, w_o, gain, w_gate, w_up, w_down, kept):
    rows, model = x.shape
    hidden_units = w_gate.shape[1]
    tile = hidden_units // 4
    half = 0 if kept else 1
    whole = lambda *shape: pl.BlockSpec(shape, lambda i: (0,) * len(shape))
    wide = lambda n: pl.BlockSpec((n, tile), lambda i: (0, i))
    return pl.pallas_call(
        feed_forward_kernel,
        grid=(4,),
        in_specs=[
            whole(rows, model), whole(model, rows), whole(model, model), whole(1, model),
            wide(model), wide(model), pl.BlockSpec((tile, model), lambda i: (i, 0)),
        ]
        + [pl.BlockSpec(memory_space=pl.ANY)] * len(kept),
        out_specs=[
            whole(rows, model), whole(rows, model), wide(rows), wide(rows),
            pl.BlockSpec((model, rows), lambda i: (0, half)),
            pl.BlockSpec((tile, rows), lambda i: (i, half)),
        ],
        out_shape=[
            jax.ShapeDtypeStruct((rows, model), f32),
            jax.ShapeDtypeStruct((rows, model), f32),
            jax.ShapeDtypeStruct((rows, hidden_units), bf16),
            jax.ShapeDtypeStruct((rows, hidden_units), bf16),
            jax.ShapeDtypeStruct((model, 2 * rows), bf16),
            jax.ShapeDtypeStruct((hidden_units, 2 * rows), bf16),
        ],
        scratch_shapes=[pltpu.VMEM((rows, model), bf16)],
        input_output_aliases={7: 4, 8: 5} if kept else {},
        compiler_params=pltpu.CompilerParams(vmem_limit_bytes=48 * 2**20),
        name="feed_forward",
        cost_estimate=cost(12),
    )(x, mixture, w_o, gain[None], w_gate, w_up, w_down, *kept)


def feed_forward_back_kernel(grad_ref, hidden_ref, gain_ref, gate_ref, up_ref, wg_ref, wu_ref,
                             wd_ref, wo_ref, *refs):
    d_gu_ref, d_hidden_ref, low_ref, g_gain_ref, d_mix_ref, total_ref = refs[-6:]
    step = pl.program_id(0)
    low = grad_ref[...].astype(bf16)
    d_active = product(low, wd_ref[...], 1, 1)
    gate, up = gate_ref[...].astype(f32), up_ref[...].astype(f32)
    sig = jax.nn.sigmoid(gate)
    d_gate = (d_active * up * sig * (1.0 + gate * (1.0 - sig))).astype(bf16)
    d_up = (d_active * gate * sig).astype(bf16)
    d_gu_ref[0] = d_gate
    d_gu_ref[1] = d_up
    term = product(d_gate, wg_ref[...], 1, 1) + product(d_up, wu_ref[...], 1, 1)

    @pl.when(step == 0)
    def _():
        total_ref[...] = term

    @pl.when(step > 0)
    def _():
        total_ref[...] += term

    @pl.when(step == pl.num_programs(0) - 1)
    def _():
        hidden = hidden_ref[...]
        scale = lax.rsqrt(jnp.mean(hidden * hidden, axis=-1, keepdims=True) + norm_epsilon)
        d_norm, g_gain = normalize_back(total_ref[...], gain_ref[...], hidden * scale, scale)
        d_hidden = grad_ref[...] + d_norm
        d_hidden_ref[...] = d_hidden
        g_gain_ref[...] = g_gain[None]
        low = d_hidden.astype(bf16)
        low_ref[...] = low
        d_mix_ref[...] = product(wo_ref[...], low, 1, 1).astype(bf16)


def feed_forward_back(grad, hidden, gain, gate, up, w_gate, w_up, w_down, w_o, kept):
    rows, model = grad.shape
    half = 1 if kept else 0
    hidden_units = gate.shape[1]
    tile = hidden_units // 4
    whole = lambda *shape: pl.BlockSpec(shape, lambda i: (0,) * len(shape))
    wide = lambda n: pl.BlockSpec((n, tile), lambda i: (0, i))
    return pl.pallas_call(
        feed_forward_back_kernel,
        grid=(4,),
        in_specs=[
            whole(rows, model), whole(rows, model), whole(1, model), wide(rows), wide(rows),
            wide(model), wide(model), pl.BlockSpec((tile, model), lambda i: (i, 0)),
            whole(model, model),
        ]
        + [pl.BlockSpec(memory_space=pl.ANY)] * len(kept),
        out_specs=[
            pl.BlockSpec((2, rows, tile), lambda i: (0, half, i)),
            whole(rows, model), whole(rows, model), whole(1, model), whole(model, rows),
        ],
        out_shape=[
            jax.ShapeDtypeStruct((2, 2 * rows, hidden_units), bf16),
            jax.ShapeDtypeStruct((rows, model), f32),
            jax.ShapeDtypeStruct((rows, model), bf16),
            jax.ShapeDtypeStruct((1, model), f32),
            jax.ShapeDtypeStruct((model, rows), bf16),
        ],
        scratch_shapes=[pltpu.VMEM((rows, model), f32)],
        input_output_aliases={9: 0} if kept else {},
        compiler_params=pltpu.CompilerParams(vmem_limit_bytes=48 * 2**20),
        name="feed_forward_back",
        cost_estimate=cost(18),
    )(grad, hidden, gain[None], gate, up, w_gate, w_up, w_down, w_o, *kept)


def projected(x, gain, w_kv, cosine, sine):
    normed, unit, scale = normalize(x, gain)
    kv = dot(normed, w_kv, "td,df->ft")
    kv = jnp.stack([rotary(kv[:KV], cosine, sine), kv[KV:]]).astype(bf16)
    return (normed, unit, scale), kv


def attention(normed, kv, w_q, where, tables, between):
    cosine, sine = tables
    count = lax.axis_size("fsdp")
    kvs = [kv]
    for step in range(1, count):
        kvs.append(climb(kvs[-1], step))
    q = rotary(dot(normed, w_q, "td,df->ft"), cosine, sine).astype(bf16) * bf16(HD**-0.5)
    state = []
    for d in range(count):
        state = attend(d, count, where, q, kvs[d], state)
        if d in between:
            between[d](state)
    return q, kvs, state


def attention_gradient(d_hidden, d_mixture, saved, weights, where, tables, between):
    gains, w_kv, w_q = weights[:3]
    (normed, unit, scale), q, kvs, (mixture, lse) = saved
    cosine, sine = tables
    count = lax.axis_size("fsdp")
    dq = moving = None
    for d in reversed(range(count)):
        step = count - 1 - d
        if step:
            got = lax.ppermute(
                moving, "fsdp", [(i, i - 1) for i in range(count - step, count)]
            )
        dq, dkv = attend_back(d, where, q, mixture, d_mixture, lse, kvs[d], dq)
        if d in between:
            dq = between[d](dq)
        moving = add(dkv, got) if step else dkv
    dkv = moving.astype(f32)
    dq = rotary(dq, cosine, -sine).astype(bf16)
    dkv = jnp.concatenate([rotary(dkv[0], cosine, -sine), dkv[1]]).astype(bf16)
    d_normed = dot(dq, w_q, "ft,df->td") + dot(dkv, w_kv, "ft,df->td")
    d_norm, g_gain = normalize_back(d_normed, gains[0], unit, scale)
    return d_hidden + d_norm, g_gain, dq, dkv


def local(
    tokens,
    lengths,
    cotangent,
    attention_gain,
    feedforward_gain,
    query_weight,
    key_weight,
    value_weight,
    out_weight,
    gate_weight,
    up_weight,
    down_weight,
):
    rows = tokens.shape[1]
    count = lax.axis_size("fsdp")
    z = lax.axis_index("fsdp")
    low, core, one, two = place()
    positions = z * rows + jnp.arange(rows, dtype=jnp.int32)
    length = lengths[0]
    where = jnp.stack([z, length - z * rows]).astype(jnp.int32)
    frequency = rotary_base ** (-jnp.arange(HD // 2, dtype=f32) * 2.0 / HD)
    angles = frequency[:, None] * positions.astype(f32)[None, :]
    tables = (jnp.cos(angles), jnp.sin(angles))
    block = query_weight.shape[0]
    model = block * count
    hidden_units = gate_weight.shape[1]

    own_gains = jnp.stack([attention_gain, feedforward_gain])
    gains = all_blocks(
        jnp.stack(
            [
                lax.ppermute(own_gains, "fsdp", [(i, (i - o) % count) for i in range(count)])
                for o in range(1, count)
            ]
        ),
        own_gains,
    )
    gains = jnp.moveaxis(gains, 0, 1).reshape(2, model).astype(f32)

    projections = jnp.concatenate([key_weight, value_weight, query_weight, out_weight], axis=1)
    lanes = projections.shape[1] // 4
    f_lanes = hidden_units // 4
    down_rows = down_weight.shape[0] // 8
    own = lax.optimization_barrier(
        (
            projection_piece(projections, low, core),
            gate_up_piece(gate_weight, up_weight, low, core),
            down_piece(down_weight, low),
        )
    )
    to_proj, to_gate_up, to_down = (Gather(v) for v in own)
    to_proj.hop()
    to_proj.hop_on()
    projections = whole_projections(projections, low, to_proj.cross())
    w_kv, w_q, w_o = (
        projections[:, : 2 * KV],
        projections[:, 2 * KV : 2 * KV + model],
        projections[:, 2 * KV + model :],
    )

    start = tokens[0].astype(f32)
    norm_1, kv = projected(start, gains[0], w_kv, *tables)
    to_gate_up.hop(kv)
    to_down.hop(kv)
    saved_first = (norm_1,) + attention(
        norm_1[0], kv, w_q, where, tables, {0: to_gate_up.hop_on, 1: to_down.hop_on}
    )
    mixture = saved_first[3][0]
    w_down = whole_down(down_weight, low, to_down.cross(mixture))
    w_gate, w_up = whole_gate_up(gate_weight, up_weight, low, to_gate_up.cross(mixture))
    weights = (gains, w_kv, w_q, w_o, w_gate, w_up, w_down)
    middle, hidden_1, gate_1, up_1, *kept = feed_forward(
        start, mixture, w_o, gains[1], w_gate, w_up, w_down, []
    )

    norm_2, kv = projected(middle, gains[0], w_kv, *tables)
    saved_second = (norm_2,) + attention(norm_2[0], kv, w_q, where, tables, {})
    final, hidden_2, gate_2, up_2, nft, active = feed_forward(
        middle, saved_second[3][0], w_o, gains[1], w_gate, w_up, w_down, kept
    )

    real = (positions < length).astype(f32)
    gradient = cotangent[0].astype(f32) * real[:, None]
    down_back = (gradient.astype(bf16),)
    d_gu, d_hidden, low_2, g_ffn_2, d_mixture = feed_forward_back(
        gradient, hidden_2, gains[1], gate_2, up_2, w_gate, w_up, w_down, w_o, []
    )
    gradient, g_attn_2, dq_2, dkv_2 = attention_gradient(
        d_hidden, d_mixture, saved_second, weights, where, tables, {}
    )

    down_back = jnp.concatenate(down_back + (gradient.astype(bf16),))
    active = active.reshape(count, 8, down_rows, 2 * rows)

    def make_down(ids, got, first):
        return grad_pieces(
            ids, got, first, active, down_back,
            pl.BlockSpec((count, 1, down_rows, 2 * rows), lambda i, ids: (0, ids[i], 0, 0)),
            pl.BlockSpec((2 * rows, model), lambda i, ids: (0, 0)),
            (count, down_rows, model),
        )

    to_g_down = Reduction(low, make_down)
    gradient = after(gradient, to_g_down.send)
    d_gu, d_hidden, low_1, g_ffn_1, d_mixture = feed_forward_back(
        gradient, hidden_1, gains[1], gate_1, up_1, w_gate, w_up, w_down, w_o, [d_gu]
    )

    def make_gate_up(ids, got, first):
        return grad_pieces(
            ids, got, first, nft, d_gu,
            pl.BlockSpec((model, 2 * rows), lambda i, ids: (0, 0)),
            pl.BlockSpec((1, 2 * rows, f_lanes), lambda i, ids: (ids[i] % 2, 0, ids[i] // 2)),
            (count, block, f_lanes),
        )

    to_g_gate_up = Reduction(low, make_gate_up)
    to_g_down.hop()
    d_mixture = after(d_mixture, to_g_gate_up.send, to_g_down.away)

    def third(dq):
        to_g_gate_up.hop()
        to_g_down.stay()
        return after(dq, to_g_gate_up.away, to_g_down.home)

    def second(dq):
        to_g_gate_up.stay()
        return after(dq, to_g_gate_up.home)

    def first(dq):
        to_g_down.hop_on()
        return after(dq, to_g_down.far, to_g_down.near)

    def zeroth(dq):
        to_g_down.shift()
        to_g_gate_up.hop_on()
        return after(dq, to_g_down.cuts, to_g_gate_up.far, to_g_gate_up.near)

    gradient, g_attn_1, dq_1, dkv_1 = attention_gradient(
        d_hidden, d_mixture, saved_first, weights, where, tables,
        {3: third, 2: second, 1: first, 0: zeroth},
    )
    to_g_gate_up.shift()

    def put_down(refs, q, c, pid, value):
        refs[0][pl.ds(pl.multiple_of(pid * down_rows, 8), down_rows), :] = value

    def put_gate_up(refs, q, c, pid, value):
        refs[c][:, lanes_at(q * f_lanes, f_lanes)] = value

    g_down = spread(low, to_g_down.give(), [(8 * down_rows, model)], put_down)[0]
    g_gate, g_up = spread(
        low, to_g_gate_up.give(), [(block, hidden_units)] * 2, put_gate_up
    )

    def both(pattern, a, b):
        return dot(a[0], b[0], pattern) + dot(a[1], b[1], pattern)

    g_proj = jnp.concatenate(
        [
            both("td,ft->df", (norm_1[0], norm_2[0]), (dkv_1, dkv_2)),
            both("td,ft->df", (norm_1[0], norm_2[0]), (dq_1, dq_2)),
            both("ft,td->fd", (mixture, saved_second[3][0]), (low_1, low_2)),
        ],
        axis=1,
    ).astype(bf16)
    half_rows = block // 2
    g_proj = g_proj.reshape(count, 2, half_rows, 4 * lanes)

    def make_proj(ids, got, first):
        pieces = []
        for i in ids:
            half = lax.dynamic_index_in_dim(g_proj, i % 2, 1, keepdims=False)
            pieces.append(lax.dynamic_slice_in_dim(half, i // 2 * lanes, lanes, 2))
        pieces = jnp.stack(pieces)
        return pieces if got is None else add(pieces, got[first : first + len(ids)])

    def put_proj(refs, q, c, pid, value):
        refs[0][c * half_rows : (c + 1) * half_rows, lanes_at(q * lanes, lanes)] = value

    to_g_proj = Reduction(low, make_proj)
    to_g_proj.hop()
    to_g_proj.stay()
    to_g_proj.hop_on()
    to_g_proj.shift()
    g_proj = spread(low, to_g_proj.give(), [(block, 4 * lanes)], put_proj)[0]

    g_gains = jnp.stack([g_attn_1 + g_attn_2, (g_ffn_1 + g_ffn_2)[0]])
    for hop in (sibling, first_hop, second_hop):
        g_gains = g_gains + swap(g_gains, hop)
    wide = lax.axis_size("dp")
    if wide > 8:
        groups = [[i + 8 * k for k in range(wide // 8)] for i in range(8)]
        g_gains = lax.psum(g_gains, "dp", axis_index_groups=groups)
    cut = g_gains.reshape(2, count, block)
    g_gains = lax.dynamic_index_in_dim(cut, z, 1, keepdims=False)
    for o in range(1, count):
        g_gains = g_gains + around(
            lax.dynamic_index_in_dim(cut, (z + o) % count, 1, keepdims=False), o
        )

    return (
        final.astype(bf16)[None],
        gradient.astype(bf16)[None],
        g_gains[0],
        g_gains[1],
        g_proj[:, 2 * KV : 2 * KV + model],
        g_proj[:, :KV],
        g_proj[:, KV : 2 * KV],
        g_proj[:, 2 * KV + model :],
        g_gate,
        g_up,
        g_down,
    )


def solution(mesh):
    rows = P("fsdp", None)
    placed = (P("dp", "fsdp", None), P("dp"), P("dp", "fsdp", None), P("fsdp"), P("fsdp")) + (
        rows,
    ) * 7
    return jax.shard_map(
        local,
        mesh=mesh,
        in_specs=placed,
        out_specs=(P("dp", "fsdp", None), P("dp", "fsdp", None), P("fsdp"), P("fsdp"))
        + (rows,) * 7,
        check_vma=False,
    )
```

```python
import jax
import jax.numpy as jnp
from jax import lax
from jax.experimental import pallas as pl
from jax.experimental.pallas import tpu as pltpu
from jax.sharding import PartitionSpec as P

HEADS = 15
KV_HEADS = 5
HD = 64
GROUP = HEADS // KV_HEADS
KV = KV_HEADS * HD

norm_epsilon = 1e-05
rotary_base = 10000.0

bf16 = jnp.bfloat16
f32 = jnp.float32


def first_hop(i):
    return i ^ (4 if i & 1 else 2)


def second_hop(i):
    return i ^ (2 if i & 1 else 4)


def sibling(i):
    return i ^ 1


def swap(value, hop):
    count = lax.axis_size("dp")
    return lax.ppermute(value, "dp", [(i, hop(i)) for i in range(count)])


def climb(value, step):
    count = lax.axis_size("fsdp")
    return lax.ppermute(value, "fsdp", [(i, i + 1) for i in range(step - 1, count - 1)])


def descend(value, step):
    count = lax.axis_size("fsdp")
    return lax.ppermute(value, "fsdp", [(i, i - 1) for i in range(1, count - step + 1)])


def place():
    low = lax.axis_index("dp") % 8
    core = low % 2
    one = jnp.where(core == 1, 4, 2)
    return low, core, one, 6 - one


def around(value, distance):
    count = lax.axis_size("fsdp")
    return lax.ppermute(value, "fsdp", [(i, (i + distance) % count) for i in range(count)])


def after(value, *first):
    return lax.optimization_barrier((value, first))[0]


class Gather:
    def __init__(self, blocks):
        self.blocks = blocks

    def hop(self, *first):
        self.mine = jnp.stack(after(self.blocks, *first))
        self.a = swap(self.mine, first_hop)
        self.b = swap(self.mine, second_hop)

    def hop_on(self, state=()):
        self.a = after(self.a, state)
        self.ab = swap(self.a, second_hop)
        return state

    def cross(self, *first):
        b, ab = after((self.b, self.ab), *first)
        mine = [self.mine, self.a, b, ab]
        return mine + [swap(v, sibling) for v in mine]


def other_blocks(own):
    return [around(own, o) for o in range(1, lax.axis_size("fsdp"))]


def piece_ids(low):
    odd = low % 2
    one = 2 + 2 * odd
    two = 6 - one
    return [low, low ^ one, low ^ two, low ^ 6, low ^ 1, low ^ 1 ^ two, low ^ 1 ^ one, low ^ 7]


def lay_out(low, pieces, own, out_shapes, moves):
    count = lax.axis_size("fsdp")
    where = jnp.stack([lax.axis_index("fsdp"), low]).astype(jnp.int32)

    def kernel(where_ref, *refs):
        piece_refs, refs = refs[:8], refs[8:]
        own_refs, refs = refs[: len(own)], refs[len(own) :]
        outs, sem = refs[:-1], refs[-1]
        z, low = where_ref[0], where_ref[1]
        for core in range(2):

            @pl.when(low % 2 == core)
            def _():
                copies = []
                for k, pid in enumerate(piece_ids(low)):
                    own_core = core if k < 4 else 1 - core
                    for o in range(count - 1):
                        block = lax.rem(z + count - 1 - o, count)
                        copies += moves(piece_refs[k].at[o], block, pid // 2, own_core, pid, outs)
                copies += own_moves(own_refs, z, outs)
                handles = [
                    pltpu.make_async_copy(src, dst, sem.at[i])
                    for i, (src, dst) in enumerate(copies)
                ]
                for h in handles:
                    h.start()
                for h in handles:
                    h.wait()

    moves, own_moves = moves
    any_spec = pl.BlockSpec(memory_space=pl.ANY)
    return pl.pallas_call(
        kernel,
        in_specs=[pl.BlockSpec(memory_space=pltpu.SMEM)] + [any_spec] * (8 + len(own)),
        out_specs=[pl.BlockSpec(memory_space=pltpu.VMEM)] * len(out_shapes),
        out_shape=[jax.ShapeDtypeStruct(shape, bf16) for shape in out_shapes],
        scratch_shapes=[pltpu.SemaphoreType.DMA((8 * (count - 1) + len(own),))],
        compiler_params=pltpu.CompilerParams(vmem_limit_bytes=40 * 2**20),
        name="lay_out",
        cost_estimate=cost(5),
    )(where, *pieces, *own)


def rows_at(start, size):
    return pl.ds(pl.multiple_of(start, 16), size)


def lanes_at(start, size):
    return pl.ds(pl.multiple_of(start, 128), size)


def projection_piece(shard, low, core):
    block, width = shard.shape
    rest = block // 2 // 16 * 16
    lanes = width // 4
    return lax.dynamic_slice(shard, (core * rest, low // 2 * lanes), (block - rest, lanes))


def gate_up_piece(gate, up, low, core):
    lanes = gate.shape[1] // 4
    gate, up = (lax.dynamic_slice_in_dim(v, low // 2 * lanes, lanes, 1) for v in (gate, up))
    return jnp.where(core == 1, up, gate)


def down_piece(shard, low):
    rows = shard.shape[0] // 8
    return lax.dynamic_slice_in_dim(shard, low * rows, rows, 0)


def whole_projections(shard, low, pieces):
    count = lax.axis_size("fsdp")
    block, width = shard.shape
    lanes = width // 4
    rest = block // 2 // 16 * 16
    held = block - rest

    def moves(src, z, q, c, pid, outs):
        size = held if c else rest
        return [
            (
                src.at[pl.ds(0, size)],
                outs[0].at[rows_at(z * block + c * rest, size), lanes_at(q * lanes, lanes)],
            )
        ]

    def own_moves(refs, z, outs):
        return [(refs[0], outs[0].at[rows_at(z * block, block)])]

    return lay_out(low, pieces, [shard], [(count * block, width)], (moves, own_moves))[0]


def whole_gate_up(gate, up, low, pieces):
    count = lax.axis_size("fsdp")
    block, width = gate.shape
    lanes = width // 4

    def moves(src, z, q, c, pid, outs):
        return [(src, outs[c].at[rows_at(z * block, block), lanes_at(q * lanes, lanes)])]

    def own_moves(refs, z, outs):
        return [(refs[k], outs[k].at[rows_at(z * block, block)]) for k in range(2)]

    return lay_out(low, pieces, [gate, up], [(count * block, width)] * 2, (moves, own_moves))


def whole_down(shard, low, pieces):
    count = lax.axis_size("fsdp")
    block, width = shard.shape
    rows = block // 8

    def moves(src, z, q, c, pid, outs):
        return [(src, outs[0].at[rows_at(z * block + pid * rows, rows)])]

    def own_moves(refs, z, outs):
        return [(refs[0], outs[0].at[rows_at(z * block, block)])]

    return lay_out(low, pieces, [shard], [(count * block, width)], (moves, own_moves))[0]


def all_blocks(others, own):
    count = lax.axis_size("fsdp")
    z = lax.axis_index("fsdp")
    both = jnp.concatenate([own[None], others])
    return jnp.stack(
        [
            lax.dynamic_index_in_dim(both, (k - z + count) % count, 0, keepdims=False)
            for k in range(count)
        ]
    )


def add(a, b):
    return (a.astype(f32) + b.astype(f32)).astype(bf16)


def cost(us):
    return pl.CostEstimate(flops=int(us * 2e10), bytes_accessed=0, transcendentals=0)


class Reduction:
    def __init__(self, low, make):
        self.low, self.make = low, make
        self.one = 2 + 2 * (low % 2)
        self.two = 6 - self.one
        other = low ^ 1
        self.send = make([other ^ self.two, other ^ 6, other, other ^ self.one], None)
        self.got = swap(self.send, sibling)

    def hop(self):
        low = self.low
        self.away, self.home = self.make(
            [low ^ self.one, low ^ 6, low, low ^ self.two], self.got
        )
        self.came = swap(self.away, first_hop)

    def hop_on(self, *first):
        came = after(self.came, *first)
        self.far = add(self.home[1], came[1])
        self.near = add(self.home[0], came[0])
        self.came = swap(self.far, second_hop)

    def shift(self, *first):
        count, z = lax.axis_size("fsdp"), lax.axis_index("fsdp")
        self.near = add(self.near, after(self.came, *first))
        self.cuts = [
            lax.dynamic_index_in_dim(self.near, (z + o) % count, 0, keepdims=False)
            for o in range(count)
        ]
        self.came = [around(self.cuts[o], o) for o in range(1, count)]

    def total(self, *first):
        came = after(self.came, *first)
        total = sum((v.astype(f32) for v in came), self.cuts[0].astype(f32))
        self.mine = total.astype(bf16)

    def hand(self):
        mine = self.mine
        wide = lax.axis_size("dp")
        if wide > 8:
            groups = [[i + 8 * k for k in range(wide // 8)] for i in range(8)]
            mine = lax.psum(mine, "dp", axis_index_groups=groups)
        b = swap(mine, second_hop)
        a, ab = swap(mine, first_hop), swap(b, first_hop)
        self.handed = [mine, a, b, ab]

    def give(self):
        return self.handed + [swap(v, sibling) for v in self.handed]


def spread(low, pieces, out_shapes, put):
    def kernel(where_ref, *refs):
        low = where_ref[0]
        for core in range(2):

            @pl.when(low % 2 == core)
            def _():
                for k, pid in enumerate(piece_ids(low)):
                    own_core = core if k < 4 else 1 - core
                    put(refs[8:], pid // 2, own_core, pid, refs[k][...].astype(f32))

    vmem = pl.BlockSpec(memory_space=pltpu.VMEM)
    return pl.pallas_call(
        kernel,
        in_specs=[pl.BlockSpec(memory_space=pltpu.SMEM)] + [vmem] * 8,
        out_specs=[vmem] * len(out_shapes),
        out_shape=[jax.ShapeDtypeStruct(shape, f32) for shape in out_shapes],
        compiler_params=pltpu.CompilerParams(vmem_limit_bytes=40 * 2**20),
        name="spread",
        cost_estimate=cost(3),
    )(low[None], *pieces)


def grad_pieces(ids, got, operands, in_specs, compute, piece_shape, us):
    block = (1,) + piece_shape
    zeros = (0,) * len(piece_shape)
    in_specs, operands = list(in_specs), list(operands)
    n = len(ids)
    if got is None:
        out_specs = pl.BlockSpec(block, lambda i, ids: (i,) + zeros)
        out_shape = jax.ShapeDtypeStruct((n,) + piece_shape, bf16)
    else:
        in_specs.append(pl.BlockSpec(block, lambda i, ids: (i,) + zeros))
        operands.append(got)
        half = n // 2
        out_specs = [
            pl.BlockSpec(block, lambda i, ids: (jnp.minimum(i, half - 1),) + zeros),
            pl.BlockSpec(block, lambda i, ids: (jnp.maximum(i - half, 0),) + zeros),
        ]
        out_shape = [jax.ShapeDtypeStruct((half,) + piece_shape, bf16)] * 2

    def kernel(ids_ref, *refs):
        step = pl.program_id(0)
        if got is None:

            def put(total):
                refs[-1][...] = total.astype(bf16).reshape(block)

            compute(ids_ref[step], put, *refs[:-1])
        else:

            def put(total):
                total = (total + refs[-3][...].reshape(total.shape).astype(f32)).astype(bf16)

                @pl.when(step < half)
                def _():
                    refs[-2][...] = total.reshape(block)

                @pl.when(step >= half)
                def _():
                    refs[-1][...] = total.reshape(block)

            compute(ids_ref[step], put, *refs[:-3])

    return pl.pallas_call(
        kernel,
        grid_spec=pltpu.PrefetchScalarGridSpec(
            num_scalar_prefetch=1, grid=(n,), in_specs=in_specs, out_specs=out_specs
        ),
        out_shape=out_shape,
        compiler_params=pltpu.CompilerParams(vmem_limit_bytes=56 * 2**20),
        name="weight_grad",
        cost_estimate=cost(us * n),
    )(jnp.stack(ids).astype(jnp.int32), *operands)


def flat_product(pid, put, left_ref, right_ref):
    left, right = left_ref[...], right_ref[...]
    put(product(left.reshape(-1, left.shape[-1]), right.reshape(right.shape[-2:]), 1, 0))


def product(a, b, over_a, over_b):
    return lax.dot_general(
        a, b, (((over_a,), (over_b,)), ((), ())), preferred_element_type=f32
    )


def side_by_side(x):
    return jnp.concatenate([x[HD * g : HD * (g + 1)] for g in range(GROUP)], axis=1)


def diagonal_mask(scores, rows, room):
    key = lax.broadcasted_iota(jnp.int32, (rows, rows), 0)
    query = lax.broadcasted_iota(jnp.int32, (rows, rows), 1)
    seen = (key <= query) & (key < room)
    return jnp.where(jnp.concatenate([seen] * GROUP, axis=1), scores, -1e30)


SUMS = 16


def attend_kernel(d, n, place_ref, q_ref, kv_ref, *refs):
    first, last = d == 0, d == n - 1
    m1_ref, a1_ref = (None, None) if first else refs[:2]
    m2_ref, a2_ref = refs[-2:]
    z, room = place_ref[0], place_ref[1]
    rows = q_ref.shape[1]

    @pl.when(z >= d)
    def _():
        ones = jnp.ones((SUMS, rows), bf16)
        for h in range(KV_HEADS):
            q = side_by_side(q_ref[GROUP * HD * h : GROUP * HD * (h + 1), :])
            k, v = (kv_ref[i, HD * h : HD * (h + 1), :] for i in range(2))
            s = product(k, q, 0, 0)
            if first:
                s = diagonal_mask(s, rows, room)
            m = jnp.max(s, axis=0, keepdims=True)
            if not first:
                m = jnp.maximum(m, m1_ref[h])
            p = jnp.exp(s - m).astype(bf16)
            total = product(jnp.concatenate([v, ones], axis=0), p, 1, 0)
            if not first:
                total = total + a1_ref[h] * jnp.exp(m1_ref[h] - m)
            m2_ref[h] = m
            a2_ref[h] = total

    if not first:

        @pl.when(z < d)
        def _():
            m2_ref[...] = m1_ref[...]
            a2_ref[...] = a1_ref[...]

    if last:
        o_ref, lse_ref = refs[2:4]
        for h in range(KV_HEADS):
            l = a2_ref[h, HD : HD + 1, :]
            o = (a2_ref[h, :HD, :] / l).astype(bf16)
            lse = m2_ref[h] + jnp.log(l)
            for g in range(GROUP):
                here = slice(HD * (GROUP * h + g), HD * (GROUP * h + g + 1))
                o_ref[here, :] = o[:, rows * g : rows * (g + 1)]
                lse_ref[h, g : g + 1, :] = lse[:, rows * g : rows * (g + 1)]


def attend(d, n, where, q, kv, state):
    rows = q.shape[1]
    state_shapes = [(KV_HEADS, 1, GROUP * rows), (KV_HEADS, HD + SUMS, GROUP * rows)]
    out_shape = [jax.ShapeDtypeStruct(shape, f32) for shape in state_shapes]
    scratch = []
    if d == n - 1:
        scratch = [pltpu.VMEM(shape, f32) for shape in state_shapes]
        out_shape = [
            jax.ShapeDtypeStruct(q.shape, bf16),
            jax.ShapeDtypeStruct((KV_HEADS, GROUP, rows), f32),
        ]
    vmem = pl.BlockSpec(memory_space=pltpu.VMEM)
    return pl.pallas_call(
        lambda *refs: attend_kernel(d, n, *refs),
        in_specs=[pl.BlockSpec(memory_space=pltpu.SMEM)] + [vmem] * (2 + len(state)),
        out_specs=[vmem, vmem],
        out_shape=out_shape,
        scratch_shapes=scratch,
        compiler_params=pltpu.CompilerParams(vmem_limit_bytes=40 * 2**20),
        name="attend",
        cost_estimate=cost(4),
    )(where, q, kv, *state)


def specs(rows):
    return (
        pl.BlockSpec((GROUP * HD, rows), lambda h, s: (h, 0)),
        pl.BlockSpec((2, HD, rows), lambda h, s: (0, h, 0)),
        pl.BlockSpec((1, GROUP, rows), lambda h, s: (h, 0, 0)),
    )


def attend_back_kernel(d, place_ref, q_ref, o_ref, do_ref, lse_ref, kv_ref, *refs):
    before_ref = refs[0] if len(refs) == 3 else None
    dq_ref, dkv_ref = refs[-2:]
    z, room = place_ref[0], place_ref[1]
    rows = q_ref.shape[1]

    @pl.when(z >= d)
    def _():
        q, do, o = (side_by_side(r[...]) for r in (q_ref, do_ref, o_ref))
        lse = jnp.concatenate([lse_ref[0, g : g + 1, :] for g in range(GROUP)], axis=1)
        delta = jnp.sum(do.astype(f32) * o.astype(f32), axis=0, keepdims=True)
        k, v = kv_ref[0], kv_ref[1]
        s = product(k, q, 0, 0)
        if d == 0:
            s = diagonal_mask(s, rows, room)
        p = jnp.exp(s - lse)
        dp = product(v, do, 0, 0)
        ds = (p * (dp - delta)).astype(bf16)
        dkv_ref[1] = product(p.astype(bf16), do, 1, 1).T.astype(bf16)
        dkv_ref[0] = product(ds, q, 1, 1).T.astype(bf16)
        dq = product(k, ds, 1, 0) * HD ** (-0.5)
        for g in range(GROUP):
            here = slice(HD * g, HD * (g + 1))
            part = dq[:, rows * g : rows * (g + 1)]
            dq_ref[here, :] = part if before_ref is None else part + before_ref[here, :]

    @pl.when(z < d)
    def _():
        dkv_ref[...] = jnp.zeros(dkv_ref.shape, bf16)
        if before_ref is None:
            dq_ref[...] = jnp.zeros(dq_ref.shape, f32)
        else:
            dq_ref[...] = before_ref[...]


def attend_back(d, where, q, o, do, lse, kv, before):
    rows = q.shape[1]
    q_spec, kv_spec, lse_spec = specs(rows)
    carried = [] if before is None else [before]
    return pl.pallas_call(
        lambda *refs: attend_back_kernel(d, *refs),
        grid_spec=pltpu.PrefetchScalarGridSpec(
            num_scalar_prefetch=1,
            grid=(KV_HEADS,),
            in_specs=[q_spec, q_spec, q_spec, lse_spec, kv_spec] + [q_spec] * len(carried),
            out_specs=[q_spec, kv_spec],
        ),
        out_shape=[jax.ShapeDtypeStruct(q.shape, f32), jax.ShapeDtypeStruct(kv.shape, bf16)],
        compiler_params=pltpu.CompilerParams(vmem_limit_bytes=40 * 2**20),
        name="attend_back",
        cost_estimate=cost(7),
    )(where, q, o, do, lse, kv, *carried)


def dot(a, b, pattern):
    return jnp.einsum(pattern, a, b, preferred_element_type=f32)


def rotary(columns, cosine, sine):
    heads = columns.shape[0] // HD
    halves = columns.reshape(heads, 2, HD // 2, columns.shape[1])
    a, b = halves[:, 0], halves[:, 1]
    return jnp.stack([a * cosine - b * sine, b * cosine + a * sine], axis=1).reshape(
        columns.shape
    )


def normalize(x, gain):
    scale = lax.rsqrt(jnp.mean(x * x, axis=-1, keepdims=True) + norm_epsilon)
    unit = x * scale
    return (unit * gain).astype(bf16), unit, scale


def normalize_back(grad, gain, unit, scale):
    grad_unit = grad * gain
    return (
        scale * (grad_unit - unit * jnp.mean(grad_unit * unit, axis=-1, keepdims=True)),
        jnp.sum(grad * unit, axis=0),
    )


def feed_forward_kernel(x_ref, mix_ref, wo_ref, gain_ref, wg_ref, wu_ref, wd_ref, *refs):
    result_ref, hidden_ref, gate_ref, up_ref, nft_ref, active_ref, nf_ref = refs[-7:]

    @pl.when(pl.program_id(0) == 0)
    def _():
        hidden = x_ref[...] + product(mix_ref[...], wo_ref[...], 0, 0)
        hidden_ref[...] = hidden
        normed, _, _ = normalize(hidden, gain_ref[...])
        nf_ref[...] = normed
        nft_ref[...] = normed.T
        result_ref[...] = hidden

    normed = nf_ref[...]
    gate = product(normed, wg_ref[...], 1, 0)
    up = product(normed, wu_ref[...], 1, 0)
    active = (gate * jax.nn.sigmoid(gate) * up).astype(bf16)
    gate_ref[...] = gate.astype(bf16)
    up_ref[...] = up.astype(bf16)
    active_ref[...] = active.T
    result_ref[...] += product(active, wd_ref[...], 1, 0)


def feed_forward(x, mixture, w_o, gain, w_gate, w_up, w_down, kept):
    rows, model = x.shape
    hidden_units = w_gate.shape[1]
    tile = hidden_units // 5
    half = 0 if kept else 1
    whole = lambda *shape: pl.BlockSpec(shape, lambda i: (0,) * len(shape))
    wide = lambda n: pl.BlockSpec((n, tile), lambda i: (0, i))
    return pl.pallas_call(
        feed_forward_kernel,
        grid=(5,),
        in_specs=[
            whole(rows, model), whole(model, rows), whole(model, model), whole(1, model),
            wide(model), wide(model), pl.BlockSpec((tile, model), lambda i: (i, 0)),
        ]
        + [pl.BlockSpec(memory_space=pl.ANY)] * len(kept),
        out_specs=[
            whole(rows, model), whole(rows, model), wide(rows), wide(rows),
            pl.BlockSpec((model, rows), lambda i: (0, half)),
            pl.BlockSpec((tile, rows), lambda i: (i, half)),
        ],
        out_shape=[
            jax.ShapeDtypeStruct((rows, model), f32),
            jax.ShapeDtypeStruct((rows, model), f32),
            jax.ShapeDtypeStruct((rows, hidden_units), bf16),
            jax.ShapeDtypeStruct((rows, hidden_units), bf16),
            jax.ShapeDtypeStruct((model, 2 * rows), bf16),
            jax.ShapeDtypeStruct((hidden_units, 2 * rows), bf16),
        ],
        scratch_shapes=[pltpu.VMEM((rows, model), bf16)],
        input_output_aliases={7: 4, 8: 5} if kept else {},
        compiler_params=pltpu.CompilerParams(vmem_limit_bytes=48 * 2**20),
        name="feed_forward",
        cost_estimate=cost(12),
    )(x, mixture, w_o, gain[None], w_gate, w_up, w_down, *kept)


def feed_forward_back_kernel(grad_ref, hidden_ref, gain_ref, gate_ref, up_ref, wg_ref, wu_ref,
                             wd_ref, wo_ref, *refs):
    d_gu_ref, d_hidden_ref, low_ref, g_gain_ref, d_mix_ref, total_ref = refs[-6:]
    step = pl.program_id(0)
    low = grad_ref[...].astype(bf16)
    d_active = product(low, wd_ref[...], 1, 1)
    gate, up = gate_ref[...].astype(f32), up_ref[...].astype(f32)
    sig = jax.nn.sigmoid(gate)
    d_gate = (d_active * up * sig * (1.0 + gate * (1.0 - sig))).astype(bf16)
    d_up = (d_active * gate * sig).astype(bf16)
    d_gu_ref[0] = d_gate
    d_gu_ref[1] = d_up
    term = product(d_gate, wg_ref[...], 1, 1) + product(d_up, wu_ref[...], 1, 1)

    @pl.when(step == 0)
    def _():
        total_ref[...] = term

    @pl.when(step > 0)
    def _():
        total_ref[...] += term

    @pl.when(step == pl.num_programs(0) - 1)
    def _():
        hidden = hidden_ref[...]
        scale = lax.rsqrt(jnp.mean(hidden * hidden, axis=-1, keepdims=True) + norm_epsilon)
        d_norm, g_gain = normalize_back(total_ref[...], gain_ref[...], hidden * scale, scale)
        d_hidden = grad_ref[...] + d_norm
        d_hidden_ref[...] = d_hidden
        g_gain_ref[...] = g_gain[None]
        low = d_hidden.astype(bf16)
        low_ref[...] = low.T
        d_mix_ref[...] = product(wo_ref[...], low, 1, 1).astype(bf16)


def feed_forward_back(grad, hidden, gain, gate, up, w_gate, w_up, w_down, w_o, kept):
    rows, model = grad.shape
    half = 1 if kept else 0
    hidden_units = gate.shape[1]
    tile = hidden_units // 5
    whole = lambda *shape: pl.BlockSpec(shape, lambda i: (0,) * len(shape))
    wide = lambda n: pl.BlockSpec((n, tile), lambda i: (0, i))
    return pl.pallas_call(
        feed_forward_back_kernel,
        grid=(5,),
        in_specs=[
            whole(rows, model), whole(rows, model), whole(1, model), wide(rows), wide(rows),
            wide(model), wide(model), pl.BlockSpec((tile, model), lambda i: (i, 0)),
            whole(model, model),
        ]
        + [pl.BlockSpec(memory_space=pl.ANY)] * len(kept),
        out_specs=[
            pl.BlockSpec((2, rows, tile), lambda i: (0, half, i)),
            whole(rows, model), whole(model, rows), whole(1, model), whole(model, rows),
        ],
        out_shape=[
            jax.ShapeDtypeStruct((2, 2 * rows, hidden_units), bf16),
            jax.ShapeDtypeStruct((rows, model), f32),
            jax.ShapeDtypeStruct((model, rows), bf16),
            jax.ShapeDtypeStruct((1, model), f32),
            jax.ShapeDtypeStruct((model, rows), bf16),
        ],
        scratch_shapes=[pltpu.VMEM((rows, model), f32)],
        input_output_aliases={9: 0} if kept else {},
        compiler_params=pltpu.CompilerParams(vmem_limit_bytes=48 * 2**20),
        name="feed_forward_back",
        cost_estimate=cost(18),
    )(grad, hidden, gain[None], gate, up, w_gate, w_up, w_down, w_o, *kept)


def turn(columns, cosine, sine, heads):
    half = HD // 2
    parts = []
    for h in range(heads):
        a = columns[HD * h : HD * h + half]
        b = columns[HD * h + half : HD * (h + 1)]
        parts += [a * cosine - b * sine, b * cosine + a * sine]
    return jnp.concatenate(parts, axis=0)


def project(normed, w, first, lanes, cosine, sine, heads, scale, name):
    rows, model = normed.shape

    def kernel(x_ref, w_ref, cos_ref, sin_ref, out_ref):
        y = product(x_ref[...], w_ref[:, first : first + lanes], 1, 0).T
        turned = turn(y[: heads * HD], cos_ref[...], sin_ref[...], heads)
        out_ref[: heads * HD, :] = turned.astype(bf16) * bf16(scale)
        if heads * HD < lanes:
            out_ref[heads * HD :, :] = y[heads * HD :].astype(bf16)

    whole = lambda *shape: pl.BlockSpec(shape, lambda i: (0,) * len(shape))
    width = first + lanes if (first + lanes) % 128 == 0 else w.shape[1]
    return pl.pallas_call(
        kernel,
        grid=(1,),
        in_specs=[
            whole(rows, model), whole(model, width), whole(HD // 2, rows), whole(HD // 2, rows)
        ],
        out_specs=whole(lanes, rows),
        out_shape=jax.ShapeDtypeStruct((lanes, rows), bf16),
        compiler_params=pltpu.CompilerParams(vmem_limit_bytes=40 * 2**20),
        name=name,
        cost_estimate=cost(4),
    )(normed, w, cosine, sine)


def projected_kv(normed, projections, tables):
    kv = project(normed, projections, 0, 2 * KV, *tables, KV_HEADS, 1.0, "keys_values")
    return kv.reshape(2, KV, normed.shape[0])


def projected_q(normed, projections, tables):
    first, lanes = 2 * KV, HEADS * HD
    return project(normed, projections, first, lanes, *tables, HEADS, HD**-0.5, "queries")


def attention(normed, kv, projections, where, tables, between):
    count = lax.axis_size("fsdp")
    kvs = [kv]
    for step in range(1, count):
        kvs.append(climb(kvs[-1], step))
    q = projected_q(normed, projections, tables)
    if -1 in between:
        q = between[-1](q)
    state = []
    for d in range(count):
        state = attend(d, count, where, q, kvs[d], state)
        if d in between:
            state = between[d](state)
    return q, kvs, state


def attention_gradient(d_hidden, d_mixture, saved, weights, where, tables, between):
    gains, w_kv, w_q = weights[:3]
    (normed, unit, scale), q, kvs, (mixture, lse) = saved
    cosine, sine = tables
    count = lax.axis_size("fsdp")
    dq = moving = None
    for d in reversed(range(count)):
        step = count - 1 - d
        if step:
            got = lax.ppermute(
                moving, "fsdp", [(i, i - 1) for i in range(count - step, count)]
            )
        dq, dkv = attend_back(d, where, q, mixture, d_mixture, lse, kvs[d], dq)
        moving = add(dkv, got) if step else dkv
        if d in between:
            dq = between[d](dq)
        dq = after(dq, moving)
    dkv = moving.astype(f32)
    dq = rotary(dq, cosine, -sine).astype(bf16)
    dkv = jnp.concatenate([rotary(dkv[0], cosine, -sine), dkv[1]]).astype(bf16)
    d_normed = dot(dq, w_q, "ft,df->td") + dot(dkv, w_kv, "ft,df->td")
    d_norm, g_gain = normalize_back(d_normed, gains[0], unit, scale)
    return d_hidden + d_norm, g_gain, dq, dkv


def local(
    tokens,
    lengths,
    cotangent,
    attention_gain,
    feedforward_gain,
    query_weight,
    key_weight,
    value_weight,
    out_weight,
    gate_weight,
    up_weight,
    down_weight,
):
    rows = tokens.shape[1]
    count = lax.axis_size("fsdp")
    z = lax.axis_index("fsdp")
    low, core, one, two = place()
    positions = z * rows + jnp.arange(rows, dtype=jnp.int32)
    length = lengths[0]
    where = jnp.stack([z, length - z * rows]).astype(jnp.int32)
    frequency = rotary_base ** (-jnp.arange(HD // 2, dtype=f32) * 2.0 / HD)
    angles = frequency[:, None] * positions.astype(f32)[None, :]
    tables = (jnp.cos(angles), jnp.sin(angles))
    block = query_weight.shape[0]
    model = block * count
    hidden_units = gate_weight.shape[1]

    projections = jnp.concatenate([key_weight, value_weight, query_weight, out_weight], axis=1)
    lanes = projections.shape[1] // 4
    f_lanes = hidden_units // 4
    down_rows = down_weight.shape[0] // 8
    own_gains = jnp.stack([attention_gain, feedforward_gain])
    piece = projection_piece(projections, low, core)
    held = piece.shape[0]
    own = lax.optimization_barrier(
        (
            jnp.concatenate([piece, jnp.pad(own_gains, ((0, 14), (0, lanes - block)))]),
            gate_up_piece(gate_weight, up_weight, low, core),
            down_piece(down_weight, low),
        )
    )
    blocks = other_blocks(own[0])
    gains = all_blocks(jnp.stack([v[held : held + 2, :block] for v in blocks[::-1]]), own_gains)
    to_proj = Gather([v[:held] for v in blocks])
    to_proj.hop()
    rest = jnp.pad(own[2][:, f_lanes:], ((0, 0), (0, 2 * f_lanes - model)))
    wide = jnp.concatenate([own[1], own[2][:, :f_lanes], rest])
    wide = lax.all_gather(wide, "fsdp")
    wide = [
        lax.dynamic_index_in_dim(wide, (z + count - o) % count, 0, keepdims=False)
        for o in range(1, count)
    ]
    to_gate_up = Gather([v[:block] for v in wide])
    to_down = Gather(
        [
            jnp.concatenate(
                [v[block : block + down_rows], v[block + down_rows :, : model - f_lanes]], axis=1
            )
            for v in wide
        ]
    )
    to_gate_up.hop()
    to_down.hop()
    gains = jnp.moveaxis(gains, 0, 1).reshape(2, model).astype(f32)
    to_proj.hop_on()
    projections = whole_projections(
        projections, low, after(to_proj.cross(), to_gate_up.mine, to_down.mine)
    )
    w_kv, w_q = projections[:, : 2 * KV], projections[:, 2 * KV : 2 * KV + model]

    start = tokens[0].astype(f32)
    norm_1 = normalize(start, gains[0])
    normed = norm_1[0]
    kv = projected_kv(normed, projections, tables)

    def with_first_hop(state):
        to_gate_up.hop_on(state)
        to_down.hop_on(state)
        return after(state, to_gate_up.a, to_down.a)

    def with_second_hop(state):
        return after(state, to_gate_up.b, to_gate_up.ab, to_down.b, to_down.ab)

    saved_first = (norm_1,) + attention(
        normed, kv, projections, where, tables, {1: with_first_hop, 2: with_second_hop}
    )
    mixture = saved_first[3][0]
    w_o = after(projections, saved_first[1])[:, 2 * KV + model :]
    w_down = whole_down(down_weight, low, to_down.cross())
    w_gate, w_up = whole_gate_up(gate_weight, up_weight, low, to_gate_up.cross())
    weights = (gains, w_kv, w_q, w_o, w_gate, w_up, w_down)
    middle, hidden_1, gate_1, up_1, *kept = feed_forward(
        start, mixture, w_o, gains[1], w_gate, w_up, w_down, []
    )

    norm_2 = normalize(middle, gains[0])
    kv = projected_kv(norm_2[0], projections, tables)
    half_rows = block // 2

    def left_of(normed, mixture):
        return jnp.stack([normed.T, mixture]).reshape(2, count, 2, half_rows, rows)

    left_1 = left_of(norm_1[0], mixture)
    saved_second = (norm_2,) + attention(
        norm_2[0], kv, projections, where, tables, {0: lambda state: after(state, left_1)}
    )
    final, hidden_2, gate_2, up_2, nft, active = feed_forward(
        middle, saved_second[3][0], w_o, gains[1], w_gate, w_up, w_down, kept
    )

    real = (positions < length).astype(f32)
    gradient = cotangent[0].astype(f32) * real[:, None]
    down_back = (gradient.astype(bf16),)
    left = jnp.concatenate([left_of(norm_2[0], saved_second[3][0]), left_1], axis=-1)
    gradient, down_back = after((gradient, down_back), left)
    d_gu, d_hidden, low_2, g_ffn_2, d_mixture = feed_forward_back(
        gradient, hidden_2, gains[1], gate_2, up_2, w_gate, w_up, w_down, w_o, []
    )
    gradient, g_attn_2, dq_2, dkv_2 = attention_gradient(
        d_hidden, d_mixture, saved_second, weights, where, tables, {}
    )

    down_back = jnp.concatenate(down_back + (gradient.astype(bf16),))
    active = active.reshape(count, 8, down_rows, 2 * rows)

    def make_down(ids, got):
        return grad_pieces(
            ids, got, [active, down_back],
            [
                pl.BlockSpec((count, 1, down_rows, 2 * rows), lambda i, ids: (0, ids[i], 0, 0)),
                pl.BlockSpec((2 * rows, model), lambda i, ids: (0, 0)),
            ],
            flat_product, (count, down_rows, model), 1.4,
        )

    to_down = Reduction(low, make_down)
    to_down.hop()
    gradient = after(gradient, to_down.away)
    d_gu, d_hidden, low_1, g_ffn_1, d_mixture = feed_forward_back(
        gradient, hidden_1, gains[1], gate_1, up_1, w_gate, w_up, w_down, w_o, [d_gu]
    )

    def make_gate_up(ids, got):
        return grad_pieces(
            ids, got, [nft, d_gu],
            [
                pl.BlockSpec((model, 2 * rows), lambda i, ids: (0, 0)),
                pl.BlockSpec(
                    (1, 2 * rows, f_lanes), lambda i, ids: (ids[i] % 2, 0, ids[i] // 2)
                ),
            ],
            flat_product, (count, block, f_lanes), 2.2,
        )

    to_gate_up = Reduction(low, make_gate_up)
    to_down.hop_on(to_gate_up.send)
    d_mixture = after(d_mixture, to_gate_up.send, to_down.far, to_down.near)

    def third(dq):
        to_gate_up.hop()
        return after(dq, to_gate_up.away)

    def second(dq):
        to_down.shift(dq)
        return after(dq, to_down.cuts)

    def first(dq):
        to_gate_up.hop_on(dq)
        return after(dq, to_gate_up.far, to_gate_up.near)

    gradient, g_attn_1, dq_1, dkv_1 = attention_gradient(
        d_hidden, d_mixture, saved_first, weights, where, tables,
        {3: third, 2: second, 1: first},
    )

    right = [jnp.concatenate(v) for v in ((dkv_2, dq_2, low_2), (dkv_1, dq_1, low_1))]
    g_gains = jnp.stack([g_attn_1 + g_attn_2, (g_ffn_1 + g_ffn_2)[0]]).reshape(2, count, block)
    g_gains = jnp.pad(g_gains.transpose(1, 0, 2), ((0, 0), (0, 6), (0, lanes - block)))

    def compute_proj(pid, put, a, b, right_2, right_1, gains_ref):
        right = jnp.concatenate([right_2[...], right_1[...]], axis=1)

        def left_of(ref):
            return ref[...].reshape(count * half_rows, 2 * rows)

        def finish(total):
            total = total.reshape(count, half_rows, lanes)
            total = jnp.concatenate([total, gains_ref[...]], axis=1)
            put(total.reshape(-1, lanes))

        @pl.when(pid // 2 != 2)
        def _():
            finish(product(left_of(a), right, 1, 1))

        @pl.when(pid // 2 == 2)
        def _():
            finish(
                jnp.concatenate(
                    [
                        product(left_of(a), right[: lanes // 2], 1, 1),
                        product(left_of(b), right[lanes // 2 :], 1, 1),
                    ],
                    axis=1,
                )
            )

    def make_proj(ids, got):
        def left_spec(k):
            return pl.BlockSpec(
                (1, count, 1, half_rows, 2 * rows),
                lambda i, ids: (jnp.where(ids[i] // 2 * 2 + k > 4, 1, 0), 0, ids[i] % 2, 0, 0),
            )

        right_spec = pl.BlockSpec((lanes, rows), lambda i, ids: (ids[i] // 2, 0))
        return grad_pieces(
            ids, got, [left, left] + right + [g_gains],
            [left_spec(0), left_spec(1)]
            + [right_spec] * 2
            + [pl.BlockSpec((count, 8, lanes), lambda i, ids: (0, 0, 0))],
            compute_proj, (count, half_rows + 8, lanes), 1.4,
        )

    to_down.total(dq_1)
    to_down.hand()
    to_gate_up.shift(dq_1)
    right[1] = after(right[1], to_down.mine, to_gate_up.cuts)
    to_proj = Reduction(low, make_proj)
    to_proj.hop()
    g_down_pieces = after(to_down.give(), to_proj.away)
    to_proj.hop_on()
    to_proj.shift()
    to_gate_up.total(to_proj.far)
    to_gate_up.hand()
    to_proj.total()
    to_proj.hand()

    def put_down(refs, q, c, pid, value):
        refs[0][pl.ds(pl.multiple_of(pid * down_rows, 8), down_rows), :] = value

    def put_gate_up(refs, q, c, pid, value):
        refs[c][:, lanes_at(q * f_lanes, f_lanes)] = value

    def put_proj(refs, q, c, pid, value):
        refs[0][c * half_rows : (c + 1) * half_rows, lanes_at(q * lanes, lanes)] = value[
            :half_rows
        ]

    g_down = spread(
        low, g_down_pieces, [(8 * down_rows, model)], put_down
    )[0]
    g_gate, g_up = spread(
        low, to_gate_up.give(), [(block, hidden_units)] * 2, put_gate_up
    )
    pieces = to_proj.give()
    g_proj = spread(low, pieces, [(block, 4 * lanes)], put_proj)[0]
    g_gains = pieces[0][half_rows : half_rows + 2, :block].astype(f32)

    return (
        final.astype(bf16)[None],
        gradient.astype(bf16)[None],
        g_gains[0],
        g_gains[1],
        g_proj[:, 2 * KV : 2 * KV + model],
        g_proj[:, :KV],
        g_proj[:, KV : 2 * KV],
        g_proj[:, 2 * KV + model :],
        g_gate,
        g_up,
        g_down,
    )


def solution(mesh):
    rows = P("fsdp", None)
    placed = (P("dp", "fsdp", None), P("dp"), P("dp", "fsdp", None), P("fsdp"), P("fsdp")) + (
        rows,
    ) * 7
    return jax.shard_map(
        local,
        mesh=mesh,
        in_specs=placed,
        out_specs=(P("dp", "fsdp", None), P("dp", "fsdp", None), P("fsdp"), P("fsdp"))
        + (rows,) * 7,
        check_vma=False,
    )
```

```python
import jax
import jax.numpy as jnp
from jax import lax
from jax.experimental import pallas as pl
from jax.experimental.pallas import tpu as pltpu
from jax.sharding import PartitionSpec as P

HEADS = 15
KV_HEADS = 5
HD = 64
GROUP = HEADS // KV_HEADS
KV = KV_HEADS * HD

norm_epsilon = 1e-05
rotary_base = 10000.0

bf16 = jnp.bfloat16
f32 = jnp.float32


def first_hop(i):
    return i ^ (4 if i & 1 else 2)


def second_hop(i):
    return i ^ (2 if i & 1 else 4)


def sibling(i):
    return i ^ 1


def swap(value, hop):
    count = lax.axis_size("dp")
    return lax.ppermute(value, "dp", [(i, hop(i)) for i in range(count)])


def climb(value, step):
    count = lax.axis_size("fsdp")
    return lax.ppermute(value, "fsdp", [(i, i + 1) for i in range(step - 1, count - 1)])


def descend(value, step):
    count = lax.axis_size("fsdp")
    return lax.ppermute(value, "fsdp", [(i, i - 1) for i in range(1, count - step + 1)])


def place():
    low = lax.axis_index("dp") % 8
    core = low % 2
    one = jnp.where(core == 1, 4, 2)
    return low, core, one, 6 - one


def around(value, distance):
    count = lax.axis_size("fsdp")
    return lax.ppermute(value, "fsdp", [(i, (i + distance) % count) for i in range(count)])


def together(*values):
    return lax.optimization_barrier(values)


def call(kernel, operands, wait_for=(), scalars=0, in_specs=(), grid=(), **rest):
    wait_for = jax.tree.leaves(wait_for)
    last = len(operands)

    def waiting(*refs):
        kernel(*refs[:last], *refs[last + len(wait_for) :])

    in_specs = list(in_specs) + [pl.BlockSpec(memory_space=pl.ANY)] * len(wait_for)
    where = dict(in_specs=in_specs, out_specs=rest.pop("out_specs"))
    scratch = rest.pop("scratch_shapes", ())
    if scalars:
        where = dict(
            grid_spec=pltpu.PrefetchScalarGridSpec(
                num_scalar_prefetch=scalars, grid=grid, scratch_shapes=scratch, **where
            )
        )
    else:
        where.update(grid=grid, scratch_shapes=scratch)
    return pl.pallas_call(waiting, **where, **rest)(*operands, *wait_for)


class Gather:
    def __init__(self, blocks):
        self.blocks = blocks

    def hop(self):
        self.mine = jnp.stack(self.blocks)
        self.a = swap(self.mine, first_hop)
        self.b = swap(self.mine, second_hop)

    def hop_on(self):
        self.ab = swap(self.a, second_hop)

    def cross(self):
        mine = [self.mine, self.a, self.b, self.ab]
        return mine + [swap(v, sibling) for v in mine]


def other_blocks(own):
    return [around(own, o) for o in range(1, lax.axis_size("fsdp"))]


def piece_ids(low):
    odd = low % 2
    one = 2 + 2 * odd
    two = 6 - one
    return [low, low ^ one, low ^ two, low ^ 6, low ^ 1, low ^ 1 ^ two, low ^ 1 ^ one, low ^ 7]


def lay_out(low, pieces, own, out_shapes, moves, wait_for=()):
    count = lax.axis_size("fsdp")
    where = jnp.stack([lax.axis_index("fsdp"), low]).astype(jnp.int32)

    def kernel(where_ref, *refs):
        piece_refs, refs = refs[:8], refs[8:]
        own_refs, refs = refs[: len(own)], refs[len(own) :]
        outs = refs
        z, low = where_ref[0], where_ref[1]
        for core in range(2):

            @pl.when(low % 2 == core)
            def _():
                copies = []
                for k, pid in enumerate(piece_ids(low)):
                    own_core = core if k < 4 else 1 - core
                    for o in range(count - 1):
                        block = lax.rem(z + count - 1 - o, count)
                        copies += moves(piece_refs[k].at[o], block, pid // 2, own_core, pid, outs)
                for source, target in copies + own_moves(own_refs, z, outs):
                    target[...] = source[...]

    moves, own_moves = moves
    vmem = pl.BlockSpec(memory_space=pltpu.VMEM)
    return call(
        kernel,
        [where, *pieces, *own],
        wait_for,
        in_specs=[pl.BlockSpec(memory_space=pltpu.SMEM)] + [vmem] * (8 + len(own)),
        out_specs=[vmem] * len(out_shapes),
        out_shape=[jax.ShapeDtypeStruct(shape, bf16) for shape in out_shapes],
        compiler_params=pltpu.CompilerParams(vmem_limit_bytes=26 * 2**20),
        name="lay_out",
        cost_estimate=cost(5),
    )


def rows_at(start, size):
    return pl.ds(pl.multiple_of(start, 16), size)


def lanes_at(start, size):
    return pl.ds(start if isinstance(start, int) else pl.multiple_of(start, 128), size)


def projection_piece(shard, low, core):
    block, width = shard.shape
    rest = block // 2 // 16 * 16
    lanes = width // 4
    return lax.dynamic_slice(shard, (core * rest, low // 2 * lanes), (block - rest, lanes))


def gate_up_piece(gate, up, low, core):
    lanes = gate.shape[1] // 4
    gate, up = (lax.dynamic_slice_in_dim(v, low // 2 * lanes, lanes, 1) for v in (gate, up))
    return jnp.where(core == 1, up, gate)


def down_piece(shard, low):
    rows = shard.shape[0] // 8
    return lax.dynamic_slice_in_dim(shard, low * rows, rows, 0)


def whole_projections(shard, low, pieces, wait_for):
    count = lax.axis_size("fsdp")
    block, width = shard.shape
    lanes = width // 4
    rest = block // 2 // 16 * 16
    held = block - rest

    def moves(src, z, q, c, pid, outs):
        size = held if c else rest
        return [
            (
                src.at[pl.ds(0, size)],
                outs[0].at[rows_at(z * block + c * rest, size), lanes_at(q * lanes, lanes)],
            )
        ]

    def own_moves(refs, z, outs):
        return [(refs[0], outs[0].at[rows_at(z * block, block)])]

    return lay_out(
        low, pieces, [shard], [(count * block, width)], (moves, own_moves), wait_for
    )[0]


def whole_gate_up(gate, up, low, pieces):
    count = lax.axis_size("fsdp")
    block, width = gate.shape
    lanes = width // 4

    def moves(src, z, q, c, pid, outs):
        return [(src, outs[c].at[rows_at(z * block, block), lanes_at(q * lanes, lanes)])]

    def own_moves(refs, z, outs):
        return [(refs[k], outs[k].at[rows_at(z * block, block)]) for k in range(2)]

    return lay_out(low, pieces, [gate, up], [(count * block, width)] * 2, (moves, own_moves))


def whole_down(shard, low, pieces):
    count = lax.axis_size("fsdp")
    block, width = shard.shape
    rows = block // 8

    def moves(src, z, q, c, pid, outs):
        return [(src, outs[0].at[rows_at(z * block + pid * rows, rows)])]

    def own_moves(refs, z, outs):
        return [(refs[0], outs[0].at[rows_at(z * block, block)])]

    return lay_out(low, pieces, [shard], [(count * block, width)], (moves, own_moves))[0]


def all_blocks(others, own):
    count = lax.axis_size("fsdp")
    z = lax.axis_index("fsdp")
    both = jnp.concatenate([own[None], others])
    return jnp.stack(
        [
            lax.dynamic_index_in_dim(both, (k - z + count) % count, 0, keepdims=False)
            for k in range(count)
        ]
    )


def add(*terms):
    return sum(v.astype(f32) for v in terms).astype(bf16)


def cost(us, weight=20):
    return pl.CostEstimate(
        flops=int(us * weight * 1.15e9), bytes_accessed=0, transcendentals=0
    )


HEAVY = 20


class Reduction:
    def __init__(self, send):
        self.got = swap(send, sibling)

    def hop(self, away, near, far):
        self.near, self.far = near, far
        self.came = swap(away, first_hop)

    def hop_on(self):
        self.add_up()
        self.go_on()

    def add_up(self):
        self.far = add(*self.far, self.came[1])
        self.near = add(*self.near, self.came[0])

    def go_on(self):
        self.came = swap(self.far, second_hop)

    def settle(self):
        count, z = lax.axis_size("fsdp"), lax.axis_index("fsdp")
        self.near = add(self.near, self.came)
        self.cuts = [
            lax.dynamic_index_in_dim(self.near, (z + o) % count, 0, keepdims=False)
            for o in range(count)
        ]

    def shift(self):
        count = lax.axis_size("fsdp")
        self.came = [around(self.cuts[o], o) for o in range(1, count)]

    def total(self):
        return over_rest(add(self.cuts[0], *self.came))


def over_rest(mine):
    wide = lax.axis_size("dp")
    if wide > 8:
        groups = [[i + 8 * k for k in range(wide // 8)] for i in range(8)]
        mine = lax.psum(mine, "dp", axis_index_groups=groups)
    return mine


def hand(mine):
    b = swap(mine, second_hop)
    a, ab = swap(mine, first_hop), swap(b, first_hop)
    return [mine, a, b, ab]


def give(handed):
    return handed + [swap(v, sibling) for v in handed]


def ids_of(low):
    one = 2 + 2 * (low % 2)
    return [low ^ one, low ^ 6, low, low ^ 6 ^ one]


def spread(low, pieces, out_shapes, put, wait_for=()):
    def turn_out(shape):
        wide, high = (-(-n // 128) * 128 for n in shape[::-1])
        return shape[0] * wide > shape[1] * high

    def kernel(where_ref, *refs):
        low = where_ref[0]
        outs, rest = list(refs[8 : 8 + len(out_shapes)]), list(refs[8 + len(out_shapes) :])
        targets = [rest.pop(0) if turn_out(s) else v for s, v in zip(out_shapes, outs)]
        for core in range(2):

            @pl.when(low % 2 == core)
            def _():
                for k, pid in enumerate(piece_ids(low)):
                    own_core = core if k < 4 else 1 - core
                    put(targets, pid // 2, own_core, pid, refs[k][...].astype(f32))

        for target, out in zip(targets, outs):
            if target is not out:
                out[...] = target[...].T

    vmem = pl.BlockSpec(memory_space=pltpu.VMEM)
    turned = [turn_out(shape) for shape in out_shapes]
    shapes = [shape[::-1] if t else shape for shape, t in zip(out_shapes, turned)]
    out = call(
        kernel,
        [low[None], *pieces],
        wait_for,
        in_specs=[pl.BlockSpec(memory_space=pltpu.SMEM)] + [vmem] * 8,
        out_specs=[vmem] * len(out_shapes),
        out_shape=[jax.ShapeDtypeStruct(shape, f32) for shape in shapes],
        scratch_shapes=[pltpu.VMEM(s, f32) for s, t in zip(out_shapes, turned) if t],
        compiler_params=pltpu.CompilerParams(vmem_limit_bytes=22 * 2**20),
        name="spread",
        cost_estimate=cost(3),
    )
    return [v.T if t else v for v, t in zip(out, turned)]


def grad_pieces(
    ids, got, operands, in_specs, compute, piece_shape, us, wait_for, vmem=56
):
    block = (1,) + piece_shape
    zeros = (0,) * len(piece_shape)
    in_specs, operands = list(in_specs), list(operands)
    n = len(ids)
    if got is None:
        out_specs = [pl.BlockSpec(block, lambda i, ids: (i,) + zeros)]
        out_shape = [jax.ShapeDtypeStruct((n,) + piece_shape, bf16)]
    else:
        in_specs.append(pl.BlockSpec(block, lambda i, ids: (i,) + zeros))
        operands.append(got)
        half = n // 2
        out_specs = [
            pl.BlockSpec(block, lambda i, ids: (jnp.minimum(i, half - 1),) + zeros),
            pl.BlockSpec(block, lambda i, ids: (jnp.maximum(i - half, 0),) + zeros),
        ]
        out_shape = [jax.ShapeDtypeStruct((half,) + piece_shape, bf16)] * 2

    out_specs.append(pl.BlockSpec((8, 128), lambda i, ids: (0, 0)))
    out_shape.append(jax.ShapeDtypeStruct((8, 128), f32))

    def kernel(ids_ref, *refs):
        step = pl.program_id(0)
        refs[-1][...] = jnp.zeros((8, 128), f32)
        refs = refs[:-1]
        if got is None:

            def put(total):
                refs[-1][...] = total.astype(bf16).reshape(block)

            compute(ids_ref[step], put, *refs[:-1])
        else:

            def put(total):
                total = (total + refs[-3][...].reshape(total.shape).astype(f32)).astype(bf16)

                @pl.when(step < half)
                def _():
                    refs[-2][...] = total.reshape(block)

                @pl.when(step >= half)
                def _():
                    refs[-1][...] = total.reshape(block)

            compute(ids_ref[step], put, *refs[:-3])

    return call(
        kernel,
        [jnp.stack(ids).astype(jnp.int32), *operands],
        wait_for,
        scalars=1,
        grid=(n,),
        in_specs=in_specs,
        out_specs=out_specs,
        out_shape=out_shape,
        compiler_params=pltpu.CompilerParams(vmem_limit_bytes=vmem * 2**20),
        name="weight_grad",
        cost_estimate=cost(us * n, HEAVY),
    )


def flat_product(pid, put, left_ref, right_ref):
    left, right = left_ref[...], right_ref[...]
    put(product(left.reshape(-1, left.shape[-1]), right.reshape(right.shape[-2:]), 1, 0))


def product(a, b, over_a, over_b):
    return lax.dot_general(
        a, b, (((over_a,), (over_b,)), ((), ())), preferred_element_type=f32
    )


def side_by_side(x):
    return jnp.concatenate([x[HD * g : HD * (g + 1)] for g in range(GROUP)], axis=1)


def diagonal_mask(scores, rows, room):
    key = lax.broadcasted_iota(jnp.int32, (rows, rows), 0)
    query = lax.broadcasted_iota(jnp.int32, (rows, rows), 1)
    seen = (key <= query) & (key < room)
    return jnp.where(jnp.concatenate([seen] * GROUP, axis=1), scores, -1e30)


SUMS = 16


def attend_kernel(d, n, place_ref, q_ref, *refs):
    joined = refs[0].shape[0] > KV
    k_ref, v_ref = refs[0], refs[0 if joined else 1]
    refs = refs[1 if joined else 2 :]
    first, last = d == 0, d == n - 1
    m1_ref, a1_ref = (None, None) if first else refs[:2]
    m2_ref, a2_ref = refs[-2:]
    z, room = place_ref[0], place_ref[1]
    rows = q_ref.shape[1]

    @pl.when(z >= d)
    def _():
        ones = jnp.ones((SUMS, rows), bf16)
        for h in range(KV_HEADS):
            q = side_by_side(q_ref[GROUP * HD * h : GROUP * HD * (h + 1), :])
            k = k_ref[HD * h : HD * (h + 1), :]
            start = HD * h + (KV if joined else 0)
            v = v_ref[start : start + HD, :]
            s = product(k, q, 0, 0)
            if first:
                s = diagonal_mask(s, rows, room)
            m = jnp.max(s, axis=0, keepdims=True)
            if not first:
                m = jnp.maximum(m, m1_ref[h])
            p = jnp.exp(s - m).astype(bf16)
            total = product(jnp.concatenate([v, ones], axis=0), p, 1, 0)
            if not first:
                total = total + a1_ref[h] * jnp.exp(m1_ref[h] - m)
            m2_ref[h] = m
            a2_ref[h] = total

    if not first:

        @pl.when(z < d)
        def _():
            m2_ref[...] = m1_ref[...]
            a2_ref[...] = a1_ref[...]

    if last:
        o_ref, lse_ref = refs[2:4]
        for h in range(KV_HEADS):
            l = a2_ref[h, HD : HD + 1, :]
            o = (a2_ref[h, :HD, :] / l).astype(bf16)
            lse = m2_ref[h] + jnp.log(l)
            for g in range(GROUP):
                here = slice(HD * (GROUP * h + g), HD * (GROUP * h + g + 1))
                o_ref[here, :] = o[:, rows * g : rows * (g + 1)]
                lse_ref[h, g : g + 1, :] = lse[:, rows * g : rows * (g + 1)]


def attend(d, n, where, q, kv, state, wait_for):
    rows = q.shape[1]
    state_shapes = [(KV_HEADS, 1, GROUP * rows), (KV_HEADS, HD + SUMS, GROUP * rows)]
    out_shape = [jax.ShapeDtypeStruct(shape, f32) for shape in state_shapes]
    scratch = []
    if d == n - 1:
        scratch = [pltpu.VMEM(shape, f32) for shape in state_shapes]
        out_shape = [
            jax.ShapeDtypeStruct(q.shape, bf16),
            jax.ShapeDtypeStruct((KV_HEADS, GROUP, rows), f32),
        ]
    vmem = pl.BlockSpec(memory_space=pltpu.VMEM)
    return call(
        lambda *refs: attend_kernel(d, n, *refs),
        [where, q, *kv, *state],
        wait_for,
        in_specs=[pl.BlockSpec(memory_space=pltpu.SMEM)] + [vmem] * (1 + len(kv) + len(state)),
        out_specs=[vmem, vmem],
        out_shape=out_shape,
        scratch_shapes=scratch,
        compiler_params=pltpu.CompilerParams(vmem_limit_bytes=24 * 2**20),
        name="attend",
        cost_estimate=cost(4),
    )


def specs(rows):
    return (
        pl.BlockSpec((GROUP * HD, rows), lambda h, s: (h, 0)),
        pl.BlockSpec((2, HD, rows), lambda h, s: (0, h, 0)),
        pl.BlockSpec((1, GROUP, rows), lambda h, s: (h, 0, 0)),
    )


def turn(columns, cosine, sine, heads):
    half = HD // 2
    parts = []
    for h in range(heads):
        a = columns[HD * h : HD * h + half]
        b = columns[HD * h + half : HD * (h + 1)]
        parts += [a * cosine - b * sine, b * cosine + a * sine]
    return jnp.concatenate(parts, axis=0)


def attend_back_kernel(d, place_ref, q_ref, o_ref, do_ref, lse_ref, k_ref, v_ref, *refs):
    dq_ref, dkv_ref = refs[-2:]
    before_ref = None if len(refs) == 2 else refs[-3]
    z, room = place_ref[0], place_ref[1]
    rows = q_ref.shape[1]

    @pl.when(z >= d)
    def _():
        q, do, o = (side_by_side(r[...]) for r in (q_ref, do_ref, o_ref))
        lse = jnp.concatenate([lse_ref[0, g : g + 1, :] for g in range(GROUP)], axis=1)
        delta = jnp.sum(do.astype(f32) * o.astype(f32), axis=0, keepdims=True)
        k, v = k_ref[...], v_ref[...]
        s = product(k, q, 0, 0)
        if d == 0:
            s = diagonal_mask(s, rows, room)
        p = jnp.exp(s - lse)
        dp = product(v, do, 0, 0)
        ds = (p * (dp - delta)).astype(bf16)
        dkv_ref[1] = product(p.astype(bf16), do, 1, 1).T.astype(bf16)
        dkv_ref[0] = product(ds, q, 1, 1).T.astype(bf16)
        dq = product(k, ds, 1, 0) * HD ** (-0.5)
        for g in range(GROUP):
            here = slice(HD * g, HD * (g + 1))
            part = dq[:, rows * g : rows * (g + 1)]
            if before_ref is not None:
                part = part + before_ref[here, :]
            if d == 0:
                part = turn(part, refs[0][...], -refs[1][...], 1).astype(bf16)
            dq_ref[here, :] = part

    if d > 0:

        @pl.when(z < d)
        def _():
            dkv_ref[...] = jnp.zeros(dkv_ref.shape, bf16)
            if before_ref is None:
                dq_ref[...] = jnp.zeros(dq_ref.shape, f32)
            else:
                dq_ref[...] = before_ref[...]


def attend_back(d, where, q, o, do, lse, kv, before, tables, wait_for):
    rows = q.shape[1]
    q_spec, kv_spec, lse_spec = specs(rows)
    k_spec = pl.BlockSpec((HD, rows), lambda h, s: (h, 0))
    skip = 0 if len(kv) > 1 else KV_HEADS
    v_spec = pl.BlockSpec((HD, rows), lambda h, s: (skip + h, 0))
    extra, extra_specs = [], []
    if d == 0:
        extra = list(tables)
        extra_specs = [pl.BlockSpec((HD // 2, rows), lambda h, s: (0, 0))] * 2
    if before is not None:
        extra.append(before)
        extra_specs.append(q_spec)
    return call(
        lambda *refs: attend_back_kernel(d, *refs),
        [where, q, o, do, lse, kv[0], kv[-1], *extra],
        wait_for,
        scalars=1,
        grid=(KV_HEADS,),
        in_specs=[q_spec, q_spec, q_spec, lse_spec, k_spec, v_spec] + extra_specs,
        out_specs=[q_spec, kv_spec],
        out_shape=[
            jax.ShapeDtypeStruct(q.shape, f32 if d else bf16),
            jax.ShapeDtypeStruct((2, KV, rows), bf16),
        ],
        compiler_params=pltpu.CompilerParams(vmem_limit_bytes=32 * 2**20),
        name="attend_back",
        cost_estimate=cost(7, HEAVY),
    )


def gradient_columns(own, got, dq, low, tables, wait_for):
    rows = dq.shape[1]
    lanes = 2 * KV + dq.shape[0] + low.shape[1]

    def kernel(own_ref, got_ref, dq_ref, low_ref, cos_ref, sin_ref, out_ref):
        dkv = own_ref[...].astype(f32) + got_ref[...].astype(f32)
        keys = turn(dkv[0], cos_ref[...], -sin_ref[...], KV_HEADS).astype(bf16)
        sides = jnp.concatenate([keys, dkv[1].astype(bf16), dq_ref[...]], axis=0)
        out_ref[...] = jnp.concatenate([sides.T, low_ref[...]], axis=1)

    vmem = pl.BlockSpec(memory_space=pltpu.VMEM)
    return call(
        kernel,
        [own, got, dq, low, *tables],
        wait_for,
        in_specs=[vmem] * 6,
        out_specs=vmem,
        out_shape=jax.ShapeDtypeStruct((rows, lanes), bf16),
        compiler_params=pltpu.CompilerParams(vmem_limit_bytes=16 * 2**20),
        name="gradient_columns",
        cost_estimate=cost(0.01),
    )


def dot(a, b, pattern):
    return jnp.einsum(pattern, a, b, preferred_element_type=f32)


def normalize(x, gain):
    scale = lax.rsqrt(jnp.mean(x * x, axis=-1, keepdims=True) + norm_epsilon)
    unit = x * scale
    return (unit * gain).astype(bf16), unit, scale


def normalize_back(grad, gain, unit, scale):
    grad_unit = grad * gain
    return scale * (grad_unit - unit * jnp.mean(grad_unit * unit, axis=-1, keepdims=True))


def feed_forward_kernel(x_ref, mix_ref, wo_ref, gain_ref, wg_ref, wu_ref, wd_ref, *refs):
    result_ref, hidden_ref, gate_ref, up_ref, nft_ref, active_ref, nf_ref = refs[-7:]

    @pl.when(pl.program_id(0) == 0)
    def _():
        hidden = x_ref[...] + product(mix_ref[...], wo_ref[...], 0, 0)
        hidden_ref[...] = hidden
        normed, _, _ = normalize(hidden, gain_ref[...])
        nf_ref[...] = normed
        nft_ref[...] = normed.T
        result_ref[...] = hidden

    normed = nf_ref[...]
    gate = product(normed, wg_ref[...], 1, 0)
    up = product(normed, wu_ref[...], 1, 0)
    active = (gate * jax.nn.sigmoid(gate) * up).astype(bf16)
    gate_ref[...] = gate.astype(bf16)
    up_ref[...] = up.astype(bf16)
    active_ref[...] = active.T
    result_ref[...] += product(active, wd_ref[...], 1, 0)


def feed_forward(x, mixture, w_o, gain, w_gate, w_up, w_down, kept):
    rows, model = x.shape
    hidden_units = w_gate.shape[1]
    tile = hidden_units // 5
    half = 0 if kept else 1
    whole = lambda *shape: pl.BlockSpec(shape, lambda i: (0,) * len(shape))
    wide = lambda n: pl.BlockSpec((n, tile), lambda i: (0, i))
    return pl.pallas_call(
        feed_forward_kernel,
        grid=(5,),
        in_specs=[
            whole(rows, model), whole(model, rows), whole(model, model), whole(1, model),
            wide(model), wide(model), pl.BlockSpec((tile, model), lambda i: (i, 0)),
        ]
        + [pl.BlockSpec(memory_space=pl.ANY)] * len(kept),
        out_specs=[
            whole(rows, model), whole(rows, model), wide(rows), wide(rows),
            pl.BlockSpec((model, rows), lambda i: (0, half)),
            pl.BlockSpec((tile, rows), lambda i: (i, half)),
        ],
        out_shape=[
            jax.ShapeDtypeStruct((rows, model), f32),
            jax.ShapeDtypeStruct((rows, model), f32),
            jax.ShapeDtypeStruct((rows, hidden_units), bf16),
            jax.ShapeDtypeStruct((rows, hidden_units), bf16),
            jax.ShapeDtypeStruct((model, 2 * rows), bf16),
            jax.ShapeDtypeStruct((hidden_units, 2 * rows), bf16),
        ],
        scratch_shapes=[pltpu.VMEM((rows, model), bf16)],
        input_output_aliases={7: 4, 8: 5} if kept else {},
        compiler_params=pltpu.CompilerParams(vmem_limit_bytes=48 * 2**20),
        name="feed_forward",
        cost_estimate=cost(12),
    )(x, mixture, w_o, gain[None], w_gate, w_up, w_down, *kept)


def feed_forward_back_kernel(grad_ref, hidden_ref, gain_ref, gate_ref, up_ref, wg_ref, wu_ref,
                             wd_ref, wo_ref, *refs):
    d_gu_ref, d_hidden_ref, low_ref, d_mix_ref, total_ref = refs[-5:]
    step = pl.program_id(0)
    low = grad_ref[...].astype(bf16)
    d_active = product(low, wd_ref[...], 1, 1)
    gate, up = gate_ref[...].astype(f32), up_ref[...].astype(f32)
    sig = jax.nn.sigmoid(gate)
    d_gate = (d_active * up * sig * (1.0 + gate * (1.0 - sig))).astype(bf16)
    d_up = (d_active * gate * sig).astype(bf16)
    d_gu_ref[0] = d_gate
    d_gu_ref[1] = d_up
    term = product(d_gate, wg_ref[...], 1, 1) + product(d_up, wu_ref[...], 1, 1)

    @pl.when(step == 0)
    def _():
        total_ref[...] = term

    @pl.when(step > 0)
    def _():
        total_ref[...] += term

    @pl.when(step == pl.num_programs(0) - 1)
    def _():
        hidden = hidden_ref[...]
        scale = lax.rsqrt(jnp.mean(hidden * hidden, axis=-1, keepdims=True) + norm_epsilon)
        d_norm = normalize_back(total_ref[...], gain_ref[...], hidden * scale, scale)
        d_hidden = grad_ref[...] + d_norm
        d_hidden_ref[...] = d_hidden
        low = d_hidden.astype(bf16)
        low_ref[...] = low
        d_mix_ref[...] = product(wo_ref[...], low, 1, 1).astype(bf16)


def feed_forward_back(
    grad, hidden, gain, gate, up, w_gate, w_up, w_down, w_o, kept, wait_for=()
):
    rows, model = grad.shape
    half = 1 if kept else 0
    hidden_units = gate.shape[1]
    tile = hidden_units // 5
    whole = lambda *shape: pl.BlockSpec(shape, lambda i: (0,) * len(shape))
    wide = lambda n: pl.BlockSpec((n, tile), lambda i: (0, i))
    return call(
        feed_forward_back_kernel,
        [grad, hidden, gain[None], gate, up, w_gate, w_up, w_down, w_o, *kept],
        wait_for,
        grid=(5,),
        in_specs=[
            whole(rows, model), whole(rows, model), whole(1, model), wide(rows), wide(rows),
            wide(model), wide(model), pl.BlockSpec((tile, model), lambda i: (i, 0)),
            whole(model, model),
        ]
        + [pl.BlockSpec(memory_space=pl.ANY)] * len(kept),
        out_specs=[
            pl.BlockSpec((2, rows, tile), lambda i: (0, half, i)),
            whole(rows, model), whole(rows, model), whole(model, rows),
        ],
        out_shape=[
            jax.ShapeDtypeStruct((2, 2 * rows, hidden_units), bf16),
            jax.ShapeDtypeStruct((rows, model), f32),
            jax.ShapeDtypeStruct((rows, model), bf16),
            jax.ShapeDtypeStruct((model, rows), bf16),
        ],
        scratch_shapes=[pltpu.VMEM((rows, model), f32)],
        input_output_aliases={9: 0} if kept else {},
        compiler_params=pltpu.CompilerParams(vmem_limit_bytes=48 * 2**20),
        name="feed_forward_back",
        cost_estimate=cost(18, HEAVY),
    )


def project(normed, w, first, lanes, cosine, sine, heads, scale, name, wait_for=(), split=True):
    rows, model = normed.shape

    cuts = [heads * HD, lanes - heads * HD]
    cuts = [n for n in cuts if n] if split else [lanes]

    def kernel(x_ref, w_ref, cos_ref, sin_ref, out_ref, *rest_ref):
        y = product(x_ref[...], w_ref[:, first : first + lanes], 1, 0).T
        turned = turn(y[: heads * HD], cos_ref[...], sin_ref[...], heads)
        out_ref[: heads * HD, :] = turned.astype(bf16) * bf16(scale)
        if heads * HD < lanes:
            ref, start = (rest_ref[0], 0) if split else (out_ref, heads * HD)
            ref[start:, :] = y[heads * HD :].astype(bf16)

    whole = lambda *shape: pl.BlockSpec(shape, lambda i: (0,) * len(shape))
    width = first + lanes if (first + lanes) % 128 == 0 else w.shape[1]
    return call(
        kernel,
        [normed, w, cosine, sine],
        wait_for,
        grid=(1,),
        in_specs=[
            whole(rows, model), whole(model, width), whole(HD // 2, rows), whole(HD // 2, rows)
        ],
        out_specs=[whole(n, rows) for n in cuts],
        out_shape=[jax.ShapeDtypeStruct((n, rows), bf16) for n in cuts],
        compiler_params=pltpu.CompilerParams(vmem_limit_bytes=24 * 2**20),
        name=name,
        cost_estimate=cost(2),
    )


def projected_kv(normed, projections, tables, split):
    return project(
        normed, projections, 0, 2 * KV, *tables, KV_HEADS, 1.0, "keys_values", (), split
    )


def projected_q(normed, projections, tables, wait_for):
    first, lanes = 2 * KV, HEADS * HD
    return project(
        normed, projections, first, lanes, *tables, HEADS, HD**-0.5, "queries", wait_for
    )[0]


def attention(normed, kv, projections, where, tables, before):
    count = lax.axis_size("fsdp")
    kvs = [kv]
    for step in range(1, count):
        kvs.append([climb(v, step) for v in kvs[-1]])
    q = projected_q(normed, projections, tables, kv[:1])
    state = []
    for d in range(count):
        wait_for = ()
        if d in before:
            wait_for, state = before[d](state)
        state = attend(d, count, where, q, kvs[d], state, wait_for)
    return q, kvs, state


def attention_gradient(d_mixture, low, saved, where, tables, before, at_end):
    q, kvs, (mixture, lse) = saved[1:]
    count = lax.axis_size("fsdp")
    dq = moving = got = None
    for d in reversed(range(count)):
        step = count - 1 - d
        wait_for = []
        if d in before:
            wait_for, dq = before[d](dq)
        if step:
            got = lax.ppermute(
                moving, "fsdp", [(i, i - 1) for i in range(count - step, count)]
            )
        dq, dkv = attend_back(
            d, where, q, mixture, d_mixture, lse, kvs[d], dq, tables, wait_for
        )
        if d:
            moving = add(dkv, got) if step else dkv
    wait_for, dq = at_end(dq)
    return gradient_columns(dkv, got, dq, low, tables, wait_for)


def layer_gradient(d_hidden, columns, norm, gain, w_qkv):
    normed, unit, scale = norm
    d_normed = dot(columns[:, : w_qkv.shape[1]], w_qkv, "tf,df->td")
    return d_hidden + normalize_back(d_normed, gain, unit, scale)


def local(
    tokens,
    lengths,
    cotangent,
    attention_gain,
    feedforward_gain,
    query_weight,
    key_weight,
    value_weight,
    out_weight,
    gate_weight,
    up_weight,
    down_weight,
):
    rows = tokens.shape[1]
    count = lax.axis_size("fsdp")
    z = lax.axis_index("fsdp")
    low, core, one, two = place()
    positions = z * rows + jnp.arange(rows, dtype=jnp.int32)
    length = lengths[0]
    where = jnp.stack([z, length - z * rows]).astype(jnp.int32)
    frequency = rotary_base ** (-jnp.arange(HD // 2, dtype=f32) * 2.0 / HD)
    angles = frequency[:, None] * positions.astype(f32)[None, :]
    tables = (jnp.cos(angles), jnp.sin(angles))
    block = query_weight.shape[0]
    model = block * count
    hidden_units = gate_weight.shape[1]

    projections = jnp.concatenate([key_weight, value_weight, query_weight, out_weight], axis=1)
    lanes = projections.shape[1] // 4
    f_lanes = hidden_units // 4
    down_rows = down_weight.shape[0] // 8
    own_gains = jnp.stack([attention_gain, feedforward_gain])
    piece = projection_piece(projections, low, core)
    held = piece.shape[0]
    own = lax.optimization_barrier(
        (
            jnp.concatenate([piece, jnp.pad(own_gains, ((0, 14), (0, lanes - block)))]),
            gate_up_piece(gate_weight, up_weight, low, core),
            down_piece(down_weight, low),
        )
    )
    blocks = other_blocks(own[0])
    gains = all_blocks(jnp.stack([v[held : held + 2, :block] for v in blocks[::-1]]), own_gains)
    to_proj = Gather([v[:held] for v in blocks])
    to_proj.hop()
    to_proj.hop_on()
    rest = jnp.pad(own[2][:, f_lanes:], ((0, 0), (0, 2 * f_lanes - model)))
    wide = jnp.concatenate([own[1], own[2][:, :f_lanes], rest])
    wide = lax.all_gather(wide, "fsdp")
    wide = [
        lax.dynamic_index_in_dim(wide, (z + count - o) % count, 0, keepdims=False)
        for o in range(1, count)
    ]
    to_gate_up = Gather([v[:block] for v in wide])
    to_down = Gather(
        [
            jnp.concatenate(
                [v[block : block + down_rows], v[block + down_rows :, : model - f_lanes]], axis=1
            )
            for v in wide
        ]
    )
    to_gate_up.hop()
    to_down.hop()
    gains = jnp.moveaxis(gains, 0, 1).reshape(2, model).astype(f32)
    projections = whole_projections(
        projections, low, to_proj.cross(), [to_gate_up.mine, to_down.mine]
    )
    w_qkv = projections[:, : 2 * KV + model]

    start = tokens[0].astype(f32)
    norm_1 = normalize(start, gains[0])
    normed = norm_1[0]
    kv = projected_kv(normed, projections, tables, False)


    def first_arrived(state):
        here = (to_gate_up.a, to_gate_up.b, to_down.a, to_down.b)
        state, here = together(state, here)
        to_gate_up.a, to_gate_up.b, to_down.a, to_down.b = here
        to_gate_up.hop_on()
        to_down.hop_on()
        return (), state

    def second_arrived(state):
        state, here = together(state, (to_gate_up.ab, to_down.ab))
        to_gate_up.ab, to_down.ab = here
        return (), state

    saved_first = (norm_1,) + attention(
        normed, kv, projections, where, tables,
        {2: first_arrived, 3: second_arrived},
    )
    mixture = saved_first[3][0]
    w_o = projections[:, 2 * KV + model :]
    w_down = whole_down(down_weight, low, to_down.cross())
    w_gate, w_up = whole_gate_up(gate_weight, up_weight, low, to_gate_up.cross())
    middle, hidden_1, gate_1, up_1, *kept = feed_forward(
        start, mixture, w_o, gains[1], w_gate, w_up, w_down, []
    )

    norm_2 = normalize(middle, gains[0])
    kv = projected_kv(norm_2[0], projections, tables, True)
    half_rows = block // 2

    def left_of(normed, mixture):
        rows_of = jnp.stack([normed.T, mixture]).reshape(2, count, 2, half_rows, rows)
        return jnp.pad(rows_of, ((0, 0),) * 3 + ((0, held - half_rows), (0, 0)))

    left_1 = left_of(norm_1[0], mixture)
    saved_second = (norm_2,) + attention(
        norm_2[0], kv, projections, where, tables, {1: lambda state: (left_1, state)}
    )
    final, hidden_2, gate_2, up_2, nft, active = feed_forward(
        middle, saved_second[3][0], w_o, gains[1], w_gate, w_up, w_down, kept
    )

    real = (positions < length).astype(f32)
    gradient = cotangent[0].astype(f32) * real[:, None]
    down_back = (gradient.astype(bf16),)
    left = jnp.concatenate([left_of(norm_2[0], saved_second[3][0]), left_1], axis=-1)
    d_gu, d_hidden, low_2, d_mixture = feed_forward_back(
        gradient, hidden_2, gains[1], gate_2, up_2, w_gate, w_up, w_down, w_o, [], [left]
    )
    columns_2 = attention_gradient(
        d_mixture, low_2, saved_second, where, tables, {}, lambda dq: ((), dq)
    )
    gradient = layer_gradient(d_hidden, columns_2, norm_2, gains[0], w_qkv)

    down_back = jnp.concatenate(down_back + (gradient.astype(bf16),))
    active = active.reshape(count, 8, down_rows, 2 * rows)
    theirs, ours = ids_of(low ^ 1), ids_of(low)

    def down_pieces(ids, got, wait_for):
        return grad_pieces(
            ids, got, [active, down_back],
            [
                pl.BlockSpec((count, 1, down_rows, 2 * rows), lambda i, ids: (0, ids[i], 0, 0)),
                pl.BlockSpec((2 * rows, model), lambda i, ids: (0, 0)),
            ],
            flat_product, (count, down_rows, model), 1.4, wait_for,
        )

    send, token = down_pieces(theirs, None, ())
    to_down = Reduction(send)
    away, home, token = down_pieces(ours, to_down.got, [token])
    to_down.hop(away, [home[0]], [home[1]])
    d_gu, d_hidden, low_1, d_mixture = feed_forward_back(
        gradient, hidden_1, gains[1], gate_1, up_1, w_gate, w_up, w_down, w_o, [d_gu], [token]
    )

    def gate_up_pieces(ids, got, wait_for):
        return grad_pieces(
            ids, got, [nft, d_gu],
            [
                pl.BlockSpec((model, 2 * rows), lambda i, ids: (0, 0)),
                pl.BlockSpec(
                    (1, 2 * rows, f_lanes), lambda i, ids: (ids[i] % 2, 0, ids[i] // 2)
                ),
            ],
            flat_product, (count, block, f_lanes), 2.2, wait_for,
        )

    send, token = gate_up_pieces(theirs, None, ())
    to_gate_up = Reduction(send)
    to_down.came, d_hidden = together(to_down.came, d_hidden)
    to_down.hop_on()

    def third(dq):
        return [token], dq

    def second(dq):
        away, home, token = gate_up_pieces(ours, to_gate_up.got, [dq])
        to_gate_up.hop(away, [home[0]], [home[1]])
        dq, to_down.came = together(dq, to_down.came)
        to_down.settle()
        return [token], dq

    def zeroth(dq):
        dq, to_gate_up.came = together(dq, to_gate_up.came)
        to_gate_up.add_up()
        dq, to_gate_up.far, to_down.cuts = together(dq, to_gate_up.far, to_down.cuts)
        to_gate_up.go_on()
        to_down.shift()
        return (), dq

    columns_1 = attention_gradient(
        d_mixture, low_1, saved_first, where, tables,
        {3: third, 2: second, 0: zeroth}, lambda dq: ((), dq),
    )
    columns_1, to_gate_up.came, to_down.came = together(
        columns_1, to_gate_up.came, to_down.came
    )
    to_gate_up.settle()
    to_gate_up.shift()

    def compute_proj(pid, put, a, b, right_2, right_1):
        right = jnp.concatenate([right_2[...], right_1[...]], axis=0)

        def product_of(ref):
            total = product(ref[...].reshape(count * held, 2 * rows), right, 1, 0)
            return total.reshape(count, held, lanes)[:, :half_rows]

        @pl.when(pid // 2 != 2)
        def _():
            put(product_of(a))

        @pl.when(pid // 2 == 2)
        def _():
            lane = lax.broadcasted_iota(jnp.int32, (count, half_rows, lanes), 2)
            put(jnp.where(lane < lanes // 2, product_of(a), product_of(b)))

    def proj_pieces(ids, wait_for, us):
        def left_spec(k):
            return pl.BlockSpec(
                (1, count, 1, held, 2 * rows),
                lambda i, ids: (jnp.where(ids[i] // 2 * 2 + k > 4, 1, 0), 0, ids[i] % 2, 0, 0),
            )

        right_spec = pl.BlockSpec((rows, lanes), lambda i, ids: (0, ids[i] // 2))
        return grad_pieces(
            ids, None, [left, left, columns_2, columns_1],
            [left_spec(0), left_spec(1), right_spec, right_spec],
            compute_proj, (count, half_rows, lanes), us, wait_for, 24,
        )

    send, token = proj_pieces(theirs, to_gate_up.cuts[0], 2)
    to_proj = Reduction(send)
    keep, token = proj_pieces(ours, [token], 0.01)
    down_handed = hand(to_down.total())
    keep, down_handed[1:3] = together(keep, down_handed[1:3])
    down_handed[3] = swap(down_handed[2], first_hop)
    got = to_proj.got
    to_proj.hop(add(keep[:2], got[:2]), [keep[2], got[2]], [keep[3], got[3]])
    (
        to_proj.came, to_gate_up.came[0], to_gate_up.came[2], down_handed[3]
    ) = together(
        to_proj.came, to_gate_up.came[0], to_gate_up.came[2], down_handed[3]
    )
    to_proj.hop_on()
    to_proj.settle()
    to_proj.cuts, to_gate_up.came[1] = together(to_proj.cuts, to_gate_up.came[1])
    gate_up_handed = hand(to_gate_up.total())
    to_proj.shift()
    proj_mine, gate_up_handed[1:] = together(to_proj.total(), gate_up_handed[1:])
    gradient = layer_gradient(d_hidden, columns_1, norm_1, gains[0], w_qkv)
    g_down = give(down_handed)
    proj_handed = hand(proj_mine)
    gate_up_handed[0], proj_handed[2] = together(gate_up_handed[0], proj_handed[2])
    proj_handed[3] = swap(proj_handed[2], first_hop)
    g_gate_up = give(gate_up_handed)

    def put_down(refs, q, c, pid, value):
        refs[0][pl.ds(pl.multiple_of(pid * down_rows, 8), down_rows), :] = value

    def put_gate_up(refs, q, c, pid, value):
        refs[c][:, lanes_at(q * f_lanes, f_lanes)] = value

    widths = [KV, KV, model, model]

    def put_proj(refs, q, c, pid, value):
        here = slice(c * half_rows, (c + 1) * half_rows)
        for quarter in range(4):

            @pl.when(q == quarter)
            def _():
                first = 0
                for ref, width in zip(refs, widths):
                    start = max(first, quarter * lanes)
                    stop = min(first + width, (quarter + 1) * lanes)
                    if start < stop:
                        ref[here, start - first : stop - first] = value[
                            :, start - quarter * lanes : stop - quarter * lanes
                        ]
                    first += width

    g_down = spread(low, g_down, [(8 * down_rows, model)], put_down)[0]
    g_gate, g_up = spread(low, g_gate_up, [(block, hidden_units)] * 2, put_gate_up)
    g_gate, g_up, proj_handed[3] = together(g_gate, g_up, proj_handed[3])
    g_proj = give(proj_handed)
    g_k, g_v, g_q, g_o = spread(
        low, g_proj, [(block, w) for w in widths], put_proj
    )

    def gain_gradient(gain, pairs):
        along = sum(jnp.sum(w.astype(f32) * g, axis=1) for w, g in pairs)
        return along / gain.astype(f32)

    g_attention_gain = gain_gradient(
        attention_gain, [(query_weight, g_q), (key_weight, g_k), (value_weight, g_v)]
    )
    g_feedforward_gain = gain_gradient(
        feedforward_gain, [(gate_weight, g_gate), (up_weight, g_up)]
    )

    return (
        final.astype(bf16)[None],
        gradient.astype(bf16)[None],
        g_attention_gain,
        g_feedforward_gain,
        g_q,
        g_k,
        g_v,
        g_o,
        g_gate,
        g_up,
        g_down,
    )


def solution(mesh):
    rows = P("fsdp", None)
    placed = (P("dp", "fsdp", None), P("dp"), P("dp", "fsdp", None), P("fsdp"), P("fsdp")) + (
        rows,
    ) * 7
    return jax.shard_map(
        local,
        mesh=mesh,
        in_specs=placed,
        out_specs=(P("dp", "fsdp", None), P("dp", "fsdp", None), P("fsdp"), P("fsdp"))
        + (rows,) * 7,
        check_vma=False,
    )
```

```python
import jax
import jax.numpy as jnp
from jax import lax
from jax.experimental import pallas as pl
from jax.experimental.pallas import tpu as pltpu
from jax.sharding import PartitionSpec as P

HEADS = 15
KV_HEADS = 5
HD = 64
GROUP = HEADS // KV_HEADS
KV = KV_HEADS * HD

norm_epsilon = 1e-05
rotary_base = 10000.0

bf16 = jnp.bfloat16
f32 = jnp.float32


def first_hop(i):
    return i ^ (4 if i & 1 else 2)


def second_hop(i):
    return i ^ (2 if i & 1 else 4)


def sibling(i):
    return i ^ 1


def swap(value, hop):
    count = lax.axis_size("dp")
    return lax.ppermute(value, "dp", [(i, hop(i)) for i in range(count)])


def climb(value, step):
    count = lax.axis_size("fsdp")
    return lax.ppermute(value, "fsdp", [(i, i + 1) for i in range(step - 1, count - 1)])


def descend(value, step):
    count = lax.axis_size("fsdp")
    return lax.ppermute(value, "fsdp", [(i, i - 1) for i in range(1, count - step + 1)])


def place():
    low = lax.axis_index("dp") % 8
    core = low % 2
    one = jnp.where(core == 1, 4, 2)
    return low, core, one, 6 - one


def around(value, distance):
    count = lax.axis_size("fsdp")
    return lax.ppermute(value, "fsdp", [(i, (i + distance) % count) for i in range(count)])


def together(*values):
    return lax.optimization_barrier(values)


def call(kernel, operands, wait_for=(), scalars=0, in_specs=(), grid=(), **rest):
    wait_for = jax.tree.leaves(wait_for)
    last = len(operands)

    def waiting(*refs):
        kernel(*refs[:last], *refs[last + len(wait_for) :])

    in_specs = list(in_specs) + [pl.BlockSpec(memory_space=pl.ANY)] * len(wait_for)
    where = dict(in_specs=in_specs, out_specs=rest.pop("out_specs"))
    scratch = rest.pop("scratch_shapes", ())
    if scalars:
        where = dict(
            grid_spec=pltpu.PrefetchScalarGridSpec(
                num_scalar_prefetch=scalars, grid=grid, scratch_shapes=scratch, **where
            )
        )
    else:
        where.update(grid=grid, scratch_shapes=scratch)
    return pl.pallas_call(waiting, **where, **rest)(*operands, *wait_for)


class Gather:
    def __init__(self, blocks):
        self.blocks = blocks

    def hop(self):
        self.mine = jnp.stack(self.blocks)
        self.a = swap(self.mine, first_hop)
        self.b = swap(self.mine, second_hop)

    def hop_on(self):
        self.ab = swap(self.a, second_hop)

    def cross(self):
        mine = [self.mine, self.a, self.b, self.ab]
        return mine + [swap(v, sibling) for v in mine]


def other_blocks(own):
    return [around(own, o) for o in range(1, lax.axis_size("fsdp"))]


def piece_ids(low):
    odd = low % 2
    one = 2 + 2 * odd
    two = 6 - one
    return [low, low ^ one, low ^ two, low ^ 6, low ^ 1, low ^ 1 ^ two, low ^ 1 ^ one, low ^ 7]


def lay_out(low, pieces, own, out_shapes, moves, wait_for=()):
    count = lax.axis_size("fsdp")
    where = jnp.stack([lax.axis_index("fsdp"), low]).astype(jnp.int32)

    def kernel(where_ref, *refs):
        piece_refs, refs = refs[:8], refs[8:]
        own_refs, refs = refs[: len(own)], refs[len(own) :]
        outs = refs
        z, low = where_ref[0], where_ref[1]
        for core in range(2):

            @pl.when(low % 2 == core)
            def _():
                copies = []
                for k, pid in enumerate(piece_ids(low)):
                    own_core = core if k < 4 else 1 - core
                    for o in range(count - 1):
                        block = lax.rem(z + count - 1 - o, count)
                        copies += moves(piece_refs[k].at[o], block, pid // 2, own_core, pid, outs)
                for source, target in copies + own_moves(own_refs, z, outs):
                    target[...] = source[...]

    moves, own_moves = moves
    vmem = pl.BlockSpec(memory_space=pltpu.VMEM)
    return call(
        kernel,
        [where, *pieces, *own],
        wait_for,
        in_specs=[pl.BlockSpec(memory_space=pltpu.SMEM)] + [vmem] * (8 + len(own)),
        out_specs=[vmem] * len(out_shapes),
        out_shape=[jax.ShapeDtypeStruct(shape, bf16) for shape in out_shapes],
        compiler_params=pltpu.CompilerParams(vmem_limit_bytes=26 * 2**20),
        name="lay_out",
        cost_estimate=cost(5),
    )


def rows_at(start, size):
    return pl.ds(pl.multiple_of(start, 16), size)


def lanes_at(start, size):
    return pl.ds(start if isinstance(start, int) else pl.multiple_of(start, 128), size)


def projection_piece(shard, low, core):
    block, width = shard.shape
    rest = block // 2 // 16 * 16
    lanes = width // 4
    return lax.dynamic_slice(shard, (core * rest, low // 2 * lanes), (block - rest, lanes))


def gate_up_piece(gate, up, low, core):
    lanes = gate.shape[1] // 4
    gate, up = (lax.dynamic_slice_in_dim(v, low // 2 * lanes, lanes, 1) for v in (gate, up))
    return jnp.where(core == 1, up, gate)


def down_piece(shard, low):
    rows = shard.shape[0] // 8
    return lax.dynamic_slice_in_dim(shard, low * rows, rows, 0)


def whole_projections(shard, low, pieces, wait_for):
    count = lax.axis_size("fsdp")
    block, width = shard.shape
    lanes = width // 4
    rest = block // 2 // 16 * 16
    held = block - rest

    def moves(src, z, q, c, pid, outs):
        size = held if c else rest
        return [
            (
                src.at[pl.ds(0, size)],
                outs[0].at[rows_at(z * block + c * rest, size), lanes_at(q * lanes, lanes)],
            )
        ]

    def own_moves(refs, z, outs):
        return [(refs[0], outs[0].at[rows_at(z * block, block)])]

    return lay_out(
        low, pieces, [shard], [(count * block, width)], (moves, own_moves), wait_for
    )[0]


def whole_gate_up(gate, up, low, pieces):
    count = lax.axis_size("fsdp")
    block, width = gate.shape
    lanes = width // 4

    def moves(src, z, q, c, pid, outs):
        return [(src, outs[c].at[rows_at(z * block, block), lanes_at(q * lanes, lanes)])]

    def own_moves(refs, z, outs):
        return [(refs[k], outs[k].at[rows_at(z * block, block)]) for k in range(2)]

    return lay_out(low, pieces, [gate, up], [(count * block, width)] * 2, (moves, own_moves))


def whole_down(shard, low, pieces):
    count = lax.axis_size("fsdp")
    block, width = shard.shape
    rows = block // 8

    def moves(src, z, q, c, pid, outs):
        return [(src, outs[0].at[rows_at(z * block + pid * rows, rows)])]

    def own_moves(refs, z, outs):
        return [(refs[0], outs[0].at[rows_at(z * block, block)])]

    return lay_out(low, pieces, [shard], [(count * block, width)], (moves, own_moves))[0]


def all_blocks(others, own):
    count = lax.axis_size("fsdp")
    z = lax.axis_index("fsdp")
    both = jnp.concatenate([own[None], others])
    return jnp.stack(
        [
            lax.dynamic_index_in_dim(both, (k - z + count) % count, 0, keepdims=False)
            for k in range(count)
        ]
    )


def add(*terms):
    return sum(v.astype(f32) for v in terms).astype(bf16)


def cost(us, weight=6):
    return pl.CostEstimate(
        flops=int(us * weight * 1.15e9), bytes_accessed=0, transcendentals=0
    )


HEAVY = 6


class Reduction:
    def __init__(self, send):
        self.got = swap(send, sibling)

    def hop(self, away, near, far):
        self.near, self.far = near, far
        self.came = swap(away, first_hop)

    def hop_on(self):
        self.add_up()
        self.go_on()

    def add_up(self):
        self.far = add(*self.far, self.came[1])
        self.near = add(*self.near, self.came[0])

    def go_on(self):
        self.came = swap(self.far, second_hop)

    def settle(self):
        count, z = lax.axis_size("fsdp"), lax.axis_index("fsdp")
        self.near = add(self.near, self.came)
        self.cuts = [
            lax.dynamic_index_in_dim(self.near, (z + o) % count, 0, keepdims=False)
            for o in range(count)
        ]

    def shift(self):
        count = lax.axis_size("fsdp")
        self.came = [around(self.cuts[o], o) for o in range(1, count)]

    def total(self):
        return over_rest(add(self.cuts[0], *self.came))


def over_rest(mine):
    wide = lax.axis_size("dp")
    if wide > 8:
        groups = [[i + 8 * k for k in range(wide // 8)] for i in range(8)]
        mine = lax.psum(mine, "dp", axis_index_groups=groups)
    return mine


def hand(mine):
    b = swap(mine, second_hop)
    a, ab = swap(mine, first_hop), swap(b, first_hop)
    return [mine, a, b, ab]


def give(handed):
    return handed + [swap(v, sibling) for v in handed]


def ids_of(low):
    one = 2 + 2 * (low % 2)
    return [low ^ one, low ^ 6, low, low ^ 6 ^ one]


def spread(low, pieces, out_shapes, put, wait_for=()):
    def turn_out(shape):
        wide, high = (-(-n // 128) * 128 for n in shape[::-1])
        return shape[0] * wide > shape[1] * high

    def kernel(where_ref, *refs):
        low = where_ref[0]
        outs, rest = list(refs[8 : 8 + len(out_shapes)]), list(refs[8 + len(out_shapes) :])
        targets = [rest.pop(0) if turn_out(s) else v for s, v in zip(out_shapes, outs)]
        for core in range(2):

            @pl.when(low % 2 == core)
            def _():
                for k, pid in enumerate(piece_ids(low)):
                    own_core = core if k < 4 else 1 - core
                    put(targets, pid // 2, own_core, pid, refs[k][...].astype(f32))

        for target, out in zip(targets, outs):
            if target is not out:
                out[...] = target[...].T

    vmem = pl.BlockSpec(memory_space=pltpu.VMEM)
    turned = [turn_out(shape) for shape in out_shapes]
    shapes = [shape[::-1] if t else shape for shape, t in zip(out_shapes, turned)]
    out = call(
        kernel,
        [low[None], *pieces],
        wait_for,
        in_specs=[pl.BlockSpec(memory_space=pltpu.SMEM)] + [vmem] * 8,
        out_specs=[vmem] * len(out_shapes),
        out_shape=[jax.ShapeDtypeStruct(shape, f32) for shape in shapes],
        scratch_shapes=[pltpu.VMEM(s, f32) for s, t in zip(out_shapes, turned) if t],
        compiler_params=pltpu.CompilerParams(vmem_limit_bytes=22 * 2**20),
        name="spread",
        cost_estimate=cost(3),
    )
    return [v.T if t else v for v, t in zip(out, turned)]


def grad_pieces(
    ids, got, operands, in_specs, compute, piece_shape, us, wait_for, vmem=56
):
    block = (1,) + piece_shape
    zeros = (0,) * len(piece_shape)
    in_specs, operands = list(in_specs), list(operands)
    n = len(ids)
    if got is None:
        out_specs = [pl.BlockSpec(block, lambda i, ids: (i,) + zeros)]
        out_shape = [jax.ShapeDtypeStruct((n,) + piece_shape, bf16)]
    else:
        in_specs.append(pl.BlockSpec(block, lambda i, ids: (i,) + zeros))
        operands.append(got)
        half = n // 2
        out_specs = [
            pl.BlockSpec(block, lambda i, ids: (jnp.minimum(i, half - 1),) + zeros),
            pl.BlockSpec(block, lambda i, ids: (jnp.maximum(i - half, 0),) + zeros),
        ]
        out_shape = [jax.ShapeDtypeStruct((half,) + piece_shape, bf16)] * 2

    out_specs.append(pl.BlockSpec((8, 128), lambda i, ids: (0, 0)))
    out_shape.append(jax.ShapeDtypeStruct((8, 128), f32))

    def kernel(ids_ref, *refs):
        step = pl.program_id(0)
        refs[-1][...] = jnp.zeros((8, 128), f32)
        refs = refs[:-1]
        if got is None:

            def put(total):
                refs[-1][...] = total.astype(bf16).reshape(block)

            compute(ids_ref[step], put, *refs[:-1])
        else:

            def put(total):
                total = (total + refs[-3][...].reshape(total.shape).astype(f32)).astype(bf16)

                @pl.when(step < half)
                def _():
                    refs[-2][...] = total.reshape(block)

                @pl.when(step >= half)
                def _():
                    refs[-1][...] = total.reshape(block)

            compute(ids_ref[step], put, *refs[:-3])

    return call(
        kernel,
        [jnp.stack(ids).astype(jnp.int32), *operands],
        wait_for,
        scalars=1,
        grid=(n,),
        in_specs=in_specs,
        out_specs=out_specs,
        out_shape=out_shape,
        compiler_params=pltpu.CompilerParams(vmem_limit_bytes=vmem * 2**20),
        name="weight_grad",
        cost_estimate=cost(us * n, HEAVY),
    )


def flat_product(pid, put, left_ref, right_ref):
    left, right = left_ref[...], right_ref[...]
    put(product(left.reshape(-1, left.shape[-1]), right.reshape(right.shape[-2:]), 1, 0))


def product(a, b, over_a, over_b):
    return lax.dot_general(
        a, b, (((over_a,), (over_b,)), ((), ())), preferred_element_type=f32
    )


def side_by_side(x):
    return jnp.concatenate([x[HD * g : HD * (g + 1)] for g in range(GROUP)], axis=1)


def diagonal_mask(scores, rows, room):
    key = lax.broadcasted_iota(jnp.int32, (rows, rows), 0)
    query = lax.broadcasted_iota(jnp.int32, (rows, rows), 1)
    seen = (key <= query) & (key < room)
    return jnp.where(jnp.concatenate([seen] * GROUP, axis=1), scores, -1e30)


SUMS = 16


def attend_kernel(d, n, place_ref, q_ref, *refs):
    joined = refs[0].shape[0] > KV
    k_ref, v_ref = refs[0], refs[0 if joined else 1]
    refs = refs[1 if joined else 2 :]
    first, last = d == 0, d == n - 1
    m1_ref, a1_ref = (None, None) if first else refs[:2]
    m2_ref, a2_ref = refs[-2:]
    z, room = place_ref[0], place_ref[1]
    rows = q_ref.shape[1]

    @pl.when(z >= d)
    def _():
        ones = jnp.ones((SUMS, rows), bf16)
        for h in range(KV_HEADS):
            q = side_by_side(q_ref[GROUP * HD * h : GROUP * HD * (h + 1), :])
            k = k_ref[HD * h : HD * (h + 1), :]
            start = HD * h + (KV if joined else 0)
            v = v_ref[start : start + HD, :]
            s = product(k, q, 0, 0)
            if first:
                s = diagonal_mask(s, rows, room)
            m = jnp.max(s, axis=0, keepdims=True)
            if not first:
                m = jnp.maximum(m, m1_ref[h])
            p = jnp.exp(s - m).astype(bf16)
            total = product(jnp.concatenate([v, ones], axis=0), p, 1, 0)
            if not first:
                total = total + a1_ref[h] * jnp.exp(m1_ref[h] - m)
            m2_ref[h] = m
            a2_ref[h] = total

    if not first:

        @pl.when(z < d)
        def _():
            m2_ref[...] = m1_ref[...]
            a2_ref[...] = a1_ref[...]

    if last:
        o_ref, lse_ref = refs[2:4]
        for h in range(KV_HEADS):
            l = a2_ref[h, HD : HD + 1, :]
            o = (a2_ref[h, :HD, :] / l).astype(bf16)
            lse = m2_ref[h] + jnp.log(l)
            for g in range(GROUP):
                here = slice(HD * (GROUP * h + g), HD * (GROUP * h + g + 1))
                o_ref[here, :] = o[:, rows * g : rows * (g + 1)]
                lse_ref[h, g : g + 1, :] = lse[:, rows * g : rows * (g + 1)]


def attend(d, n, where, q, kv, state, wait_for):
    rows = q.shape[1]
    state_shapes = [(KV_HEADS, 1, GROUP * rows), (KV_HEADS, HD + SUMS, GROUP * rows)]
    out_shape = [jax.ShapeDtypeStruct(shape, f32) for shape in state_shapes]
    scratch = []
    if d == n - 1:
        scratch = [pltpu.VMEM(shape, f32) for shape in state_shapes]
        out_shape = [
            jax.ShapeDtypeStruct(q.shape, bf16),
            jax.ShapeDtypeStruct((KV_HEADS, GROUP, rows), f32),
        ]
    vmem = pl.BlockSpec(memory_space=pltpu.VMEM)
    return call(
        lambda *refs: attend_kernel(d, n, *refs),
        [where, q, *kv, *state],
        wait_for,
        in_specs=[pl.BlockSpec(memory_space=pltpu.SMEM)] + [vmem] * (1 + len(kv) + len(state)),
        out_specs=[vmem, vmem],
        out_shape=out_shape,
        scratch_shapes=scratch,
        compiler_params=pltpu.CompilerParams(vmem_limit_bytes=24 * 2**20),
        name="attend",
        cost_estimate=cost(4),
    )


def specs(rows):
    return (
        pl.BlockSpec((GROUP * HD, rows), lambda h, s: (h, 0)),
        pl.BlockSpec((2, HD, rows), lambda h, s: (0, h, 0)),
        pl.BlockSpec((1, GROUP, rows), lambda h, s: (h, 0, 0)),
    )


def turn(columns, cosine, sine, heads):
    half = HD // 2
    parts = []
    for h in range(heads):
        a = columns[HD * h : HD * h + half]
        b = columns[HD * h + half : HD * (h + 1)]
        parts += [a * cosine - b * sine, b * cosine + a * sine]
    return jnp.concatenate(parts, axis=0)


def attend_back_kernel(d, place_ref, q_ref, o_ref, do_ref, lse_ref, k_ref, v_ref, *refs):
    dq_ref, dkv_ref = refs[-2:]
    before_ref = None if len(refs) == 2 else refs[-3]
    z, room = place_ref[0], place_ref[1]
    rows = q_ref.shape[1]

    @pl.when(z >= d)
    def _():
        q, do, o = (side_by_side(r[...]) for r in (q_ref, do_ref, o_ref))
        lse = jnp.concatenate([lse_ref[0, g : g + 1, :] for g in range(GROUP)], axis=1)
        delta = jnp.sum(do.astype(f32) * o.astype(f32), axis=0, keepdims=True)
        k, v = k_ref[...], v_ref[...]
        s = product(k, q, 0, 0)
        if d == 0:
            s = diagonal_mask(s, rows, room)
        p = jnp.exp(s - lse)
        dp = product(v, do, 0, 0)
        ds = (p * (dp - delta)).astype(bf16)
        dkv_ref[1] = product(p.astype(bf16), do, 1, 1).T.astype(bf16)
        dkv_ref[0] = product(ds, q, 1, 1).T.astype(bf16)
        dq = product(k, ds, 1, 0) * HD ** (-0.5)
        for g in range(GROUP):
            here = slice(HD * g, HD * (g + 1))
            part = dq[:, rows * g : rows * (g + 1)]
            if before_ref is not None:
                part = part + before_ref[here, :]
            if d == 0:
                part = turn(part, refs[0][...], -refs[1][...], 1).astype(bf16)
            dq_ref[here, :] = part

    if d > 0:

        @pl.when(z < d)
        def _():
            dkv_ref[...] = jnp.zeros(dkv_ref.shape, bf16)
            if before_ref is None:
                dq_ref[...] = jnp.zeros(dq_ref.shape, f32)
            else:
                dq_ref[...] = before_ref[...]


def attend_back(d, where, q, o, do, lse, kv, before, tables, wait_for):
    rows = q.shape[1]
    q_spec, kv_spec, lse_spec = specs(rows)
    k_spec = pl.BlockSpec((HD, rows), lambda h, s: (h, 0))
    skip = 0 if len(kv) > 1 else KV_HEADS
    v_spec = pl.BlockSpec((HD, rows), lambda h, s: (skip + h, 0))
    extra, extra_specs = [], []
    if d == 0:
        extra = list(tables)
        extra_specs = [pl.BlockSpec((HD // 2, rows), lambda h, s: (0, 0))] * 2
    if before is not None:
        extra.append(before)
        extra_specs.append(q_spec)
    return call(
        lambda *refs: attend_back_kernel(d, *refs),
        [where, q, o, do, lse, kv[0], kv[-1], *extra],
        wait_for,
        scalars=1,
        grid=(KV_HEADS,),
        in_specs=[q_spec, q_spec, q_spec, lse_spec, k_spec, v_spec] + extra_specs,
        out_specs=[q_spec, kv_spec],
        out_shape=[
            jax.ShapeDtypeStruct(q.shape, f32 if d else bf16),
            jax.ShapeDtypeStruct((2, KV, rows), bf16),
        ],
        compiler_params=pltpu.CompilerParams(vmem_limit_bytes=32 * 2**20),
        name="attend_back",
        cost_estimate=cost(7, HEAVY),
    )


def gradient_columns(own, got, dq, low, tables, wait_for):
    rows = dq.shape[1]
    lanes = 2 * KV + dq.shape[0] + low.shape[1]

    def kernel(own_ref, got_ref, dq_ref, low_ref, cos_ref, sin_ref, out_ref):
        dkv = own_ref[...].astype(f32) + got_ref[...].astype(f32)
        keys = turn(dkv[0], cos_ref[...], -sin_ref[...], KV_HEADS).astype(bf16)
        sides = jnp.concatenate([keys, dkv[1].astype(bf16), dq_ref[...]], axis=0)
        out_ref[...] = jnp.concatenate([sides.T, low_ref[...]], axis=1)

    vmem = pl.BlockSpec(memory_space=pltpu.VMEM)
    return call(
        kernel,
        [own, got, dq, low, *tables],
        wait_for,
        in_specs=[vmem] * 6,
        out_specs=vmem,
        out_shape=jax.ShapeDtypeStruct((rows, lanes), bf16),
        compiler_params=pltpu.CompilerParams(vmem_limit_bytes=16 * 2**20),
        name="gradient_columns",
        cost_estimate=cost(0.01),
    )


def dot(a, b, pattern):
    return jnp.einsum(pattern, a, b, preferred_element_type=f32)


def normalize(x, gain):
    scale = lax.rsqrt(jnp.mean(x * x, axis=-1, keepdims=True) + norm_epsilon)
    unit = x * scale
    return (unit * gain).astype(bf16), unit, scale


def normalize_back(grad, gain, unit, scale):
    grad_unit = grad * gain
    return scale * (grad_unit - unit * jnp.mean(grad_unit * unit, axis=-1, keepdims=True))


def feed_forward_kernel(x_ref, mix_ref, wo_ref, gain_ref, wg_ref, wu_ref, wd_ref, *refs):
    result_ref, hidden_ref, gate_ref, up_ref, nft_ref, active_ref, nf_ref = refs[-7:]

    @pl.when(pl.program_id(0) == 0)
    def _():
        hidden = x_ref[...] + product(mix_ref[...], wo_ref[...], 0, 0)
        hidden_ref[...] = hidden
        normed, _, _ = normalize(hidden, gain_ref[...])
        nf_ref[...] = normed
        nft_ref[...] = normed.T
        result_ref[...] = hidden

    normed = nf_ref[...]
    gate = product(normed, wg_ref[...], 1, 0)
    up = product(normed, wu_ref[...], 1, 0)
    active = (gate * jax.nn.sigmoid(gate) * up).astype(bf16)
    gate_ref[...] = gate.astype(bf16)
    up_ref[...] = up.astype(bf16)
    active_ref[...] = active.T
    result_ref[...] += product(active, wd_ref[...], 1, 0)


def feed_forward(x, mixture, w_o, gain, w_gate, w_up, w_down, kept):
    rows, model = x.shape
    hidden_units = w_gate.shape[1]
    tile = hidden_units // 5
    half = 0 if kept else 1
    whole = lambda *shape: pl.BlockSpec(shape, lambda i: (0,) * len(shape))
    wide = lambda n: pl.BlockSpec((n, tile), lambda i: (0, i))
    return pl.pallas_call(
        feed_forward_kernel,
        grid=(5,),
        in_specs=[
            whole(rows, model), whole(model, rows), whole(model, model), whole(1, model),
            wide(model), wide(model), pl.BlockSpec((tile, model), lambda i: (i, 0)),
        ]
        + [pl.BlockSpec(memory_space=pl.ANY)] * len(kept),
        out_specs=[
            whole(rows, model), whole(rows, model), wide(rows), wide(rows),
            pl.BlockSpec((model, rows), lambda i: (0, half)),
            pl.BlockSpec((tile, rows), lambda i: (i, half)),
        ],
        out_shape=[
            jax.ShapeDtypeStruct((rows, model), f32),
            jax.ShapeDtypeStruct((rows, model), f32),
            jax.ShapeDtypeStruct((rows, hidden_units), bf16),
            jax.ShapeDtypeStruct((rows, hidden_units), bf16),
            jax.ShapeDtypeStruct((model, 2 * rows), bf16),
            jax.ShapeDtypeStruct((hidden_units, 2 * rows), bf16),
        ],
        scratch_shapes=[pltpu.VMEM((rows, model), bf16)],
        input_output_aliases={7: 4, 8: 5} if kept else {},
        compiler_params=pltpu.CompilerParams(vmem_limit_bytes=48 * 2**20),
        name="feed_forward",
        cost_estimate=cost(12),
    )(x, mixture, w_o, gain[None], w_gate, w_up, w_down, *kept)


def feed_forward_back_kernel(grad_ref, hidden_ref, gain_ref, gate_ref, up_ref, wg_ref, wu_ref,
                             wd_ref, wo_ref, *refs):
    d_gu_ref, d_hidden_ref, low_ref, d_mix_ref, total_ref = refs[-5:]
    step = pl.program_id(0)
    low = grad_ref[...].astype(bf16)
    d_active = product(low, wd_ref[...], 1, 1)
    gate, up = gate_ref[...].astype(f32), up_ref[...].astype(f32)
    sig = jax.nn.sigmoid(gate)
    d_gate = (d_active * up * sig * (1.0 + gate * (1.0 - sig))).astype(bf16)
    d_up = (d_active * gate * sig).astype(bf16)
    d_gu_ref[0] = d_gate
    d_gu_ref[1] = d_up
    term = product(d_gate, wg_ref[...], 1, 1) + product(d_up, wu_ref[...], 1, 1)

    @pl.when(step == 0)
    def _():
        total_ref[...] = term

    @pl.when(step > 0)
    def _():
        total_ref[...] += term

    @pl.when(step == pl.num_programs(0) - 1)
    def _():
        hidden = hidden_ref[...]
        scale = lax.rsqrt(jnp.mean(hidden * hidden, axis=-1, keepdims=True) + norm_epsilon)
        d_norm = normalize_back(total_ref[...], gain_ref[...], hidden * scale, scale)
        d_hidden = grad_ref[...] + d_norm
        d_hidden_ref[...] = d_hidden
        low = d_hidden.astype(bf16)
        low_ref[...] = low
        d_mix_ref[...] = product(wo_ref[...], low, 1, 1).astype(bf16)


def feed_forward_back(
    grad, hidden, gain, gate, up, w_gate, w_up, w_down, w_o, kept, wait_for=()
):
    rows, model = grad.shape
    half = 1 if kept else 0
    hidden_units = gate.shape[1]
    tile = hidden_units // 5
    whole = lambda *shape: pl.BlockSpec(shape, lambda i: (0,) * len(shape))
    wide = lambda n: pl.BlockSpec((n, tile), lambda i: (0, i))
    return call(
        feed_forward_back_kernel,
        [grad, hidden, gain[None], gate, up, w_gate, w_up, w_down, w_o, *kept],
        wait_for,
        grid=(5,),
        in_specs=[
            whole(rows, model), whole(rows, model), whole(1, model), wide(rows), wide(rows),
            wide(model), wide(model), pl.BlockSpec((tile, model), lambda i: (i, 0)),
            whole(model, model),
        ]
        + [pl.BlockSpec(memory_space=pl.ANY)] * len(kept),
        out_specs=[
            pl.BlockSpec((2, rows, tile), lambda i: (0, half, i)),
            whole(rows, model), whole(rows, model), whole(model, rows),
        ],
        out_shape=[
            jax.ShapeDtypeStruct((2, 2 * rows, hidden_units), bf16),
            jax.ShapeDtypeStruct((rows, model), f32),
            jax.ShapeDtypeStruct((rows, model), bf16),
            jax.ShapeDtypeStruct((model, rows), bf16),
        ],
        scratch_shapes=[pltpu.VMEM((rows, model), f32)],
        input_output_aliases={9: 0} if kept else {},
        compiler_params=pltpu.CompilerParams(vmem_limit_bytes=48 * 2**20),
        name="feed_forward_back",
        cost_estimate=cost(18, HEAVY),
    )


def project(normed, w, first, lanes, cosine, sine, heads, scale, name, wait_for=(), split=True):
    rows, model = normed.shape

    cuts = [heads * HD, lanes - heads * HD]
    cuts = [n for n in cuts if n] if split else [lanes]

    def kernel(x_ref, w_ref, cos_ref, sin_ref, out_ref, *rest_ref):
        y = product(x_ref[...], w_ref[:, first : first + lanes], 1, 0).T
        turned = turn(y[: heads * HD], cos_ref[...], sin_ref[...], heads)
        out_ref[: heads * HD, :] = turned.astype(bf16) * bf16(scale)
        if heads * HD < lanes:
            ref, start = (rest_ref[0], 0) if split else (out_ref, heads * HD)
            ref[start:, :] = y[heads * HD :].astype(bf16)

    whole = lambda *shape: pl.BlockSpec(shape, lambda i: (0,) * len(shape))
    width = first + lanes if (first + lanes) % 128 == 0 else w.shape[1]
    return call(
        kernel,
        [normed, w, cosine, sine],
        wait_for,
        grid=(1,),
        in_specs=[
            whole(rows, model), whole(model, width), whole(HD // 2, rows), whole(HD // 2, rows)
        ],
        out_specs=[whole(n, rows) for n in cuts],
        out_shape=[jax.ShapeDtypeStruct((n, rows), bf16) for n in cuts],
        compiler_params=pltpu.CompilerParams(vmem_limit_bytes=24 * 2**20),
        name=name,
        cost_estimate=cost(2),
    )


def projected_kv(normed, projections, tables, split):
    return project(
        normed, projections, 0, 2 * KV, *tables, KV_HEADS, 1.0, "keys_values", (), split
    )


def projected_q(normed, projections, tables, wait_for):
    first, lanes = 2 * KV, HEADS * HD
    return project(
        normed, projections, first, lanes, *tables, HEADS, HD**-0.5, "queries", wait_for
    )[0]


def attention(normed, kv, projections, where, tables, before):
    count = lax.axis_size("fsdp")
    kvs = [kv]
    for step in range(1, count):
        kvs.append([climb(v, step) for v in kvs[-1]])
    q = projected_q(normed, projections, tables, kv[:1])
    state = []
    for d in range(count):
        wait_for = ()
        if d in before:
            wait_for, state = before[d](state)
        state = attend(d, count, where, q, kvs[d], state, wait_for)
    return q, kvs, state


def attention_gradient(d_mixture, low, saved, where, tables, before, at_end):
    q, kvs, (mixture, lse) = saved[1:]
    count = lax.axis_size("fsdp")
    dq = moving = got = None
    for d in reversed(range(count)):
        step = count - 1 - d
        wait_for = []
        if d in before:
            wait_for, dq = before[d](dq)
        if step:
            got = lax.ppermute(
                moving, "fsdp", [(i, i - 1) for i in range(count - step, count)]
            )
        dq, dkv = attend_back(
            d, where, q, mixture, d_mixture, lse, kvs[d], dq, tables, wait_for
        )
        if d:
            moving = add(dkv, got) if step else dkv
    wait_for, dq = at_end(dq)
    return gradient_columns(dkv, got, dq, low, tables, wait_for)


def layer_gradient(d_hidden, columns, norm, gain, w_qkv):
    normed, unit, scale = norm
    d_normed = dot(columns[:, : w_qkv.shape[1]], w_qkv, "tf,df->td")
    return d_hidden + normalize_back(d_normed, gain, unit, scale)


def local(
    tokens,
    lengths,
    cotangent,
    attention_gain,
    feedforward_gain,
    query_weight,
    key_weight,
    value_weight,
    out_weight,
    gate_weight,
    up_weight,
    down_weight,
):
    rows = tokens.shape[1]
    count = lax.axis_size("fsdp")
    z = lax.axis_index("fsdp")
    low, core, one, two = place()
    positions = z * rows + jnp.arange(rows, dtype=jnp.int32)
    length = lengths[0]
    where = jnp.stack([z, length - z * rows]).astype(jnp.int32)
    frequency = rotary_base ** (-jnp.arange(HD // 2, dtype=f32) * 2.0 / HD)
    angles = frequency[:, None] * positions.astype(f32)[None, :]
    tables = (jnp.cos(angles), jnp.sin(angles))
    block = query_weight.shape[0]
    model = block * count
    hidden_units = gate_weight.shape[1]

    projections = jnp.concatenate([key_weight, value_weight, query_weight, out_weight], axis=1)
    lanes = projections.shape[1] // 4
    f_lanes = hidden_units // 4
    down_rows = down_weight.shape[0] // 8
    own_gains = jnp.stack([attention_gain, feedforward_gain])
    piece = projection_piece(projections, low, core)
    held = piece.shape[0]
    own = lax.optimization_barrier(
        (
            jnp.concatenate([piece, jnp.pad(own_gains, ((0, 14), (0, lanes - block)))]),
            gate_up_piece(gate_weight, up_weight, low, core),
            down_piece(down_weight, low),
        )
    )
    blocks = other_blocks(own[0])
    gains = all_blocks(jnp.stack([v[held : held + 2, :block] for v in blocks[::-1]]), own_gains)
    to_proj = Gather([v[:held] for v in blocks])
    to_proj.hop()
    to_proj.hop_on()
    rest = jnp.pad(own[2][:, f_lanes:], ((0, 0), (0, 2 * f_lanes - model)))
    wide = jnp.concatenate([own[1], own[2][:, :f_lanes], rest])
    wide = lax.all_gather(wide, "fsdp")
    wide = [
        lax.dynamic_index_in_dim(wide, (z + count - o) % count, 0, keepdims=False)
        for o in range(1, count)
    ]
    to_gate_up = Gather([v[:block] for v in wide])
    to_down = Gather(
        [
            jnp.concatenate(
                [v[block : block + down_rows], v[block + down_rows :, : model - f_lanes]], axis=1
            )
            for v in wide
        ]
    )
    to_gate_up.hop()
    to_down.hop()
    gains = jnp.moveaxis(gains, 0, 1).reshape(2, model).astype(f32)
    projections = whole_projections(
        projections, low, to_proj.cross(), [to_gate_up.mine, to_down.mine]
    )
    w_qkv = projections[:, : 2 * KV + model]

    start = tokens[0].astype(f32)
    norm_1 = normalize(start, gains[0])
    normed = norm_1[0]
    kv = projected_kv(normed, projections, tables, False)


    def first_arrived(state):
        here = (to_gate_up.a, to_gate_up.b, to_down.a, to_down.b)
        state, here = together(state, here)
        to_gate_up.a, to_gate_up.b, to_down.a, to_down.b = here
        to_gate_up.hop_on()
        to_down.hop_on()
        return (), state

    def second_arrived(state):
        state, here = together(state, (to_gate_up.ab, to_down.ab))
        to_gate_up.ab, to_down.ab = here
        return (), state

    saved_first = (norm_1,) + attention(
        normed, kv, projections, where, tables,
        {2: first_arrived, 3: second_arrived},
    )
    mixture = saved_first[3][0]
    w_o = projections[:, 2 * KV + model :]
    w_down = whole_down(down_weight, low, to_down.cross())
    w_gate, w_up = whole_gate_up(gate_weight, up_weight, low, to_gate_up.cross())
    middle, hidden_1, gate_1, up_1, *kept = feed_forward(
        start, mixture, w_o, gains[1], w_gate, w_up, w_down, []
    )

    norm_2 = normalize(middle, gains[0])
    kv = projected_kv(norm_2[0], projections, tables, True)
    half_rows = block // 2

    def left_of(normed, mixture):
        rows_of = jnp.stack([normed.T, mixture]).reshape(2, count, 2, half_rows, rows)
        return jnp.pad(rows_of, ((0, 0),) * 3 + ((0, held - half_rows), (0, 0)))

    left_1 = left_of(norm_1[0], mixture)
    saved_second = (norm_2,) + attention(
        norm_2[0], kv, projections, where, tables, {1: lambda state: (left_1, state)}
    )
    final, hidden_2, gate_2, up_2, nft, active = feed_forward(
        middle, saved_second[3][0], w_o, gains[1], w_gate, w_up, w_down, kept
    )

    real = (positions < length).astype(f32)
    gradient = cotangent[0].astype(f32) * real[:, None]
    down_back = (gradient.astype(bf16),)
    left = jnp.concatenate([left_of(norm_2[0], saved_second[3][0]), left_1], axis=-1)
    d_gu, d_hidden, low_2, d_mixture = feed_forward_back(
        gradient, hidden_2, gains[1], gate_2, up_2, w_gate, w_up, w_down, w_o, [], [left]
    )
    columns_2 = attention_gradient(
        d_mixture, low_2, saved_second, where, tables, {}, lambda dq: ((), dq)
    )
    gradient = layer_gradient(d_hidden, columns_2, norm_2, gains[0], w_qkv)

    down_back = jnp.concatenate(down_back + (gradient.astype(bf16),))
    active = active.reshape(count, 8, down_rows, 2 * rows)
    theirs, ours = ids_of(low ^ 1), ids_of(low)

    def down_pieces(ids, got, wait_for):
        return grad_pieces(
            ids, got, [active, down_back],
            [
                pl.BlockSpec((count, 1, down_rows, 2 * rows), lambda i, ids: (0, ids[i], 0, 0)),
                pl.BlockSpec((2 * rows, model), lambda i, ids: (0, 0)),
            ],
            flat_product, (count, down_rows, model), 1.4, wait_for,
        )

    send, token = down_pieces(theirs, None, ())
    to_down = Reduction(send)
    away, home, token = down_pieces(ours, to_down.got, [token])
    to_down.hop(away, [home[0]], [home[1]])
    d_gu, d_hidden, low_1, d_mixture = feed_forward_back(
        gradient, hidden_1, gains[1], gate_1, up_1, w_gate, w_up, w_down, w_o, [d_gu], [token]
    )

    def gate_up_pieces(ids, got, wait_for):
        return grad_pieces(
            ids, got, [nft, d_gu],
            [
                pl.BlockSpec((model, 2 * rows), lambda i, ids: (0, 0)),
                pl.BlockSpec(
                    (1, 2 * rows, f_lanes), lambda i, ids: (ids[i] % 2, 0, ids[i] // 2)
                ),
            ],
            flat_product, (count, block, f_lanes), 2.2, wait_for,
        )

    send, token = gate_up_pieces(theirs, None, ())
    to_gate_up = Reduction(send)
    to_down.came, d_hidden = together(to_down.came, d_hidden)
    to_down.hop_on()

    def third(dq):
        return [token], dq

    def second(dq):
        away, home, token = gate_up_pieces(ours, to_gate_up.got, [dq])
        to_gate_up.hop(away, [home[0]], [home[1]])
        dq, to_down.came = together(dq, to_down.came)
        to_down.settle()
        return [token], dq

    def zeroth(dq):
        dq, to_gate_up.came = together(dq, to_gate_up.came)
        to_gate_up.add_up()
        dq, to_gate_up.far, to_down.cuts = together(dq, to_gate_up.far, to_down.cuts)
        to_gate_up.go_on()
        to_down.shift()
        return (), dq

    columns_1 = attention_gradient(
        d_mixture, low_1, saved_first, where, tables,
        {3: third, 2: second, 0: zeroth}, lambda dq: ((), dq),
    )
    columns_1, to_gate_up.came, to_down.came = together(
        columns_1, to_gate_up.came, to_down.came
    )
    to_gate_up.settle()
    to_gate_up.shift()

    def compute_proj(pid, put, a, b, right_2, right_1):
        right = jnp.concatenate([right_2[...], right_1[...]], axis=0)

        def product_of(ref):
            total = product(ref[...].reshape(count * held, 2 * rows), right, 1, 0)
            return total.reshape(count, held, lanes)[:, :half_rows]

        @pl.when(pid // 2 != 2)
        def _():
            put(product_of(a))

        @pl.when(pid // 2 == 2)
        def _():
            lane = lax.broadcasted_iota(jnp.int32, (count, half_rows, lanes), 2)
            put(jnp.where(lane < lanes // 2, product_of(a), product_of(b)))

    def proj_pieces(ids, wait_for, us):
        def left_spec(k):
            return pl.BlockSpec(
                (1, count, 1, held, 2 * rows),
                lambda i, ids: (jnp.where(ids[i] // 2 * 2 + k > 4, 1, 0), 0, ids[i] % 2, 0, 0),
            )

        right_spec = pl.BlockSpec((rows, lanes), lambda i, ids: (0, ids[i] // 2))
        return grad_pieces(
            ids, None, [left, left, columns_2, columns_1],
            [left_spec(0), left_spec(1), right_spec, right_spec],
            compute_proj, (count, half_rows, lanes), us, wait_for, 24,
        )

    send, token = proj_pieces(theirs, to_gate_up.cuts[0], 2)
    to_proj = Reduction(send)
    keep, token = proj_pieces(ours, [token], 0.01)
    down_handed = hand(to_down.total())
    keep, down_handed[1:3] = together(keep, down_handed[1:3])
    down_handed[3] = swap(down_handed[2], first_hop)
    got = to_proj.got
    to_proj.hop(add(keep[:2], got[:2]), [keep[2], got[2]], [keep[3], got[3]])
    (
        to_proj.came, to_gate_up.came[0], to_gate_up.came[2], down_handed[3]
    ) = together(
        to_proj.came, to_gate_up.came[0], to_gate_up.came[2], down_handed[3]
    )
    to_proj.hop_on()
    to_proj.settle()
    to_proj.cuts, to_gate_up.came[1] = together(to_proj.cuts, to_gate_up.came[1])
    gate_up_handed = hand(to_gate_up.total())
    to_proj.shift()
    proj_mine, gate_up_handed[1:] = together(to_proj.total(), gate_up_handed[1:])
    gradient = layer_gradient(d_hidden, columns_1, norm_1, gains[0], w_qkv)
    g_down = give(down_handed)
    proj_handed = hand(proj_mine)
    gate_up_handed[0], proj_handed[2] = together(gate_up_handed[0], proj_handed[2])
    proj_handed[3] = swap(proj_handed[2], first_hop)
    g_gate_up = give(gate_up_handed)

    def put_down(refs, q, c, pid, value):
        refs[0][pl.ds(pl.multiple_of(pid * down_rows, 8), down_rows), :] = value

    def put_gate_up(refs, q, c, pid, value):
        refs[c][:, lanes_at(q * f_lanes, f_lanes)] = value

    widths = [KV, KV, model, model]

    def put_proj(refs, q, c, pid, value):
        here = slice(c * half_rows, (c + 1) * half_rows)
        for quarter in range(4):

            @pl.when(q == quarter)
            def _():
                first = 0
                for ref, width in zip(refs, widths):
                    start = max(first, quarter * lanes)
                    stop = min(first + width, (quarter + 1) * lanes)
                    if start < stop:
                        ref[here, start - first : stop - first] = value[
                            :, start - quarter * lanes : stop - quarter * lanes
                        ]
                    first += width

    g_down = spread(low, g_down, [(8 * down_rows, model)], put_down)[0]
    g_gate, g_up = spread(low, g_gate_up, [(block, hidden_units)] * 2, put_gate_up)
    g_gate, g_up, proj_handed[3] = together(g_gate, g_up, proj_handed[3])
    g_proj = give(proj_handed)
    g_k, g_v, g_q, g_o = spread(
        low, g_proj, [(block, w) for w in widths], put_proj
    )

    def gain_gradient(gain, pairs):
        along = sum(jnp.sum(w.astype(f32) * g, axis=1) for w, g in pairs)
        return along / gain.astype(f32)

    g_attention_gain = gain_gradient(
        attention_gain, [(query_weight, g_q), (key_weight, g_k), (value_weight, g_v)]
    )
    g_feedforward_gain = gain_gradient(
        feedforward_gain, [(gate_weight, g_gate), (up_weight, g_up)]
    )

    return (
        final.astype(bf16)[None],
        gradient.astype(bf16)[None],
        g_attention_gain,
        g_feedforward_gain,
        g_q,
        g_k,
        g_v,
        g_o,
        g_gate,
        g_up,
        g_down,
    )


def solution(mesh):
    rows = P("fsdp", None)
    placed = (P("dp", "fsdp", None), P("dp"), P("dp", "fsdp", None), P("fsdp"), P("fsdp")) + (
        rows,
    ) * 7
    return jax.shard_map(
        local,
        mesh=mesh,
        in_specs=placed,
        out_specs=(P("dp", "fsdp", None), P("dp", "fsdp", None), P("fsdp"), P("fsdp"))
        + (rows,) * 7,
        check_vma=False,
    )
```

```python
import jax
import jax.numpy as jnp
from jax import lax
from jax.experimental import pallas as pl
from jax.experimental.pallas import tpu as pltpu
from jax.sharding import PartitionSpec as P

HEADS = 15
KV_HEADS = 5
HD = 64
GROUP = HEADS // KV_HEADS
KV = KV_HEADS * HD

norm_epsilon = 1e-05
rotary_base = 10000.0

bf16 = jnp.bfloat16
f32 = jnp.float32


def first_hop(i):
    return i ^ (4 if i & 1 else 2)


def second_hop(i):
    return i ^ (2 if i & 1 else 4)


def sibling(i):
    return i ^ 1


def swap(value, hop):
    count = lax.axis_size("dp")
    return lax.ppermute(value, "dp", [(i, hop(i)) for i in range(count)])


def climb(value, step):
    count = lax.axis_size("fsdp")
    return lax.ppermute(value, "fsdp", [(i, i + 1) for i in range(step - 1, count - 1)])


def descend(value, step):
    count = lax.axis_size("fsdp")
    return lax.ppermute(value, "fsdp", [(i, i - 1) for i in range(1, count - step + 1)])


def place():
    low = lax.axis_index("dp") % 8
    core = low % 2
    one = jnp.where(core == 1, 4, 2)
    return low, core, one, 6 - one


def around(value, distance):
    count = lax.axis_size("fsdp")
    return lax.ppermute(value, "fsdp", [(i, (i + distance) % count) for i in range(count)])


def together(*values):
    return lax.optimization_barrier(values)


def call(kernel, operands, wait_for=(), scalars=0, in_specs=(), grid=(), **rest):
    wait_for = jax.tree.leaves(wait_for)
    last = len(operands)

    def waiting(*refs):
        kernel(*refs[:last], *refs[last + len(wait_for) :])

    in_specs = list(in_specs) + [pl.BlockSpec(memory_space=pl.ANY)] * len(wait_for)
    where = dict(in_specs=in_specs, out_specs=rest.pop("out_specs"))
    scratch = rest.pop("scratch_shapes", ())
    if scalars:
        where = dict(
            grid_spec=pltpu.PrefetchScalarGridSpec(
                num_scalar_prefetch=scalars, grid=grid, scratch_shapes=scratch, **where
            )
        )
    else:
        where.update(grid=grid, scratch_shapes=scratch)
    return pl.pallas_call(waiting, **where, **rest)(*operands, *wait_for)


class Gather:
    def __init__(self, blocks):
        self.blocks = blocks

    def hop(self):
        self.mine = jnp.stack(self.blocks)
        self.a = swap(self.mine, first_hop)
        self.b = swap(self.mine, second_hop)

    def hop_on(self):
        self.ab = swap(self.a, second_hop)

    def cross(self):
        mine = [self.mine, self.a, self.b, self.ab]
        return mine + [swap(v, sibling) for v in mine]


def other_blocks(own):
    return [around(own, o) for o in range(1, lax.axis_size("fsdp"))]


def piece_ids(low):
    odd = low % 2
    one = 2 + 2 * odd
    two = 6 - one
    return [low, low ^ one, low ^ two, low ^ 6, low ^ 1, low ^ 1 ^ two, low ^ 1 ^ one, low ^ 7]


def lay_out(low, pieces, own, out_shapes, moves, wait_for=()):
    count = lax.axis_size("fsdp")
    where = jnp.stack([lax.axis_index("fsdp"), low]).astype(jnp.int32)

    def kernel(where_ref, *refs):
        piece_refs, refs = refs[:8], refs[8:]
        own_refs, refs = refs[: len(own)], refs[len(own) :]
        outs = refs
        z, low = where_ref[0], where_ref[1]
        for core in range(2):

            @pl.when(low % 2 == core)
            def _():
                copies = []
                for k, pid in enumerate(piece_ids(low)):
                    own_core = core if k < 4 else 1 - core
                    for o in range(count - 1):
                        block = lax.rem(z + count - 1 - o, count)
                        copies += moves(piece_refs[k].at[o], block, pid // 2, own_core, pid, outs)
                for source, target in copies + own_moves(own_refs, z, outs):
                    target[...] = source[...]

    moves, own_moves = moves
    vmem = pl.BlockSpec(memory_space=pltpu.VMEM)
    return call(
        kernel,
        [where, *pieces, *own],
        wait_for,
        in_specs=[pl.BlockSpec(memory_space=pltpu.SMEM)] + [vmem] * (8 + len(own)),
        out_specs=[vmem] * len(out_shapes),
        out_shape=[jax.ShapeDtypeStruct(shape, bf16) for shape in out_shapes],
        compiler_params=pltpu.CompilerParams(vmem_limit_bytes=26 * 2**20),
        name="lay_out",
        cost_estimate=cost(5),
    )


def rows_at(start, size):
    return pl.ds(pl.multiple_of(start, 16), size)


def lanes_at(start, size):
    return pl.ds(start if isinstance(start, int) else pl.multiple_of(start, 128), size)


def projection_piece(shard, low, core):
    block, width = shard.shape
    rest = block // 2 // 16 * 16
    lanes = width // 4
    return lax.dynamic_slice(shard, (core * rest, low // 2 * lanes), (block - rest, lanes))


def gate_up_piece(gate, up, low, core):
    lanes = gate.shape[1] // 4
    gate, up = (lax.dynamic_slice_in_dim(v, low // 2 * lanes, lanes, 1) for v in (gate, up))
    return jnp.where(core == 1, up, gate)


def down_piece(shard, low):
    rows = shard.shape[0] // 8
    return lax.dynamic_slice_in_dim(shard, low * rows, rows, 0)


def whole_projections(shard, low, pieces, wait_for):
    count = lax.axis_size("fsdp")
    block, width = shard.shape
    lanes = width // 4
    rest = block // 2 // 16 * 16
    held = block - rest

    def moves(src, z, q, c, pid, outs):
        size = held if c else rest
        return [
            (
                src.at[pl.ds(0, size)],
                outs[0].at[rows_at(z * block + c * rest, size), lanes_at(q * lanes, lanes)],
            )
        ]

    def own_moves(refs, z, outs):
        return [(refs[0], outs[0].at[rows_at(z * block, block)])]

    return lay_out(
        low, pieces, [shard], [(count * block, width)], (moves, own_moves), wait_for
    )[0]


def whole_gate_up(gate, up, low, pieces):
    count = lax.axis_size("fsdp")
    block, width = gate.shape
    lanes = width // 4

    def moves(src, z, q, c, pid, outs):
        return [(src, outs[c].at[rows_at(z * block, block), lanes_at(q * lanes, lanes)])]

    def own_moves(refs, z, outs):
        return [(refs[k], outs[k].at[rows_at(z * block, block)]) for k in range(2)]

    return lay_out(low, pieces, [gate, up], [(count * block, width)] * 2, (moves, own_moves))


def whole_down(shard, low, pieces):
    count = lax.axis_size("fsdp")
    block, width = shard.shape
    rows = block // 8

    def moves(src, z, q, c, pid, outs):
        return [(src, outs[0].at[rows_at(z * block + pid * rows, rows)])]

    def own_moves(refs, z, outs):
        return [(refs[0], outs[0].at[rows_at(z * block, block)])]

    return lay_out(low, pieces, [shard], [(count * block, width)], (moves, own_moves))[0]


def all_blocks(others, own):
    count = lax.axis_size("fsdp")
    z = lax.axis_index("fsdp")
    both = jnp.concatenate([own[None], others])
    return jnp.stack(
        [
            lax.dynamic_index_in_dim(both, (k - z + count) % count, 0, keepdims=False)
            for k in range(count)
        ]
    )


def add(*terms):
    return sum(v.astype(f32) for v in terms).astype(bf16)


def cost(us, weight=6):
    return pl.CostEstimate(
        flops=int(us * weight * 1.15e9), bytes_accessed=0, transcendentals=0
    )


HEAVY = 6


class Reduction:
    def __init__(self, send):
        self.got = swap(send, sibling)

    def hop(self, away, near, far):
        self.near, self.far = near, far
        self.came = swap(away, first_hop)

    def hop_on(self):
        self.add_up()
        self.go_on()

    def add_up(self):
        self.far = add(*self.far, self.came[1])
        self.near = add(*self.near, self.came[0])

    def go_on(self):
        self.came = swap(self.far, second_hop)

    def settle(self):
        count, z = lax.axis_size("fsdp"), lax.axis_index("fsdp")
        self.near = add(self.near, self.came)
        self.cuts = [
            lax.dynamic_index_in_dim(self.near, (z + o) % count, 0, keepdims=False)
            for o in range(count)
        ]

    def shift(self):
        count = lax.axis_size("fsdp")
        self.came = [around(self.cuts[o], o) for o in range(1, count)]

    def total(self):
        return over_rest(add(self.cuts[0], *self.came))


def over_rest(mine):
    wide = lax.axis_size("dp")
    if wide > 8:
        groups = [[i + 8 * k for k in range(wide // 8)] for i in range(8)]
        mine = lax.psum(mine, "dp", axis_index_groups=groups)
    return mine


def hand(mine):
    b = swap(mine, second_hop)
    a, ab = swap(mine, first_hop), swap(b, first_hop)
    return [mine, a, b, ab]


def give(handed):
    return handed + [swap(v, sibling) for v in handed]


def ids_of(low):
    one = 2 + 2 * (low % 2)
    return [low ^ one, low ^ 6, low, low ^ 6 ^ one]


def spread(low, pieces, out_shapes, put, wait_for=()):
    def turn_out(shape):
        wide, high = (-(-n // 128) * 128 for n in shape[::-1])
        return shape[0] * wide > shape[1] * high

    def kernel(where_ref, *refs):
        low = where_ref[0]
        outs, rest = list(refs[8 : 8 + len(out_shapes)]), list(refs[8 + len(out_shapes) :])
        targets = [rest.pop(0) if turn_out(s) else v for s, v in zip(out_shapes, outs)]
        for core in range(2):

            @pl.when(low % 2 == core)
            def _():
                for k, pid in enumerate(piece_ids(low)):
                    own_core = core if k < 4 else 1 - core
                    put(targets, pid // 2, own_core, pid, refs[k][...].astype(f32))

        for target, out in zip(targets, outs):
            if target is not out:
                out[...] = target[...].T

    vmem = pl.BlockSpec(memory_space=pltpu.VMEM)
    turned = [turn_out(shape) for shape in out_shapes]
    shapes = [shape[::-1] if t else shape for shape, t in zip(out_shapes, turned)]
    out = call(
        kernel,
        [low[None], *pieces],
        wait_for,
        in_specs=[pl.BlockSpec(memory_space=pltpu.SMEM)] + [vmem] * 8,
        out_specs=[vmem] * len(out_shapes),
        out_shape=[jax.ShapeDtypeStruct(shape, f32) for shape in shapes],
        scratch_shapes=[pltpu.VMEM(s, f32) for s, t in zip(out_shapes, turned) if t],
        compiler_params=pltpu.CompilerParams(vmem_limit_bytes=22 * 2**20),
        name="spread",
        cost_estimate=cost(3),
    )
    return [v.T if t else v for v, t in zip(out, turned)]


def grad_pieces(
    ids, got, operands, in_specs, compute, piece_shape, us, wait_for, vmem=56
):
    block = (1,) + piece_shape
    zeros = (0,) * len(piece_shape)
    in_specs, operands = list(in_specs), list(operands)
    n = len(ids)
    if got is None:
        out_specs = [pl.BlockSpec(block, lambda i, ids: (i,) + zeros)]
        out_shape = [jax.ShapeDtypeStruct((n,) + piece_shape, bf16)]
    else:
        in_specs.append(pl.BlockSpec(block, lambda i, ids: (i,) + zeros))
        operands.append(got)
        half = n // 2
        out_specs = [
            pl.BlockSpec(block, lambda i, ids: (jnp.minimum(i, half - 1),) + zeros),
            pl.BlockSpec(block, lambda i, ids: (jnp.maximum(i - half, 0),) + zeros),
        ]
        out_shape = [jax.ShapeDtypeStruct((half,) + piece_shape, bf16)] * 2

    out_specs.append(pl.BlockSpec((8, 128), lambda i, ids: (0, 0)))
    out_shape.append(jax.ShapeDtypeStruct((8, 128), f32))

    def kernel(ids_ref, *refs):
        step = pl.program_id(0)
        refs[-1][...] = jnp.zeros((8, 128), f32)
        refs = refs[:-1]
        if got is None:

            def put(total):
                refs[-1][...] = total.astype(bf16).reshape(block)

            compute(ids_ref[step], put, *refs[:-1])
        else:

            def put(total):
                total = (total + refs[-3][...].reshape(total.shape).astype(f32)).astype(bf16)

                @pl.when(step < half)
                def _():
                    refs[-2][...] = total.reshape(block)

                @pl.when(step >= half)
                def _():
                    refs[-1][...] = total.reshape(block)

            compute(ids_ref[step], put, *refs[:-3])

    return call(
        kernel,
        [jnp.stack(ids).astype(jnp.int32), *operands],
        wait_for,
        scalars=1,
        grid=(n,),
        in_specs=in_specs,
        out_specs=out_specs,
        out_shape=out_shape,
        compiler_params=pltpu.CompilerParams(vmem_limit_bytes=vmem * 2**20),
        name="weight_grad",
        cost_estimate=cost(us * n, HEAVY),
    )


def flat_product(pid, put, left_ref, right_ref):
    left, right = left_ref[...], right_ref[...]
    put(product(left.reshape(-1, left.shape[-1]), right.reshape(right.shape[-2:]), 1, 0))


def product(a, b, over_a, over_b):
    return lax.dot_general(
        a, b, (((over_a,), (over_b,)), ((), ())), preferred_element_type=f32
    )


def side_by_side(x):
    return jnp.concatenate([x[HD * g : HD * (g + 1)] for g in range(GROUP)], axis=1)


def diagonal_mask(scores, rows, room):
    key = lax.broadcasted_iota(jnp.int32, (rows, rows), 0)
    query = lax.broadcasted_iota(jnp.int32, (rows, rows), 1)
    seen = (key <= query) & (key < room)
    return jnp.where(jnp.concatenate([seen] * GROUP, axis=1), scores, -1e30)


SUMS = 16


def attend_kernel(d, n, place_ref, q_ref, *refs):
    joined = refs[0].shape[0] > KV
    k_ref, v_ref = refs[0], refs[0 if joined else 1]
    refs = refs[1 if joined else 2 :]
    first, last = d == 0, d == n - 1
    m1_ref, a1_ref = (None, None) if first else refs[:2]
    m2_ref, a2_ref = refs[-2:]
    z, room = place_ref[0], place_ref[1]
    rows = q_ref.shape[1]

    @pl.when(z >= d)
    def _():
        ones = jnp.ones((SUMS, rows), bf16)
        for h in range(KV_HEADS):
            q = side_by_side(q_ref[GROUP * HD * h : GROUP * HD * (h + 1), :])
            k = k_ref[HD * h : HD * (h + 1), :]
            start = HD * h + (KV if joined else 0)
            v = v_ref[start : start + HD, :]
            s = product(k, q, 0, 0)
            if first:
                s = diagonal_mask(s, rows, room)
            m = jnp.max(s, axis=0, keepdims=True)
            if not first:
                m = jnp.maximum(m, m1_ref[h])
            p = jnp.exp(s - m).astype(bf16)
            total = product(jnp.concatenate([v, ones], axis=0), p, 1, 0)
            if not first:
                total = total + a1_ref[h] * jnp.exp(m1_ref[h] - m)
            m2_ref[h] = m
            a2_ref[h] = total

    if not first:

        @pl.when(z < d)
        def _():
            m2_ref[...] = m1_ref[...]
            a2_ref[...] = a1_ref[...]

    if last:
        o_ref, lse_ref = refs[2:4]
        for h in range(KV_HEADS):
            l = a2_ref[h, HD : HD + 1, :]
            o = (a2_ref[h, :HD, :] / l).astype(bf16)
            lse = m2_ref[h] + jnp.log(l)
            for g in range(GROUP):
                here = slice(HD * (GROUP * h + g), HD * (GROUP * h + g + 1))
                o_ref[here, :] = o[:, rows * g : rows * (g + 1)]
                lse_ref[h, g : g + 1, :] = lse[:, rows * g : rows * (g + 1)]


def attend(d, n, where, q, kv, state, wait_for):
    rows = q.shape[1]
    state_shapes = [(KV_HEADS, 1, GROUP * rows), (KV_HEADS, HD + SUMS, GROUP * rows)]
    out_shape = [jax.ShapeDtypeStruct(shape, f32) for shape in state_shapes]
    scratch = []
    if d == n - 1:
        scratch = [pltpu.VMEM(shape, f32) for shape in state_shapes]
        out_shape = [
            jax.ShapeDtypeStruct(q.shape, bf16),
            jax.ShapeDtypeStruct((KV_HEADS, GROUP, rows), f32),
        ]
    vmem = pl.BlockSpec(memory_space=pltpu.VMEM)
    return call(
        lambda *refs: attend_kernel(d, n, *refs),
        [where, q, *kv, *state],
        wait_for,
        in_specs=[pl.BlockSpec(memory_space=pltpu.SMEM)] + [vmem] * (1 + len(kv) + len(state)),
        out_specs=[vmem, vmem],
        out_shape=out_shape,
        scratch_shapes=scratch,
        compiler_params=pltpu.CompilerParams(vmem_limit_bytes=24 * 2**20),
        name="attend",
        cost_estimate=cost(4),
    )


def specs(rows):
    return (
        pl.BlockSpec((GROUP * HD, rows), lambda h, s: (h, 0)),
        pl.BlockSpec((2, HD, rows), lambda h, s: (0, h, 0)),
        pl.BlockSpec((1, GROUP, rows), lambda h, s: (h, 0, 0)),
    )


def turn(columns, cosine, sine, heads):
    half = HD // 2
    parts = []
    for h in range(heads):
        a = columns[HD * h : HD * h + half]
        b = columns[HD * h + half : HD * (h + 1)]
        parts += [a * cosine - b * sine, b * cosine + a * sine]
    return jnp.concatenate(parts, axis=0)


def attend_back_kernel(d, place_ref, q_ref, o_ref, do_ref, lse_ref, k_ref, v_ref, *refs):
    dq_ref, dk_ref, dv_ref = refs[-3:]
    before_ref = None if len(refs) == 3 else refs[-4]
    z, room = place_ref[0], place_ref[1]
    rows = q_ref.shape[1]

    @pl.when(z >= d)
    def _():
        q, do, o = (side_by_side(r[...]) for r in (q_ref, do_ref, o_ref))
        lse = jnp.concatenate([lse_ref[0, g : g + 1, :] for g in range(GROUP)], axis=1)
        delta = jnp.sum(do.astype(f32) * o.astype(f32), axis=0, keepdims=True)
        k, v = k_ref[...], v_ref[...]
        s = product(k, q, 0, 0)
        if d == 0:
            s = diagonal_mask(s, rows, room)
        p = jnp.exp(s - lse)
        dp = product(v, do, 0, 0)
        ds = (p * (dp - delta)).astype(bf16)
        dv_ref[...] = product(p.astype(bf16), do, 1, 1).T.astype(bf16)
        dk_ref[...] = product(ds, q, 1, 1).T.astype(bf16)
        dq = product(k, ds, 1, 0) * HD ** (-0.5)
        for g in range(GROUP):
            here = slice(HD * g, HD * (g + 1))
            part = dq[:, rows * g : rows * (g + 1)]
            if before_ref is not None:
                part = part + before_ref[here, :]
            if d == 0:
                part = turn(part, refs[0][...], -refs[1][...], 1).astype(bf16)
            dq_ref[here, :] = part

    if d > 0:

        @pl.when(z < d)
        def _():
            dk_ref[...] = jnp.zeros(dk_ref.shape, bf16)
            dv_ref[...] = jnp.zeros(dv_ref.shape, bf16)
            if before_ref is None:
                dq_ref[...] = jnp.zeros(dq_ref.shape, f32)
            else:
                dq_ref[...] = before_ref[...]


def attend_back(d, where, q, o, do, lse, kv, before, tables, wait_for):
    rows = q.shape[1]
    q_spec, kv_spec, lse_spec = specs(rows)
    k_spec = pl.BlockSpec((HD, rows), lambda h, s: (h, 0))
    skip = 0 if len(kv) > 1 else KV_HEADS
    v_spec = pl.BlockSpec((HD, rows), lambda h, s: (skip + h, 0))
    extra, extra_specs = [], []
    if d == 0:
        extra = list(tables)
        extra_specs = [pl.BlockSpec((HD // 2, rows), lambda h, s: (0, 0))] * 2
    if before is not None:
        extra.append(before)
        extra_specs.append(q_spec)
    return call(
        lambda *refs: attend_back_kernel(d, *refs),
        [where, q, o, do, lse, kv[0], kv[-1], *extra],
        wait_for,
        scalars=1,
        grid=(KV_HEADS,),
        in_specs=[q_spec, q_spec, q_spec, lse_spec, k_spec, v_spec] + extra_specs,
        out_specs=[q_spec, k_spec, k_spec],
        out_shape=[
            jax.ShapeDtypeStruct(q.shape, f32 if d else bf16),
            jax.ShapeDtypeStruct((KV, rows), bf16),
            jax.ShapeDtypeStruct((KV, rows), bf16),
        ],
        compiler_params=pltpu.CompilerParams(vmem_limit_bytes=32 * 2**20),
        name="attend_back",
        cost_estimate=cost(7, HEAVY),
    )


def gradient_columns(own, got, dq, low, tables, wait_for):
    rows = dq.shape[1]
    lanes = 2 * KV + dq.shape[0] + low.shape[1]

    def kernel(
        dk_ref, dv_ref, got_k_ref, got_v_ref, dq_ref, low_ref, cos_ref, sin_ref, out_ref
    ):
        dk = dk_ref[...].astype(f32) + got_k_ref[...].astype(f32)
        dv = dv_ref[...].astype(f32) + got_v_ref[...].astype(f32)
        keys = turn(dk, cos_ref[...], -sin_ref[...], KV_HEADS).astype(bf16)
        sides = jnp.concatenate([keys, dv.astype(bf16), dq_ref[...]], axis=0)
        out_ref[...] = jnp.concatenate([sides.T, low_ref[...]], axis=1)

    vmem = pl.BlockSpec(memory_space=pltpu.VMEM)
    return call(
        kernel,
        [*own, *got, dq, low, *tables],
        wait_for,
        in_specs=[vmem] * 8,
        out_specs=vmem,
        out_shape=jax.ShapeDtypeStruct((rows, lanes), bf16),
        compiler_params=pltpu.CompilerParams(vmem_limit_bytes=16 * 2**20),
        name="gradient_columns",
        cost_estimate=cost(0.01),
    )


def dot(a, b, pattern):
    return jnp.einsum(pattern, a, b, preferred_element_type=f32)


def normalize(x, gain):
    scale = lax.rsqrt(jnp.mean(x * x, axis=-1, keepdims=True) + norm_epsilon)
    unit = x * scale
    return (unit * gain).astype(bf16), unit, scale


def normalize_back(grad, gain, unit, scale):
    grad_unit = grad * gain
    return scale * (grad_unit - unit * jnp.mean(grad_unit * unit, axis=-1, keepdims=True))


def feed_forward_kernel(x_ref, mix_ref, wo_ref, gain_ref, wg_ref, wu_ref, wd_ref, *refs):
    result_ref, hidden_ref, gate_ref, up_ref, nft_ref, active_ref, nf_ref = refs[-7:]

    @pl.when(pl.program_id(0) == 0)
    def _():
        hidden = x_ref[...] + product(mix_ref[...], wo_ref[...], 0, 0)
        hidden_ref[...] = hidden
        normed, _, _ = normalize(hidden, gain_ref[...])
        nf_ref[...] = normed
        nft_ref[...] = normed.T
        result_ref[...] = hidden

    normed = nf_ref[...]
    gate = product(normed, wg_ref[...], 1, 0)
    up = product(normed, wu_ref[...], 1, 0)
    active = (gate * jax.nn.sigmoid(gate) * up).astype(bf16)
    gate_ref[...] = gate.astype(bf16)
    up_ref[...] = up.astype(bf16)
    active_ref[...] = active.T
    result_ref[...] += product(active, wd_ref[...], 1, 0)


def feed_forward(x, mixture, w_o, gain, w_gate, w_up, w_down, kept):
    rows, model = x.shape
    hidden_units = w_gate.shape[1]
    tile = hidden_units // 5
    half = 0 if kept else 1
    whole = lambda *shape: pl.BlockSpec(shape, lambda i: (0,) * len(shape))
    wide = lambda n: pl.BlockSpec((n, tile), lambda i: (0, i))
    return pl.pallas_call(
        feed_forward_kernel,
        grid=(5,),
        in_specs=[
            whole(rows, model), whole(model, rows), whole(model, model), whole(1, model),
            wide(model), wide(model), pl.BlockSpec((tile, model), lambda i: (i, 0)),
        ]
        + [pl.BlockSpec(memory_space=pl.ANY)] * len(kept),
        out_specs=[
            whole(rows, model), whole(rows, model), wide(rows), wide(rows),
            pl.BlockSpec((model, rows), lambda i: (0, half)),
            pl.BlockSpec((tile, rows), lambda i: (i, half)),
        ],
        out_shape=[
            jax.ShapeDtypeStruct((rows, model), f32),
            jax.ShapeDtypeStruct((rows, model), f32),
            jax.ShapeDtypeStruct((rows, hidden_units), bf16),
            jax.ShapeDtypeStruct((rows, hidden_units), bf16),
            jax.ShapeDtypeStruct((model, 2 * rows), bf16),
            jax.ShapeDtypeStruct((hidden_units, 2 * rows), bf16),
        ],
        scratch_shapes=[pltpu.VMEM((rows, model), bf16)],
        input_output_aliases={7: 4, 8: 5} if kept else {},
        compiler_params=pltpu.CompilerParams(vmem_limit_bytes=48 * 2**20),
        name="feed_forward",
        cost_estimate=cost(12),
    )(x, mixture, w_o, gain[None], w_gate, w_up, w_down, *kept)


def feed_forward_back_kernel(grad_ref, hidden_ref, gain_ref, gate_ref, up_ref, wg_ref, wu_ref,
                             wd_ref, wo_ref, *refs):
    d_gu_ref, d_hidden_ref, low_ref, d_mix_ref, total_ref = refs[-5:]
    step = pl.program_id(0)
    low = grad_ref[...].astype(bf16)
    d_active = product(low, wd_ref[...], 1, 1)
    gate, up = gate_ref[...].astype(f32), up_ref[...].astype(f32)
    sig = jax.nn.sigmoid(gate)
    d_gate = (d_active * up * sig * (1.0 + gate * (1.0 - sig))).astype(bf16)
    d_up = (d_active * gate * sig).astype(bf16)
    d_gu_ref[0] = d_gate
    d_gu_ref[1] = d_up
    term = product(d_gate, wg_ref[...], 1, 1) + product(d_up, wu_ref[...], 1, 1)

    @pl.when(step == 0)
    def _():
        total_ref[...] = term

    @pl.when(step > 0)
    def _():
        total_ref[...] += term

    @pl.when(step == pl.num_programs(0) - 1)
    def _():
        hidden = hidden_ref[...]
        scale = lax.rsqrt(jnp.mean(hidden * hidden, axis=-1, keepdims=True) + norm_epsilon)
        d_norm = normalize_back(total_ref[...], gain_ref[...], hidden * scale, scale)
        d_hidden = grad_ref[...] + d_norm
        d_hidden_ref[...] = d_hidden
        low = d_hidden.astype(bf16)
        low_ref[...] = low
        d_mix_ref[...] = product(wo_ref[...], low, 1, 1).astype(bf16)


def feed_forward_back(
    grad, hidden, gain, gate, up, w_gate, w_up, w_down, w_o, kept, wait_for=()
):
    rows, model = grad.shape
    half = 1 if kept else 0
    hidden_units = gate.shape[1]
    tile = hidden_units // 5
    whole = lambda *shape: pl.BlockSpec(shape, lambda i: (0,) * len(shape))
    wide = lambda n: pl.BlockSpec((n, tile), lambda i: (0, i))
    return call(
        feed_forward_back_kernel,
        [grad, hidden, gain[None], gate, up, w_gate, w_up, w_down, w_o, *kept],
        wait_for,
        grid=(5,),
        in_specs=[
            whole(rows, model), whole(rows, model), whole(1, model), wide(rows), wide(rows),
            wide(model), wide(model), pl.BlockSpec((tile, model), lambda i: (i, 0)),
            whole(model, model),
        ]
        + [pl.BlockSpec(memory_space=pl.ANY)] * len(kept),
        out_specs=[
            pl.BlockSpec((2, rows, tile), lambda i: (0, half, i)),
            whole(rows, model), whole(rows, model), whole(model, rows),
        ],
        out_shape=[
            jax.ShapeDtypeStruct((2, 2 * rows, hidden_units), bf16),
            jax.ShapeDtypeStruct((rows, model), f32),
            jax.ShapeDtypeStruct((rows, model), bf16),
            jax.ShapeDtypeStruct((model, rows), bf16),
        ],
        scratch_shapes=[pltpu.VMEM((rows, model), f32)],
        input_output_aliases={9: 0} if kept else {},
        compiler_params=pltpu.CompilerParams(vmem_limit_bytes=48 * 2**20),
        name="feed_forward_back",
        cost_estimate=cost(18, HEAVY),
    )


def project(normed, w, first, lanes, cosine, sine, heads, scale, name, wait_for=(), split=True):
    rows, model = normed.shape

    cuts = [heads * HD, lanes - heads * HD]
    cuts = [n for n in cuts if n] if split else [lanes]

    def kernel(x_ref, w_ref, cos_ref, sin_ref, out_ref, *rest_ref):
        y = product(x_ref[...], w_ref[:, first : first + lanes], 1, 0).T
        turned = turn(y[: heads * HD], cos_ref[...], sin_ref[...], heads)
        out_ref[: heads * HD, :] = turned.astype(bf16) * bf16(scale)
        if heads * HD < lanes:
            ref, start = (rest_ref[0], 0) if split else (out_ref, heads * HD)
            ref[start:, :] = y[heads * HD :].astype(bf16)

    whole = lambda *shape: pl.BlockSpec(shape, lambda i: (0,) * len(shape))
    width = first + lanes if (first + lanes) % 128 == 0 else w.shape[1]
    return call(
        kernel,
        [normed, w, cosine, sine],
        wait_for,
        grid=(1,),
        in_specs=[
            whole(rows, model), whole(model, width), whole(HD // 2, rows), whole(HD // 2, rows)
        ],
        out_specs=[whole(n, rows) for n in cuts],
        out_shape=[jax.ShapeDtypeStruct((n, rows), bf16) for n in cuts],
        compiler_params=pltpu.CompilerParams(vmem_limit_bytes=24 * 2**20),
        name=name,
        cost_estimate=cost(2),
    )


def projected_kv(normed, projections, tables, split):
    return project(
        normed, projections, 0, 2 * KV, *tables, KV_HEADS, 1.0, "keys_values", (), split
    )


def projected_q(normed, projections, tables, wait_for):
    first, lanes = 2 * KV, HEADS * HD
    return project(
        normed, projections, first, lanes, *tables, HEADS, HD**-0.5, "queries", wait_for
    )[0]


def attention(normed, kv, projections, where, tables, before):
    count = lax.axis_size("fsdp")
    kvs = [kv]
    for step in range(1, count):
        kvs.append([climb(v, step) for v in kvs[-1]])
    q = projected_q(normed, projections, tables, kv[:1])
    state = []
    for d in range(count):
        wait_for = ()
        if d in before:
            wait_for, state = before[d](state)
        state = attend(d, count, where, q, kvs[d], state, wait_for)
    return q, kvs, state


def attention_gradient(d_mixture, low, saved, where, tables, before, at_end):
    q, kvs, (mixture, lse) = saved[1:]
    count = lax.axis_size("fsdp")
    dq = moving = got = None
    for d in reversed(range(count)):
        step = count - 1 - d
        wait_for = []
        if d in before:
            wait_for, dq = before[d](dq)
        if step:
            pairs = [(i, i - 1) for i in range(count - step, count)]
            got = [lax.ppermute(v, "fsdp", pairs) for v in moving]
        dq, *dkv = attend_back(
            d, where, q, mixture, d_mixture, lse, kvs[d], dq, tables, wait_for
        )
        if d:
            moving = [add(a, b) for a, b in zip(dkv, got)] if step else dkv
    wait_for, dq = at_end(dq)
    return gradient_columns(dkv, got, dq, low, tables, wait_for)


def layer_gradient(d_hidden, columns, norm, gain, w_qkv):
    normed, unit, scale = norm
    d_normed = dot(columns[:, : w_qkv.shape[1]], w_qkv, "tf,df->td")
    return d_hidden + normalize_back(d_normed, gain, unit, scale)


def local(
    tokens,
    lengths,
    cotangent,
    attention_gain,
    feedforward_gain,
    query_weight,
    key_weight,
    value_weight,
    out_weight,
    gate_weight,
    up_weight,
    down_weight,
):
    rows = tokens.shape[1]
    count = lax.axis_size("fsdp")
    z = lax.axis_index("fsdp")
    low, core, one, two = place()
    positions = z * rows + jnp.arange(rows, dtype=jnp.int32)
    length = lengths[0]
    where = jnp.stack([z, length - z * rows]).astype(jnp.int32)
    frequency = rotary_base ** (-jnp.arange(HD // 2, dtype=f32) * 2.0 / HD)
    angles = frequency[:, None] * positions.astype(f32)[None, :]
    tables = (jnp.cos(angles), jnp.sin(angles))
    block = query_weight.shape[0]
    model = block * count
    hidden_units = gate_weight.shape[1]

    projections = jnp.concatenate([key_weight, value_weight, query_weight, out_weight], axis=1)
    lanes = projections.shape[1] // 4
    f_lanes = hidden_units // 4
    down_rows = down_weight.shape[0] // 8
    own_gains = jnp.stack([attention_gain, feedforward_gain])
    piece = projection_piece(projections, low, core)
    held = piece.shape[0]
    own = lax.optimization_barrier(
        (
            jnp.concatenate([piece, jnp.pad(own_gains, ((0, 14), (0, lanes - block)))]),
            gate_up_piece(gate_weight, up_weight, low, core),
            down_piece(down_weight, low),
        )
    )
    blocks = other_blocks(own[0])
    gains = all_blocks(jnp.stack([v[held : held + 2, :block] for v in blocks[::-1]]), own_gains)
    to_proj = Gather([v[:held] for v in blocks])
    to_proj.hop()
    to_proj.hop_on()
    rest = jnp.pad(own[2][:, f_lanes:], ((0, 0), (0, 2 * f_lanes - model)))
    wide = jnp.concatenate([own[1], own[2][:, :f_lanes], rest])
    wide = lax.all_gather(wide, "fsdp")
    wide = [
        lax.dynamic_index_in_dim(wide, (z + count - o) % count, 0, keepdims=False)
        for o in range(1, count)
    ]
    to_gate_up = Gather([v[:block] for v in wide])
    to_down = Gather(
        [
            jnp.concatenate(
                [v[block : block + down_rows], v[block + down_rows :, : model - f_lanes]], axis=1
            )
            for v in wide
        ]
    )
    to_gate_up.hop()
    to_down.hop()
    gains = jnp.moveaxis(gains, 0, 1).reshape(2, model).astype(f32)
    projections = whole_projections(
        projections, low, to_proj.cross(), [to_gate_up.mine, to_down.mine]
    )
    w_qkv = projections[:, : 2 * KV + model]

    start = tokens[0].astype(f32)
    norm_1 = normalize(start, gains[0])
    normed = norm_1[0]
    kv = projected_kv(normed, projections, tables, False)


    def first_arrived(state):
        here = (to_gate_up.a, to_gate_up.b, to_down.a, to_down.b)
        state, here = together(state, here)
        to_gate_up.a, to_gate_up.b, to_down.a, to_down.b = here
        to_gate_up.hop_on()
        to_down.hop_on()
        return (), state

    def second_arrived(state):
        state, here = together(state, (to_gate_up.ab, to_down.ab))
        to_gate_up.ab, to_down.ab = here
        return (), state

    saved_first = (norm_1,) + attention(
        normed, kv, projections, where, tables,
        {2: first_arrived, 3: second_arrived},
    )
    mixture = saved_first[3][0]
    w_o = projections[:, 2 * KV + model :]
    w_down = whole_down(down_weight, low, to_down.cross())
    w_gate, w_up = whole_gate_up(gate_weight, up_weight, low, to_gate_up.cross())
    middle, hidden_1, gate_1, up_1, *kept = feed_forward(
        start, mixture, w_o, gains[1], w_gate, w_up, w_down, []
    )

    norm_2 = normalize(middle, gains[0])
    kv = projected_kv(norm_2[0], projections, tables, True)
    half_rows = block // 2

    def left_of(normed, mixture):
        rows_of = jnp.stack([normed.T, mixture]).reshape(2, count, 2, half_rows, rows)
        return jnp.pad(rows_of, ((0, 0),) * 3 + ((0, held - half_rows), (0, 0)))

    left_1 = left_of(norm_1[0], mixture)
    saved_second = (norm_2,) + attention(
        norm_2[0], kv, projections, where, tables, {1: lambda state: (left_1, state)}
    )
    final, hidden_2, gate_2, up_2, nft, active = feed_forward(
        middle, saved_second[3][0], w_o, gains[1], w_gate, w_up, w_down, kept
    )

    real = (positions < length).astype(f32)
    gradient = cotangent[0].astype(f32) * real[:, None]
    down_back = (gradient.astype(bf16),)
    left = jnp.concatenate([left_of(norm_2[0], saved_second[3][0]), left_1], axis=-1)
    d_gu, d_hidden, low_2, d_mixture = feed_forward_back(
        gradient, hidden_2, gains[1], gate_2, up_2, w_gate, w_up, w_down, w_o, [], [left]
    )
    columns_2 = attention_gradient(
        d_mixture, low_2, saved_second, where, tables, {}, lambda dq: ((), dq)
    )
    gradient = layer_gradient(d_hidden, columns_2, norm_2, gains[0], w_qkv)

    down_back = jnp.concatenate(down_back + (gradient.astype(bf16),))
    active = active.reshape(count, 8, down_rows, 2 * rows)
    theirs, ours = ids_of(low ^ 1), ids_of(low)

    def down_pieces(ids, got, wait_for):
        return grad_pieces(
            ids, got, [active, down_back],
            [
                pl.BlockSpec((count, 1, down_rows, 2 * rows), lambda i, ids: (0, ids[i], 0, 0)),
                pl.BlockSpec((2 * rows, model), lambda i, ids: (0, 0)),
            ],
            flat_product, (count, down_rows, model), 1.4, wait_for,
        )

    send, token = down_pieces(theirs, None, ())
    to_down = Reduction(send)
    away, home, token = down_pieces(ours, to_down.got, [token])
    to_down.hop(away, [home[0]], [home[1]])
    d_gu, d_hidden, low_1, d_mixture = feed_forward_back(
        gradient, hidden_1, gains[1], gate_1, up_1, w_gate, w_up, w_down, w_o, [d_gu], [token]
    )

    def gate_up_pieces(ids, got, wait_for):
        return grad_pieces(
            ids, got, [nft, d_gu],
            [
                pl.BlockSpec((model, 2 * rows), lambda i, ids: (0, 0)),
                pl.BlockSpec(
                    (1, 2 * rows, f_lanes), lambda i, ids: (ids[i] % 2, 0, ids[i] // 2)
                ),
            ],
            flat_product, (count, block, f_lanes), 2.2, wait_for,
        )

    send, token = gate_up_pieces(theirs, None, ())
    to_gate_up = Reduction(send)
    to_down.came, d_hidden = together(to_down.came, d_hidden)
    to_down.hop_on()

    def third(dq):
        return [token], dq

    def second(dq):
        away, home, token = gate_up_pieces(ours, to_gate_up.got, [dq])
        to_gate_up.hop(away, [home[0]], [home[1]])
        dq, to_down.came = together(dq, to_down.came)
        to_down.settle()
        return [token], dq

    def zeroth(dq):
        dq, to_gate_up.came = together(dq, to_gate_up.came)
        to_gate_up.add_up()
        dq, to_gate_up.far, to_down.cuts = together(dq, to_gate_up.far, to_down.cuts)
        to_gate_up.go_on()
        to_down.shift()
        return (), dq

    columns_1 = attention_gradient(
        d_mixture, low_1, saved_first, where, tables,
        {3: third, 2: second, 0: zeroth}, lambda dq: ((), dq),
    )
    columns_1, to_gate_up.came, to_down.came = together(
        columns_1, to_gate_up.came, to_down.came
    )
    to_gate_up.settle()
    to_gate_up.shift()

    def compute_proj(pid, put, a, b, right_2, right_1):
        right = jnp.concatenate([right_2[...], right_1[...]], axis=0)

        def product_of(ref):
            total = product(ref[...].reshape(count * held, 2 * rows), right, 1, 0)
            return total.reshape(count, held, lanes)[:, :half_rows]

        @pl.when(pid // 2 != 2)
        def _():
            put(product_of(a))

        @pl.when(pid // 2 == 2)
        def _():
            lane = lax.broadcasted_iota(jnp.int32, (count, half_rows, lanes), 2)
            put(jnp.where(lane < lanes // 2, product_of(a), product_of(b)))

    def proj_pieces(ids, wait_for, us):
        def left_spec(k):
            return pl.BlockSpec(
                (1, count, 1, held, 2 * rows),
                lambda i, ids: (jnp.where(ids[i] // 2 * 2 + k > 4, 1, 0), 0, ids[i] % 2, 0, 0),
            )

        right_spec = pl.BlockSpec((rows, lanes), lambda i, ids: (0, ids[i] // 2))
        return grad_pieces(
            ids, None, [left, left, columns_2, columns_1],
            [left_spec(0), left_spec(1), right_spec, right_spec],
            compute_proj, (count, half_rows, lanes), us, wait_for, 24,
        )

    send, token = proj_pieces(theirs, to_gate_up.cuts[0], 2)
    to_proj = Reduction(send)
    keep, token = proj_pieces(ours, [token], 0.01)
    down_handed = hand(to_down.total())
    keep, down_handed[1:3] = together(keep, down_handed[1:3])
    down_handed[3] = swap(down_handed[2], first_hop)
    got = to_proj.got
    to_proj.hop(add(keep[:2], got[:2]), [keep[2], got[2]], [keep[3], got[3]])
    (
        to_proj.came, to_gate_up.came[0], to_gate_up.came[2], down_handed[3]
    ) = together(
        to_proj.came, to_gate_up.came[0], to_gate_up.came[2], down_handed[3]
    )
    to_proj.hop_on()
    to_proj.settle()
    to_proj.cuts, to_gate_up.came[1] = together(to_proj.cuts, to_gate_up.came[1])
    gate_up_handed = hand(to_gate_up.total())
    to_proj.shift()
    proj_mine, gate_up_handed[1:] = together(to_proj.total(), gate_up_handed[1:])
    gradient = layer_gradient(d_hidden, columns_1, norm_1, gains[0], w_qkv)
    g_down = give(down_handed)
    proj_handed = hand(proj_mine)
    gate_up_handed[0], proj_handed[2] = together(gate_up_handed[0], proj_handed[2])
    proj_handed[3] = swap(proj_handed[2], first_hop)
    g_gate_up = give(gate_up_handed)

    def put_down(refs, q, c, pid, value):
        refs[0][pl.ds(pl.multiple_of(pid * down_rows, 8), down_rows), :] = value

    def put_gate_up(refs, q, c, pid, value):
        refs[c][:, lanes_at(q * f_lanes, f_lanes)] = value

    widths = [KV, KV, model, model]

    def put_proj(refs, q, c, pid, value):
        here = slice(c * half_rows, (c + 1) * half_rows)
        for quarter in range(4):

            @pl.when(q == quarter)
            def _():
                first = 0
                for ref, width in zip(refs, widths):
                    start = max(first, quarter * lanes)
                    stop = min(first + width, (quarter + 1) * lanes)
                    if start < stop:
                        ref[here, start - first : stop - first] = value[
                            :, start - quarter * lanes : stop - quarter * lanes
                        ]
                    first += width

    g_down = spread(low, g_down, [(8 * down_rows, model)], put_down)[0]
    g_gate, g_up = spread(low, g_gate_up, [(block, hidden_units)] * 2, put_gate_up)
    g_gate, g_up, proj_handed[3] = together(g_gate, g_up, proj_handed[3])
    g_proj = give(proj_handed)
    g_k, g_v, g_q, g_o = spread(
        low, g_proj, [(block, w) for w in widths], put_proj
    )

    def gain_gradient(gain, pairs):
        along = sum(jnp.sum(w.astype(f32) * g, axis=1) for w, g in pairs)
        return along / gain.astype(f32)

    g_attention_gain = gain_gradient(
        attention_gain, [(query_weight, g_q), (key_weight, g_k), (value_weight, g_v)]
    )
    g_feedforward_gain = gain_gradient(
        feedforward_gain, [(gate_weight, g_gate), (up_weight, g_up)]
    )

    return (
        final.astype(bf16)[None],
        gradient.astype(bf16)[None],
        g_attention_gain,
        g_feedforward_gain,
        g_q,
        g_k,
        g_v,
        g_o,
        g_gate,
        g_up,
        g_down,
    )


def solution(mesh):
    rows = P("fsdp", None)
    placed = (P("dp", "fsdp", None), P("dp"), P("dp", "fsdp", None), P("fsdp"), P("fsdp")) + (
        rows,
    ) * 7
    return jax.shard_map(
        local,
        mesh=mesh,
        in_specs=placed,
        out_specs=(P("dp", "fsdp", None), P("dp", "fsdp", None), P("fsdp"), P("fsdp"))
        + (rows,) * 7,
        check_vma=False,
    )
```

```python
import jax
import jax.numpy as jnp
from jax import lax
from jax.experimental import pallas as pl
from jax.experimental.pallas import tpu as pltpu
from jax.sharding import PartitionSpec as P

HEADS = 15
KV_HEADS = 5
HD = 64
GROUP = HEADS // KV_HEADS
KV = KV_HEADS * HD

norm_epsilon = 1e-05
rotary_base = 10000.0

bf16 = jnp.bfloat16
f32 = jnp.float32


def first_hop(i):
    return i ^ (4 if i & 1 else 2)


def second_hop(i):
    return i ^ (2 if i & 1 else 4)


def sibling(i):
    return i ^ 1


def swap(value, hop):
    count = lax.axis_size("dp")
    return lax.ppermute(value, "dp", [(i, hop(i)) for i in range(count)])


def climb(value, step):
    count = lax.axis_size("fsdp")
    return lax.ppermute(value, "fsdp", [(i, i + 1) for i in range(step - 1, count - 1)])


def descend(value, step):
    count = lax.axis_size("fsdp")
    return lax.ppermute(value, "fsdp", [(i, i - 1) for i in range(1, count - step + 1)])


def place():
    low = lax.axis_index("dp") % 8
    core = low % 2
    one = jnp.where(core == 1, 4, 2)
    return low, core, one, 6 - one


def around(value, distance):
    count = lax.axis_size("fsdp")
    return lax.ppermute(value, "fsdp", [(i, (i + distance) % count) for i in range(count)])


def together(*values):
    return lax.optimization_barrier(values)


def call(kernel, operands, wait_for=(), scalars=0, in_specs=(), grid=(), **rest):
    wait_for = jax.tree.leaves(wait_for)
    last = len(operands)

    def waiting(*refs):
        kernel(*refs[:last], *refs[last + len(wait_for) :])

    in_specs = list(in_specs) + [pl.BlockSpec(memory_space=pl.ANY)] * len(wait_for)
    where = dict(in_specs=in_specs, out_specs=rest.pop("out_specs"))
    scratch = rest.pop("scratch_shapes", ())
    if scalars:
        where = dict(
            grid_spec=pltpu.PrefetchScalarGridSpec(
                num_scalar_prefetch=scalars, grid=grid, scratch_shapes=scratch, **where
            )
        )
    else:
        where.update(grid=grid, scratch_shapes=scratch)
    return pl.pallas_call(waiting, **where, **rest)(*operands, *wait_for)


class Gather:
    def __init__(self, blocks):
        self.blocks = blocks

    def hop(self):
        self.mine = jnp.stack(self.blocks)
        self.a = swap(self.mine, first_hop)
        self.b = swap(self.mine, second_hop)

    def hop_on(self):
        self.ab = swap(self.a, second_hop)

    def cross(self):
        mine = [self.mine, self.a, self.b, self.ab]
        return mine + [swap(v, sibling) for v in mine]


def other_blocks(own):
    return [around(own, o) for o in range(1, lax.axis_size("fsdp"))]


def piece_ids(low):
    odd = low % 2
    one = 2 + 2 * odd
    two = 6 - one
    return [low, low ^ one, low ^ two, low ^ 6, low ^ 1, low ^ 1 ^ two, low ^ 1 ^ one, low ^ 7]


def lay_out(low, pieces, own, out_shapes, moves, wait_for=()):
    count = lax.axis_size("fsdp")
    where = jnp.stack([lax.axis_index("fsdp"), low]).astype(jnp.int32)

    def kernel(where_ref, *refs):
        piece_refs, refs = refs[:8], refs[8:]
        own_refs, refs = refs[: len(own)], refs[len(own) :]
        outs = refs
        z, low = where_ref[0], where_ref[1]
        for core in range(2):

            @pl.when(low % 2 == core)
            def _():
                copies = []
                for k, pid in enumerate(piece_ids(low)):
                    own_core = core if k < 4 else 1 - core
                    for o in range(count - 1):
                        block = lax.rem(z + count - 1 - o, count)
                        copies += moves(piece_refs[k].at[o], block, pid // 2, own_core, pid, outs)
                for source, target in copies + own_moves(own_refs, z, outs):
                    target[...] = source[...]

    moves, own_moves = moves
    vmem = pl.BlockSpec(memory_space=pltpu.VMEM)
    return call(
        kernel,
        [where, *pieces, *own],
        wait_for,
        in_specs=[pl.BlockSpec(memory_space=pltpu.SMEM)] + [vmem] * (8 + len(own)),
        out_specs=[vmem] * len(out_shapes),
        out_shape=[jax.ShapeDtypeStruct(shape, bf16) for shape in out_shapes],
        compiler_params=pltpu.CompilerParams(vmem_limit_bytes=26 * 2**20),
        name="lay_out",
        cost_estimate=cost(5),
    )


def rows_at(start, size):
    return pl.ds(pl.multiple_of(start, 16), size)


def lanes_at(start, size):
    return pl.ds(start if isinstance(start, int) else pl.multiple_of(start, 128), size)


def projection_piece(shard, low, core):
    block, width = shard.shape
    rest = block // 2 // 16 * 16
    lanes = width // 4
    return lax.dynamic_slice(shard, (core * rest, low // 2 * lanes), (block - rest, lanes))


def gate_up_piece(gate, up, low, core):
    lanes = gate.shape[1] // 4
    gate, up = (lax.dynamic_slice_in_dim(v, low // 2 * lanes, lanes, 1) for v in (gate, up))
    return jnp.where(core == 1, up, gate)


def down_piece(shard, low):
    rows = shard.shape[0] // 8
    return lax.dynamic_slice_in_dim(shard, low * rows, rows, 0)


def whole_projections(shard, low, pieces, wait_for):
    count = lax.axis_size("fsdp")
    block, width = shard.shape
    lanes = width // 4
    rest = block // 2 // 16 * 16
    held = block - rest

    def moves(src, z, q, c, pid, outs):
        size = held if c else rest
        return [
            (
                src.at[pl.ds(0, size)],
                outs[0].at[rows_at(z * block + c * rest, size), lanes_at(q * lanes, lanes)],
            )
        ]

    def own_moves(refs, z, outs):
        return [(refs[0], outs[0].at[rows_at(z * block, block)])]

    return lay_out(
        low, pieces, [shard], [(count * block, width)], (moves, own_moves), wait_for
    )[0]


def whole_gate_up(gate, up, low, pieces):
    count = lax.axis_size("fsdp")
    block, width = gate.shape
    lanes = width // 4

    def moves(src, z, q, c, pid, outs):
        return [(src, outs[c].at[rows_at(z * block, block), lanes_at(q * lanes, lanes)])]

    def own_moves(refs, z, outs):
        return [(refs[k], outs[k].at[rows_at(z * block, block)]) for k in range(2)]

    return lay_out(low, pieces, [gate, up], [(count * block, width)] * 2, (moves, own_moves))


def whole_down(shard, low, pieces):
    count = lax.axis_size("fsdp")
    block, width = shard.shape
    rows = block // 8

    def moves(src, z, q, c, pid, outs):
        return [(src, outs[0].at[rows_at(z * block + pid * rows, rows)])]

    def own_moves(refs, z, outs):
        return [(refs[0], outs[0].at[rows_at(z * block, block)])]

    return lay_out(low, pieces, [shard], [(count * block, width)], (moves, own_moves))[0]


def all_blocks(others, own):
    count = lax.axis_size("fsdp")
    z = lax.axis_index("fsdp")
    both = jnp.concatenate([own[None], others])
    return jnp.stack(
        [
            lax.dynamic_index_in_dim(both, (k - z + count) % count, 0, keepdims=False)
            for k in range(count)
        ]
    )


def add(*terms):
    return sum(v.astype(f32) for v in terms).astype(bf16)


def cost(us, weight=8):
    return pl.CostEstimate(
        flops=int(us * weight * 1.15e9), bytes_accessed=0, transcendentals=0
    )


HEAVY = 8


class Reduction:
    def __init__(self, send):
        self.got = swap(send, sibling)

    def hop(self, away, near, far):
        self.near, self.far = near, far
        self.came = swap(away, first_hop)

    def hop_on(self):
        self.add_up()
        self.go_on()

    def add_up(self):
        self.far = add(*self.far, self.came[1])
        self.near = add(*self.near, self.came[0])

    def go_on(self):
        self.came = swap(self.far, second_hop)

    def settle(self):
        count, z = lax.axis_size("fsdp"), lax.axis_index("fsdp")
        self.near = add(self.near, self.came)
        self.cuts = [
            lax.dynamic_index_in_dim(self.near, (z + o) % count, 0, keepdims=False)
            for o in range(count)
        ]

    def shift(self):
        count = lax.axis_size("fsdp")
        self.came = [around(self.cuts[o], o) for o in range(1, count)]

    def total(self):
        return over_rest(add(self.cuts[0], *self.came))


def over_rest(mine):
    wide = lax.axis_size("dp")
    if wide > 8:
        groups = [[i + 8 * k for k in range(wide // 8)] for i in range(8)]
        mine = lax.psum(mine, "dp", axis_index_groups=groups)
    return mine


def hand(mine):
    b = swap(mine, second_hop)
    a, ab = swap(mine, first_hop), swap(b, first_hop)
    return [mine, a, b, ab]


def give(handed):
    return handed + [swap(v, sibling) for v in handed]


def ids_of(low):
    one = 2 + 2 * (low % 2)
    return [low ^ one, low ^ 6, low, low ^ 6 ^ one]


def spread(low, pieces, out_shapes, put, wait_for=()):
    def turn_out(shape):
        wide, high = (-(-n // 128) * 128 for n in shape[::-1])
        return shape[0] * wide > shape[1] * high

    def kernel(where_ref, *refs):
        low = where_ref[0]
        outs, rest = list(refs[8 : 8 + len(out_shapes)]), list(refs[8 + len(out_shapes) :])
        targets = [rest.pop(0) if turn_out(s) else v for s, v in zip(out_shapes, outs)]
        for core in range(2):

            @pl.when(low % 2 == core)
            def _():
                for k, pid in enumerate(piece_ids(low)):
                    own_core = core if k < 4 else 1 - core
                    put(targets, pid // 2, own_core, pid, refs[k][...].astype(f32))

        for target, out in zip(targets, outs):
            if target is not out:
                out[...] = target[...].T

    vmem = pl.BlockSpec(memory_space=pltpu.VMEM)
    turned = [turn_out(shape) for shape in out_shapes]
    shapes = [shape[::-1] if t else shape for shape, t in zip(out_shapes, turned)]
    out = call(
        kernel,
        [low[None], *pieces],
        wait_for,
        in_specs=[pl.BlockSpec(memory_space=pltpu.SMEM)] + [vmem] * 8,
        out_specs=[vmem] * len(out_shapes),
        out_shape=[jax.ShapeDtypeStruct(shape, f32) for shape in shapes],
        scratch_shapes=[pltpu.VMEM(s, f32) for s, t in zip(out_shapes, turned) if t],
        compiler_params=pltpu.CompilerParams(vmem_limit_bytes=22 * 2**20),
        name="spread",
        cost_estimate=cost(3),
    )
    return [v.T if t else v for v, t in zip(out, turned)]


def grad_pieces(
    ids, got, operands, in_specs, compute, piece_shape, us, wait_for, vmem=56
):
    block = (1,) + piece_shape
    zeros = (0,) * len(piece_shape)
    in_specs, operands = list(in_specs), list(operands)
    n = len(ids)
    if got is None:
        out_specs = [pl.BlockSpec(block, lambda i, ids: (i,) + zeros)]
        out_shape = [jax.ShapeDtypeStruct((n,) + piece_shape, bf16)]
    else:
        in_specs.append(pl.BlockSpec(block, lambda i, ids: (i,) + zeros))
        operands.append(got)
        half = n // 2
        out_specs = [
            pl.BlockSpec(block, lambda i, ids: (jnp.minimum(i, half - 1),) + zeros),
            pl.BlockSpec(block, lambda i, ids: (jnp.maximum(i - half, 0),) + zeros),
        ]
        out_shape = [jax.ShapeDtypeStruct((half,) + piece_shape, bf16)] * 2

    out_specs.append(pl.BlockSpec((8, 128), lambda i, ids: (0, 0)))
    out_shape.append(jax.ShapeDtypeStruct((8, 128), f32))

    def kernel(ids_ref, *refs):
        step = pl.program_id(0)
        refs[-1][...] = jnp.zeros((8, 128), f32)
        refs = refs[:-1]
        if got is None:

            def put(total):
                refs[-1][...] = total.astype(bf16).reshape(block)

            compute(ids_ref[step], put, *refs[:-1])
        else:

            def put(total):
                total = (total + refs[-3][...].reshape(total.shape).astype(f32)).astype(bf16)

                @pl.when(step < half)
                def _():
                    refs[-2][...] = total.reshape(block)

                @pl.when(step >= half)
                def _():
                    refs[-1][...] = total.reshape(block)

            compute(ids_ref[step], put, *refs[:-3])

    return call(
        kernel,
        [jnp.stack(ids).astype(jnp.int32), *operands],
        wait_for,
        scalars=1,
        grid=(n,),
        in_specs=in_specs,
        out_specs=out_specs,
        out_shape=out_shape,
        compiler_params=pltpu.CompilerParams(vmem_limit_bytes=vmem * 2**20),
        name="weight_grad",
        cost_estimate=cost(us * n, HEAVY),
    )


def flat_product(pid, put, left_ref, right_ref):
    left, right = left_ref[...], right_ref[...]
    put(product(left.reshape(-1, left.shape[-1]), right.reshape(right.shape[-2:]), 1, 0))


def product(a, b, over_a, over_b):
    return lax.dot_general(
        a, b, (((over_a,), (over_b,)), ((), ())), preferred_element_type=f32
    )


def side_by_side(x):
    return jnp.concatenate([x[HD * g : HD * (g + 1)] for g in range(GROUP)], axis=1)


def diagonal_mask(scores, rows, room):
    key = lax.broadcasted_iota(jnp.int32, (rows, rows), 0)
    query = lax.broadcasted_iota(jnp.int32, (rows, rows), 1)
    seen = (key <= query) & (key < room)
    return jnp.where(jnp.concatenate([seen] * GROUP, axis=1), scores, -1e30)


SUMS = 16


def attend_kernel(d, n, place_ref, q_ref, *refs):
    joined = refs[0].shape[0] > KV
    k_ref, v_ref = refs[0], refs[0 if joined else 1]
    refs = refs[1 if joined else 2 :]
    first, last = d == 0, d == n - 1
    m1_ref, a1_ref = (None, None) if first else refs[:2]
    m2_ref, a2_ref = refs[-2:]
    z, room = place_ref[0], place_ref[1]
    rows = q_ref.shape[1]

    @pl.when(z >= d)
    def _():
        ones = jnp.ones((SUMS, rows), bf16)
        for h in range(KV_HEADS):
            q = side_by_side(q_ref[GROUP * HD * h : GROUP * HD * (h + 1), :])
            k = k_ref[HD * h : HD * (h + 1), :]
            start = HD * h + (KV if joined else 0)
            v = v_ref[start : start + HD, :]
            s = product(k, q, 0, 0)
            if first:
                s = diagonal_mask(s, rows, room)
            m = jnp.max(s, axis=0, keepdims=True)
            if not first:
                m = jnp.maximum(m, m1_ref[h])
            p = jnp.exp(s - m).astype(bf16)
            total = product(jnp.concatenate([v, ones], axis=0), p, 1, 0)
            if not first:
                total = total + a1_ref[h] * jnp.exp(m1_ref[h] - m)
            m2_ref[h] = m
            a2_ref[h] = total

    if not first:

        @pl.when(z < d)
        def _():
            m2_ref[...] = m1_ref[...]
            a2_ref[...] = a1_ref[...]

    if last:
        o_ref, lse_ref = refs[2:4]
        for h in range(KV_HEADS):
            l = a2_ref[h, HD : HD + 1, :]
            o = (a2_ref[h, :HD, :] / l).astype(bf16)
            lse = m2_ref[h] + jnp.log(l)
            for g in range(GROUP):
                here = slice(HD * (GROUP * h + g), HD * (GROUP * h + g + 1))
                o_ref[here, :] = o[:, rows * g : rows * (g + 1)]
                lse_ref[h, g : g + 1, :] = lse[:, rows * g : rows * (g + 1)]


def attend(d, n, where, q, kv, state, wait_for):
    rows = q.shape[1]
    state_shapes = [(KV_HEADS, 1, GROUP * rows), (KV_HEADS, HD + SUMS, GROUP * rows)]
    out_shape = [jax.ShapeDtypeStruct(shape, f32) for shape in state_shapes]
    scratch = []
    if d == n - 1:
        scratch = [pltpu.VMEM(shape, f32) for shape in state_shapes]
        out_shape = [
            jax.ShapeDtypeStruct(q.shape, bf16),
            jax.ShapeDtypeStruct((KV_HEADS, GROUP, rows), f32),
        ]
    vmem = pl.BlockSpec(memory_space=pltpu.VMEM)
    return call(
        lambda *refs: attend_kernel(d, n, *refs),
        [where, q, *kv, *state],
        wait_for,
        in_specs=[pl.BlockSpec(memory_space=pltpu.SMEM)] + [vmem] * (1 + len(kv) + len(state)),
        out_specs=[vmem, vmem],
        out_shape=out_shape,
        scratch_shapes=scratch,
        compiler_params=pltpu.CompilerParams(vmem_limit_bytes=24 * 2**20),
        name="attend",
        cost_estimate=cost(4),
    )


def specs(rows):
    return (
        pl.BlockSpec((GROUP * HD, rows), lambda h, s: (h, 0)),
        pl.BlockSpec((2, HD, rows), lambda h, s: (0, h, 0)),
        pl.BlockSpec((1, GROUP, rows), lambda h, s: (h, 0, 0)),
    )


def turn(columns, cosine, sine, heads):
    half = HD // 2
    parts = []
    for h in range(heads):
        a = columns[HD * h : HD * h + half]
        b = columns[HD * h + half : HD * (h + 1)]
        parts += [a * cosine - b * sine, b * cosine + a * sine]
    return jnp.concatenate(parts, axis=0)


def attend_back_kernel(d, place_ref, q_ref, o_ref, do_ref, lse_ref, k_ref, v_ref, *refs):
    dq_ref, dk_ref, dv_ref = refs[-3:]
    before_ref = None if len(refs) == 3 else refs[-4]
    z, room = place_ref[0], place_ref[1]
    rows = q_ref.shape[1]

    @pl.when(z >= d)
    def _():
        q, do, o = (side_by_side(r[...]) for r in (q_ref, do_ref, o_ref))
        lse = jnp.concatenate([lse_ref[0, g : g + 1, :] for g in range(GROUP)], axis=1)
        delta = jnp.sum(do.astype(f32) * o.astype(f32), axis=0, keepdims=True)
        k, v = k_ref[...], v_ref[...]
        s = product(k, q, 0, 0)
        if d == 0:
            s = diagonal_mask(s, rows, room)
        p = jnp.exp(s - lse)
        dp = product(v, do, 0, 0)
        ds = (p * (dp - delta)).astype(bf16)
        dv_ref[...] = product(p.astype(bf16), do, 1, 1).T.astype(bf16)
        dk_ref[...] = product(ds, q, 1, 1).T.astype(bf16)
        dq = product(k, ds, 1, 0) * HD ** (-0.5)
        for g in range(GROUP):
            here = slice(HD * g, HD * (g + 1))
            part = dq[:, rows * g : rows * (g + 1)]
            if before_ref is not None:
                part = part + before_ref[here, :]
            if d == 0:
                part = turn(part, refs[0][...], -refs[1][...], 1).astype(bf16)
            dq_ref[here, :] = part

    if d > 0:

        @pl.when(z < d)
        def _():
            dk_ref[...] = jnp.zeros(dk_ref.shape, bf16)
            dv_ref[...] = jnp.zeros(dv_ref.shape, bf16)
            if before_ref is None:
                dq_ref[...] = jnp.zeros(dq_ref.shape, f32)
            else:
                dq_ref[...] = before_ref[...]


def attend_back(d, where, q, o, do, lse, kv, before, tables, wait_for):
    rows = q.shape[1]
    q_spec, kv_spec, lse_spec = specs(rows)
    k_spec = pl.BlockSpec((HD, rows), lambda h, s: (h, 0))
    skip = 0 if len(kv) > 1 else KV_HEADS
    v_spec = pl.BlockSpec((HD, rows), lambda h, s: (skip + h, 0))
    extra, extra_specs = [], []
    if d == 0:
        extra = list(tables)
        extra_specs = [pl.BlockSpec((HD // 2, rows), lambda h, s: (0, 0))] * 2
    if before is not None:
        extra.append(before)
        extra_specs.append(q_spec)
    return call(
        lambda *refs: attend_back_kernel(d, *refs),
        [where, q, o, do, lse, kv[0], kv[-1], *extra],
        wait_for,
        scalars=1,
        grid=(KV_HEADS,),
        in_specs=[q_spec, q_spec, q_spec, lse_spec, k_spec, v_spec] + extra_specs,
        out_specs=[q_spec, k_spec, k_spec],
        out_shape=[
            jax.ShapeDtypeStruct(q.shape, f32 if d else bf16),
            jax.ShapeDtypeStruct((KV, rows), bf16),
            jax.ShapeDtypeStruct((KV, rows), bf16),
        ],
        compiler_params=pltpu.CompilerParams(vmem_limit_bytes=32 * 2**20),
        name="attend_back",
        cost_estimate=cost(7, HEAVY),
    )


def gradient_columns(own, got, dq, low, tables, wait_for):
    rows = dq.shape[1]
    lanes = 2 * KV + dq.shape[0] + low.shape[1]

    def kernel(
        dk_ref, dv_ref, got_k_ref, got_v_ref, dq_ref, low_ref, cos_ref, sin_ref, out_ref
    ):
        dk = dk_ref[...].astype(f32) + got_k_ref[...].astype(f32)
        dv = dv_ref[...].astype(f32) + got_v_ref[...].astype(f32)
        keys = turn(dk, cos_ref[...], -sin_ref[...], KV_HEADS).astype(bf16)
        sides = jnp.concatenate([keys, dv.astype(bf16), dq_ref[...]], axis=0)
        out_ref[...] = jnp.concatenate([sides.T, low_ref[...]], axis=1)

    vmem = pl.BlockSpec(memory_space=pltpu.VMEM)
    return call(
        kernel,
        [*own, *got, dq, low, *tables],
        wait_for,
        in_specs=[vmem] * 8,
        out_specs=vmem,
        out_shape=jax.ShapeDtypeStruct((rows, lanes), bf16),
        compiler_params=pltpu.CompilerParams(vmem_limit_bytes=16 * 2**20),
        name="gradient_columns",
        cost_estimate=cost(0.01),
    )


def dot(a, b, pattern):
    return jnp.einsum(pattern, a, b, preferred_element_type=f32)


def normalize(x, gain):
    scale = lax.rsqrt(jnp.mean(x * x, axis=-1, keepdims=True) + norm_epsilon)
    unit = x * scale
    return (unit * gain).astype(bf16), unit, scale


def normalize_back(grad, gain, unit, scale):
    grad_unit = grad * gain
    return scale * (grad_unit - unit * jnp.mean(grad_unit * unit, axis=-1, keepdims=True))


def feed_forward_kernel(x_ref, mix_ref, wo_ref, gain_ref, wg_ref, wu_ref, wd_ref, *refs):
    result_ref, hidden_ref, gate_ref, up_ref, nft_ref, active_ref, nf_ref = refs[-7:]

    @pl.when(pl.program_id(0) == 0)
    def _():
        hidden = x_ref[...] + product(mix_ref[...], wo_ref[...], 0, 0)
        hidden_ref[...] = hidden
        normed, _, _ = normalize(hidden, gain_ref[...])
        nf_ref[...] = normed
        nft_ref[...] = normed.T
        result_ref[...] = hidden

    normed = nf_ref[...]
    gate = product(normed, wg_ref[...], 1, 0)
    up = product(normed, wu_ref[...], 1, 0)
    active = (gate * jax.nn.sigmoid(gate) * up).astype(bf16)
    gate_ref[...] = gate.astype(bf16)
    up_ref[...] = up.astype(bf16)
    active_ref[...] = active.T
    result_ref[...] += product(active, wd_ref[...], 1, 0)


def feed_forward(x, mixture, w_o, gain, w_gate, w_up, w_down, kept):
    rows, model = x.shape
    hidden_units = w_gate.shape[1]
    tile = hidden_units // 5
    half = 0 if kept else 1
    whole = lambda *shape: pl.BlockSpec(shape, lambda i: (0,) * len(shape))
    wide = lambda n: pl.BlockSpec((n, tile), lambda i: (0, i))
    return pl.pallas_call(
        feed_forward_kernel,
        grid=(5,),
        in_specs=[
            whole(rows, model), whole(model, rows), whole(model, model), whole(1, model),
            wide(model), wide(model), pl.BlockSpec((tile, model), lambda i: (i, 0)),
        ]
        + [pl.BlockSpec(memory_space=pl.ANY)] * len(kept),
        out_specs=[
            whole(rows, model), whole(rows, model), wide(rows), wide(rows),
            pl.BlockSpec((model, rows), lambda i: (0, half)),
            pl.BlockSpec((tile, rows), lambda i: (i, half)),
        ],
        out_shape=[
            jax.ShapeDtypeStruct((rows, model), f32),
            jax.ShapeDtypeStruct((rows, model), f32),
            jax.ShapeDtypeStruct((rows, hidden_units), bf16),
            jax.ShapeDtypeStruct((rows, hidden_units), bf16),
            jax.ShapeDtypeStruct((model, 2 * rows), bf16),
            jax.ShapeDtypeStruct((hidden_units, 2 * rows), bf16),
        ],
        scratch_shapes=[pltpu.VMEM((rows, model), bf16)],
        input_output_aliases={7: 4, 8: 5} if kept else {},
        compiler_params=pltpu.CompilerParams(vmem_limit_bytes=48 * 2**20),
        name="feed_forward",
        cost_estimate=cost(12),
    )(x, mixture, w_o, gain[None], w_gate, w_up, w_down, *kept)


def feed_forward_back_kernel(grad_ref, hidden_ref, gain_ref, gate_ref, up_ref, wg_ref, wu_ref,
                             wd_ref, wo_ref, *refs):
    d_gu_ref, d_hidden_ref, low_ref, d_mix_ref, total_ref = refs[-5:]
    step = pl.program_id(0)
    low = grad_ref[...].astype(bf16)
    d_active = product(low, wd_ref[...], 1, 1)
    gate, up = gate_ref[...].astype(f32), up_ref[...].astype(f32)
    sig = jax.nn.sigmoid(gate)
    d_gate = (d_active * up * sig * (1.0 + gate * (1.0 - sig))).astype(bf16)
    d_up = (d_active * gate * sig).astype(bf16)
    d_gu_ref[0] = d_gate
    d_gu_ref[1] = d_up
    term = product(d_gate, wg_ref[...], 1, 1) + product(d_up, wu_ref[...], 1, 1)

    @pl.when(step == 0)
    def _():
        total_ref[...] = term

    @pl.when(step > 0)
    def _():
        total_ref[...] += term

    @pl.when(step == pl.num_programs(0) - 1)
    def _():
        hidden = hidden_ref[...]
        scale = lax.rsqrt(jnp.mean(hidden * hidden, axis=-1, keepdims=True) + norm_epsilon)
        d_norm = normalize_back(total_ref[...], gain_ref[...], hidden * scale, scale)
        d_hidden = grad_ref[...] + d_norm
        d_hidden_ref[...] = d_hidden
        low = d_hidden.astype(bf16)
        low_ref[...] = low
        d_mix_ref[...] = product(wo_ref[...], low, 1, 1).astype(bf16)


def feed_forward_back(
    grad, hidden, gain, gate, up, w_gate, w_up, w_down, w_o, kept, wait_for=()
):
    rows, model = grad.shape
    half = 1 if kept else 0
    hidden_units = gate.shape[1]
    tile = hidden_units // 5
    whole = lambda *shape: pl.BlockSpec(shape, lambda i: (0,) * len(shape))
    wide = lambda n: pl.BlockSpec((n, tile), lambda i: (0, i))
    return call(
        feed_forward_back_kernel,
        [grad, hidden, gain[None], gate, up, w_gate, w_up, w_down, w_o, *kept],
        wait_for,
        grid=(5,),
        in_specs=[
            whole(rows, model), whole(rows, model), whole(1, model), wide(rows), wide(rows),
            wide(model), wide(model), pl.BlockSpec((tile, model), lambda i: (i, 0)),
            whole(model, model),
        ]
        + [pl.BlockSpec(memory_space=pl.ANY)] * len(kept),
        out_specs=[
            pl.BlockSpec((2, rows, tile), lambda i: (0, half, i)),
            whole(rows, model), whole(rows, model), whole(model, rows),
        ],
        out_shape=[
            jax.ShapeDtypeStruct((2, 2 * rows, hidden_units), bf16),
            jax.ShapeDtypeStruct((rows, model), f32),
            jax.ShapeDtypeStruct((rows, model), bf16),
            jax.ShapeDtypeStruct((model, rows), bf16),
        ],
        scratch_shapes=[pltpu.VMEM((rows, model), f32)],
        input_output_aliases={9: 0} if kept else {},
        compiler_params=pltpu.CompilerParams(vmem_limit_bytes=48 * 2**20),
        name="feed_forward_back",
        cost_estimate=cost(18, HEAVY),
    )


def project(normed, w, first, lanes, cosine, sine, heads, scale, name, wait_for=(), split=True):
    rows, model = normed.shape

    cuts = [heads * HD, lanes - heads * HD]
    cuts = [n for n in cuts if n] if split else [lanes]

    def kernel(x_ref, w_ref, cos_ref, sin_ref, out_ref, *rest_ref):
        y = product(x_ref[...], w_ref[:, first : first + lanes], 1, 0).T
        turned = turn(y[: heads * HD], cos_ref[...], sin_ref[...], heads)
        out_ref[: heads * HD, :] = turned.astype(bf16) * bf16(scale)
        if heads * HD < lanes:
            ref, start = (rest_ref[0], 0) if split else (out_ref, heads * HD)
            ref[start:, :] = y[heads * HD :].astype(bf16)

    whole = lambda *shape: pl.BlockSpec(shape, lambda i: (0,) * len(shape))
    width = first + lanes if (first + lanes) % 128 == 0 else w.shape[1]
    return call(
        kernel,
        [normed, w, cosine, sine],
        wait_for,
        grid=(1,),
        in_specs=[
            whole(rows, model), whole(model, width), whole(HD // 2, rows), whole(HD // 2, rows)
        ],
        out_specs=[whole(n, rows) for n in cuts],
        out_shape=[jax.ShapeDtypeStruct((n, rows), bf16) for n in cuts],
        compiler_params=pltpu.CompilerParams(vmem_limit_bytes=24 * 2**20),
        name=name,
        cost_estimate=cost(2),
    )


def projected_kv(normed, projections, tables, split):
    return project(
        normed, projections, 0, 2 * KV, *tables, KV_HEADS, 1.0, "keys_values", (), split
    )


def projected_q(normed, projections, tables, wait_for):
    first, lanes = 2 * KV, HEADS * HD
    return project(
        normed, projections, first, lanes, *tables, HEADS, HD**-0.5, "queries", wait_for
    )[0]


def attention(normed, kv, projections, where, tables, before):
    count = lax.axis_size("fsdp")
    kvs = [kv]
    for step in range(1, count):
        kvs.append([climb(v, step) for v in kvs[-1]])
    q = projected_q(normed, projections, tables, kv[:1])
    state = []
    for d in range(count):
        wait_for = ()
        if d in before:
            wait_for, state = before[d](state)
        state = attend(d, count, where, q, kvs[d], state, wait_for)
    return q, kvs, state


def attention_gradient(d_mixture, low, saved, where, tables, before, at_end):
    q, kvs, (mixture, lse) = saved[1:]
    count = lax.axis_size("fsdp")
    dq = moving = got = None
    for d in reversed(range(count)):
        step = count - 1 - d
        wait_for = []
        if d in before:
            wait_for, dq = before[d](dq)
        if step:
            pairs = [(i, i - 1) for i in range(count - step, count)]
            got = [lax.ppermute(v, "fsdp", pairs) for v in moving]
        dq, *dkv = attend_back(
            d, where, q, mixture, d_mixture, lse, kvs[d], dq, tables, wait_for
        )
        if d:
            moving = [add(a, b) for a, b in zip(dkv, got)] if step else dkv
    wait_for, dq = at_end(dq)
    return gradient_columns(dkv, got, dq, low, tables, wait_for)


def layer_gradient(d_hidden, columns, norm, gain, w_qkv):
    normed, unit, scale = norm
    d_normed = dot(columns[:, : w_qkv.shape[1]], w_qkv, "tf,df->td")
    return d_hidden + normalize_back(d_normed, gain, unit, scale)


def local(
    tokens,
    lengths,
    cotangent,
    attention_gain,
    feedforward_gain,
    query_weight,
    key_weight,
    value_weight,
    out_weight,
    gate_weight,
    up_weight,
    down_weight,
):
    rows = tokens.shape[1]
    count = lax.axis_size("fsdp")
    z = lax.axis_index("fsdp")
    low, core, one, two = place()
    positions = z * rows + jnp.arange(rows, dtype=jnp.int32)
    length = lengths[0]
    where = jnp.stack([z, length - z * rows]).astype(jnp.int32)
    frequency = rotary_base ** (-jnp.arange(HD // 2, dtype=f32) * 2.0 / HD)
    angles = frequency[:, None] * positions.astype(f32)[None, :]
    tables = (jnp.cos(angles), jnp.sin(angles))
    block = query_weight.shape[0]
    model = block * count
    hidden_units = gate_weight.shape[1]

    projections = jnp.concatenate([key_weight, value_weight, query_weight, out_weight], axis=1)
    lanes = projections.shape[1] // 4
    f_lanes = hidden_units // 4
    down_rows = down_weight.shape[0] // 8
    own_gains = jnp.stack([attention_gain, feedforward_gain])
    piece = projection_piece(projections, low, core)
    held = piece.shape[0]
    own = lax.optimization_barrier(
        (
            jnp.concatenate([piece, jnp.pad(own_gains, ((0, 14), (0, lanes - block)))]),
            gate_up_piece(gate_weight, up_weight, low, core),
            down_piece(down_weight, low),
        )
    )
    blocks = other_blocks(own[0])
    gains = all_blocks(jnp.stack([v[held : held + 2, :block] for v in blocks[::-1]]), own_gains)
    to_proj = Gather([v[:held] for v in blocks])
    to_proj.hop()
    to_proj.hop_on()
    rest = jnp.pad(own[2][:, f_lanes:], ((0, 0), (0, 2 * f_lanes - model)))
    wide = jnp.concatenate([own[1], own[2][:, :f_lanes], rest])
    wide = lax.all_gather(wide, "fsdp")
    wide = [
        lax.dynamic_index_in_dim(wide, (z + count - o) % count, 0, keepdims=False)
        for o in range(1, count)
    ]
    to_gate_up = Gather([v[:block] for v in wide])
    to_down = Gather(
        [
            jnp.concatenate(
                [v[block : block + down_rows], v[block + down_rows :, : model - f_lanes]], axis=1
            )
            for v in wide
        ]
    )
    to_gate_up.hop()
    to_down.hop()
    gains = jnp.moveaxis(gains, 0, 1).reshape(2, model).astype(f32)
    projections = whole_projections(
        projections, low, to_proj.cross(), [to_gate_up.mine, to_down.mine]
    )
    w_qkv = projections[:, : 2 * KV + model]

    start = tokens[0].astype(f32)
    norm_1 = normalize(start, gains[0])
    normed = norm_1[0]
    kv = projected_kv(normed, projections, tables, False)


    def first_arrived(state):
        here = (to_gate_up.a, to_gate_up.b, to_down.a, to_down.b)
        state, here = together(state, here)
        to_gate_up.a, to_gate_up.b, to_down.a, to_down.b = here
        to_gate_up.hop_on()
        to_down.hop_on()
        return (), state

    def second_arrived(state):
        state, here = together(state, (to_gate_up.ab, to_down.ab))
        to_gate_up.ab, to_down.ab = here
        return (), state

    saved_first = (norm_1,) + attention(
        normed, kv, projections, where, tables,
        {2: first_arrived, 3: second_arrived},
    )
    mixture = saved_first[3][0]
    w_o = projections[:, 2 * KV + model :]
    w_down = whole_down(down_weight, low, to_down.cross())
    w_gate, w_up = whole_gate_up(gate_weight, up_weight, low, to_gate_up.cross())
    middle, hidden_1, gate_1, up_1, *kept = feed_forward(
        start, mixture, w_o, gains[1], w_gate, w_up, w_down, []
    )

    norm_2 = normalize(middle, gains[0])
    kv = projected_kv(norm_2[0], projections, tables, True)
    half_rows = block // 2

    def left_of(normed, mixture):
        rows_of = jnp.stack([normed.T, mixture]).reshape(2, count, 2, half_rows, rows)
        return jnp.pad(rows_of, ((0, 0),) * 3 + ((0, held - half_rows), (0, 0)))

    left_1 = left_of(norm_1[0], mixture)
    saved_second = (norm_2,) + attention(
        norm_2[0], kv, projections, where, tables, {1: lambda state: (left_1, state)}
    )
    final, hidden_2, gate_2, up_2, nft, active = feed_forward(
        middle, saved_second[3][0], w_o, gains[1], w_gate, w_up, w_down, kept
    )

    real = (positions < length).astype(f32)
    gradient = cotangent[0].astype(f32) * real[:, None]
    down_back = (gradient.astype(bf16),)
    left = jnp.concatenate([left_of(norm_2[0], saved_second[3][0]), left_1], axis=-1)
    d_gu, d_hidden, low_2, d_mixture = feed_forward_back(
        gradient, hidden_2, gains[1], gate_2, up_2, w_gate, w_up, w_down, w_o, [], [left]
    )
    columns_2 = attention_gradient(
        d_mixture, low_2, saved_second, where, tables, {}, lambda dq: ((), dq)
    )
    gradient = layer_gradient(d_hidden, columns_2, norm_2, gains[0], w_qkv)

    down_back = jnp.concatenate(down_back + (gradient.astype(bf16),))
    active = active.reshape(count, 8, down_rows, 2 * rows)
    theirs, ours = ids_of(low ^ 1), ids_of(low)

    def down_pieces(ids, got, wait_for):
        return grad_pieces(
            ids, got, [active, down_back],
            [
                pl.BlockSpec((count, 1, down_rows, 2 * rows), lambda i, ids: (0, ids[i], 0, 0)),
                pl.BlockSpec((2 * rows, model), lambda i, ids: (0, 0)),
            ],
            flat_product, (count, down_rows, model), 1.4, wait_for,
        )

    send, token = down_pieces(theirs, None, ())
    to_down = Reduction(send)
    away, home, token = down_pieces(ours, to_down.got, [token])
    to_down.hop(away, [home[0]], [home[1]])
    d_gu, d_hidden, low_1, d_mixture = feed_forward_back(
        gradient, hidden_1, gains[1], gate_1, up_1, w_gate, w_up, w_down, w_o, [d_gu], [token]
    )

    def gate_up_pieces(ids, got, wait_for):
        return grad_pieces(
            ids, got, [nft, d_gu],
            [
                pl.BlockSpec((model, 2 * rows), lambda i, ids: (0, 0)),
                pl.BlockSpec(
                    (1, 2 * rows, f_lanes), lambda i, ids: (ids[i] % 2, 0, ids[i] // 2)
                ),
            ],
            flat_product, (count, block, f_lanes), 2.2, wait_for,
        )

    send, token = gate_up_pieces(theirs, None, ())
    to_gate_up = Reduction(send)
    to_down.came, d_hidden = together(to_down.came, d_hidden)
    to_down.hop_on()

    def third(dq):
        return [token], dq

    def second(dq):
        away, home, token = gate_up_pieces(ours, to_gate_up.got, [dq])
        to_gate_up.hop(away, [home[0]], [home[1]])
        dq, to_down.came = together(dq, to_down.came)
        to_down.settle()
        return [token], dq

    def zeroth(dq):
        dq, to_gate_up.came = together(dq, to_gate_up.came)
        to_gate_up.add_up()
        dq, to_gate_up.far, to_down.cuts = together(dq, to_gate_up.far, to_down.cuts)
        to_gate_up.go_on()
        to_down.shift()
        return (), dq

    columns_1 = attention_gradient(
        d_mixture, low_1, saved_first, where, tables,
        {3: third, 2: second, 0: zeroth}, lambda dq: ((), dq),
    )
    columns_1, to_gate_up.came, to_down.came = together(
        columns_1, to_gate_up.came, to_down.came
    )
    to_gate_up.settle()
    to_gate_up.shift()

    def compute_proj(pid, put, a, b, right_2, right_1):
        right = jnp.concatenate([right_2[...], right_1[...]], axis=0)

        def product_of(ref):
            total = product(ref[...].reshape(count * held, 2 * rows), right, 1, 0)
            return total.reshape(count, held, lanes)[:, :half_rows]

        @pl.when(pid // 2 != 2)
        def _():
            put(product_of(a))

        @pl.when(pid // 2 == 2)
        def _():
            lane = lax.broadcasted_iota(jnp.int32, (count, half_rows, lanes), 2)
            put(jnp.where(lane < lanes // 2, product_of(a), product_of(b)))

    def proj_pieces(ids, wait_for, us):
        def left_spec(k):
            return pl.BlockSpec(
                (1, count, 1, held, 2 * rows),
                lambda i, ids: (jnp.where(ids[i] // 2 * 2 + k > 4, 1, 0), 0, ids[i] % 2, 0, 0),
            )

        right_spec = pl.BlockSpec((rows, lanes), lambda i, ids: (0, ids[i] // 2))
        return grad_pieces(
            ids, None, [left, left, columns_2, columns_1],
            [left_spec(0), left_spec(1), right_spec, right_spec],
            compute_proj, (count, half_rows, lanes), us, wait_for, 24,
        )

    send, token = proj_pieces(theirs, to_gate_up.cuts[0], 2)
    to_proj = Reduction(send)
    keep, token = proj_pieces(ours, [token], 0.01)
    down_handed = hand(to_down.total())
    keep, down_handed[1:3] = together(keep, down_handed[1:3])
    down_handed[3] = swap(down_handed[2], first_hop)
    got = to_proj.got
    to_proj.hop(add(keep[:2], got[:2]), [keep[2], got[2]], [keep[3], got[3]])
    (
        to_proj.came, to_gate_up.came[0], to_gate_up.came[2], down_handed[3]
    ) = together(
        to_proj.came, to_gate_up.came[0], to_gate_up.came[2], down_handed[3]
    )
    to_proj.hop_on()
    to_proj.settle()
    to_proj.cuts, to_gate_up.came[1] = together(to_proj.cuts, to_gate_up.came[1])
    gate_up_handed = hand(to_gate_up.total())
    to_proj.shift()
    proj_mine, gate_up_handed[1:] = together(to_proj.total(), gate_up_handed[1:])
    gradient = layer_gradient(d_hidden, columns_1, norm_1, gains[0], w_qkv)
    g_down = give(down_handed)
    proj_handed = hand(proj_mine)
    gate_up_handed[0], proj_handed[2] = together(gate_up_handed[0], proj_handed[2])
    proj_handed[3] = swap(proj_handed[2], first_hop)
    g_gate_up = give(gate_up_handed)

    def put_down(refs, q, c, pid, value):
        refs[0][pl.ds(pl.multiple_of(pid * down_rows, 8), down_rows), :] = value

    def put_gate_up(refs, q, c, pid, value):
        refs[c][:, lanes_at(q * f_lanes, f_lanes)] = value

    widths = [KV, KV, model, model]

    def put_proj(refs, q, c, pid, value):
        here = slice(c * half_rows, (c + 1) * half_rows)
        for quarter in range(4):

            @pl.when(q == quarter)
            def _():
                first = 0
                for ref, width in zip(refs, widths):
                    start = max(first, quarter * lanes)
                    stop = min(first + width, (quarter + 1) * lanes)
                    if start < stop:
                        ref[here, start - first : stop - first] = value[
                            :, start - quarter * lanes : stop - quarter * lanes
                        ]
                    first += width

    g_down = spread(low, g_down, [(8 * down_rows, model)], put_down)[0]
    g_gate, g_up = spread(low, g_gate_up, [(block, hidden_units)] * 2, put_gate_up)
    g_gate, g_up, proj_handed[3] = together(g_gate, g_up, proj_handed[3])
    g_proj = give(proj_handed)
    g_k, g_v, g_q, g_o = spread(
        low, g_proj, [(block, w) for w in widths], put_proj
    )

    def gain_gradient(gain, pairs):
        along = sum(jnp.sum(w.astype(f32) * g, axis=1) for w, g in pairs)
        return along / gain.astype(f32)

    g_attention_gain = gain_gradient(
        attention_gain, [(query_weight, g_q), (key_weight, g_k), (value_weight, g_v)]
    )
    g_feedforward_gain = gain_gradient(
        feedforward_gain, [(gate_weight, g_gate), (up_weight, g_up)]
    )

    return (
        final.astype(bf16)[None],
        gradient.astype(bf16)[None],
        g_attention_gain,
        g_feedforward_gain,
        g_q,
        g_k,
        g_v,
        g_o,
        g_gate,
        g_up,
        g_down,
    )


def solution(mesh):
    rows = P("fsdp", None)
    placed = (P("dp", "fsdp", None), P("dp"), P("dp", "fsdp", None), P("fsdp"), P("fsdp")) + (
        rows,
    ) * 7
    return jax.shard_map(
        local,
        mesh=mesh,
        in_specs=placed,
        out_specs=(P("dp", "fsdp", None), P("dp", "fsdp", None), P("fsdp"), P("fsdp"))
        + (rows,) * 7,
        check_vma=False,
    )
```
